32 devices in a mesh: groups: 2 (over y), dp: 4 (over x, core), mp: 4 (over z).
Axes of the slice: x: 2, y: 2, z: 4, core: 2. Of those that a mesh axis runs over, the one named last changes fastest.
Arguments:
- hidden: bfloat16 [8192, 8192], P(('groups', 'dp'), 'mp'), parts along dimension 0, may hold values from -6 to 6
- w_kv: bfloat16 [8192, 2048], P('mp'), may hold values from -0.0625 to 0.0625
- grad_kv: bfloat16 [8192, 2048], P(('groups', 'dp', 'mp')), parts along dimension 0, may hold values from -6 to 6
- proj_in: bfloat16 [8192, 128], P('mp'), may hold values from -0.0625 to 0.0625
- proj_out: bfloat16 [2, 1024, 64], replicated, may hold values from -0.1875 to 0.1875
- queries: bfloat16 [2048, 8192], P('dp', 'mp'), may hold values from -0.001953125 to 0.001953125
Outputs:
- input_grad: bfloat16 [8192, 8192], P(('groups', 'dp'), 'mp'), parts along dimension 0
- scores: float32 [8, 2048], P(('groups', 'dp'), 'mp'), parts along dimension 0
The draws below stay inside these ranges and needn't reach their ends.
There are 2 independent parts, one for each index of `groups`. The reference program is written for one: setup_inputs(seed, part) draws one part's arguments, and reference() takes and returns one part's arrays. A program takes and returns all parts, laid end to end along the dimension named above; an argument that names none is the same for every part. Nothing has to cross between parts.
All inputs are finite; a program needn't handle non-finite values.
Results may differ from the reference program's by a relative error of at most 0.001.
Values may be sent and summed in bfloat16 or wider, within the bound.
No kernel may reach another device: no remote copies, remote signals or barrier semaphores. Data moves between devices by JAX's collectives and lax.ppermute only.
A program may use at most 128 MiB of HBM per device.

```python
import jax
import jax.numpy as jnp
from jax import lax

D = 8192
KV = 1024
RANK = 64
SEQ = 1024
TOKENS = 4096
QUERIES = 2048
FEATS = 8192


def shard_levels(own_key, dims, shards, least, largest):
    def one(position, blocks):
        draws = jax.random.uniform(jax.random.fold_in(jax.random.fold_in(own_key, 6), position), (blocks,), jnp.float32, least / len(shards), largest / len(shards))
        return jnp.repeat(jnp.exp(draws), dims[position] // blocks).reshape((-1,) + (1,) * (len(dims) - position - 1))

    level = one(*shards[0])
    for cut in shards[1:]:
        level = level * one(*cut)
    return level


def noise(key, extent, scale, most, split=(), held_as=jnp.bfloat16):
    entries = scale * jax.random.normal(key, extent, jnp.float32)
    if split:
        entries = entries * shard_levels(key, extent, split, -0.22, 0.18)
    return jnp.clip(entries, -most, most).astype(held_as)


def setup_inputs(seed: int = 0, part: int = 0) -> dict:
    seeds = jax.random.split(jax.random.key(seed), 7)
    own_keys = jax.random.split(jax.random.fold_in(seeds[6], part), 7)
    return {
        "hidden": noise(own_keys[0], (TOKENS, D), 1.0, 6.0, ((0, 4), (1, 4))),
        "w_kv": noise(seeds[1], (D, 2 * KV), D ** -0.5, 0.0625, ((0, 4),)),
        "grad_kv": noise(own_keys[2], (TOKENS, 2 * KV), 1.0, 6.0, ((0, 16),)),
        "proj_in": noise(seeds[3], (D, 2 * RANK), D ** -0.5, 0.0625, ((0, 4),)),
        "proj_out": noise(seeds[4], (2, KV, RANK), KV ** -0.5, 0.1875),
        "queries": noise(seeds[5], (QUERIES, FEATS), (FEATS * SEQ) ** -0.5, 0.001953125, ((0, 4), (1, 4))),
    }


def reference(hidden, w_kv, grad_kv, proj_in, proj_out, queries):
    input_grad = lax.dot_general(grad_kv, w_kv, (((1,), (1,)), ((), ())), preferred_element_type=jnp.float32).astype(jnp.bfloat16)
    low_in = jnp.dot(hidden, proj_in, preferred_element_type=jnp.float32)
    key_low = jnp.dot(grad_kv[:, :KV], proj_out[0], preferred_element_type=jnp.float32)
    value_low = jnp.dot(grad_kv[:, KV:], proj_out[1], preferred_element_type=jnp.float32)
    low_out = jnp.concatenate([key_low, value_low], axis=1)
    count = hidden.shape[0] // SEQ
    left = low_in.reshape(count, SEQ, 2, RANK)
    right = low_out.reshape(count, SEQ, 2, RANK)
    per_example = jnp.einsum("esla,eslb->elab", left, right, precision=lax.Precision.HIGHEST).reshape(count, FEATS)
    scores = lax.dot_general(per_example, queries.astype(jnp.float32), (((1,), (1,)), ((), ())), precision=lax.Precision.HIGHEST, preferred_element_type=jnp.float32)
    return input_grad, scores
```

```python
import jax
import jax.numpy as jnp
from jax import lax
from jax.sharding import PartitionSpec as P

SEQ = 1024
CHUNKS = 2


def three_terms(value):
    high = lax.reduce_precision(value, 8, 7)
    rest = value - high
    middle = lax.reduce_precision(rest, 8, 7)
    low = rest - middle
    return [term.astype(jnp.bfloat16) for term in (high, middle, low)]


def low_rank_rows(rows, proj_out):
    width = rows.shape[1] // 2
    parts = [
        jnp.dot(rows[:, layer * width : (layer + 1) * width], proj_out[layer], preferred_element_type=jnp.float32)
        for layer in range(2)
    ]
    return jnp.concatenate(parts, axis=1)


def on_device(hidden, w_kv, grad_kv, proj_in, proj_out, queries):
    rows = hidden.shape[0]
    local_rows = grad_kv.shape[0]
    count = rows // SEQ
    rank = proj_out.shape[2]
    n = lax.axis_size("mp")
    me = lax.axis_index("mp")
    half = n // 2
    lower = me < half
    chunk_rows = local_rows // CHUNKS

    own = [grad_kv[c * chunk_rows : (c + 1) * chunk_rows] for c in range(CHUNKS)]
    down = [own]
    up = [own]
    for step in range(1, n):
        down_pairs = [(source, source - 1) for source in range(1, n - step + 1)]
        up_pairs = [(source, source + 1) for source in range(step - 1, n - 1)]
        down_now, up_now = [], []
        for c in range(CHUNKS):
            down_now.append(lax.ppermute(down[-1][c], "mp", down_pairs))
            up_now.append(lax.ppermute(up[-1][c], "mp", up_pairs))
        down.append(down_now)
        up.append(up_now)

    def near(step, c):
        return jnp.where(lower, down[step][c], up[step][c])

    def other(step, c):
        return jnp.where(lower, up[step][c], down[step][c])

    def near_block(step):
        return jnp.where(lower, me + step, me - step + n) % n

    output = jnp.zeros((n * CHUNKS, chunk_rows, w_kv.shape[0]), jnp.bfloat16)
    for step in range(n):
        for c in range(CHUNKS):
            if step == 0:
                chunk = own[c]
            elif step <= half:
                chunk = near(step, c)
            else:
                inside = jnp.where(lower, me + step < n, me - step >= 0)
                chunk = jnp.where(inside, near(step, c), other(n - step, c))
            product = lax.dot_general(
                chunk, w_kv, (((1,), (1,)), ((), ())), preferred_element_type=jnp.float32
            ).astype(jnp.bfloat16)
            place = near_block(step) * CHUNKS + c
            output = lax.dynamic_update_slice(output, product[None], (place, jnp.int32(0), jnp.int32(0)))
    input_grad = output.reshape(rows, w_kv.shape[0])

    partial_in = jnp.dot(hidden, proj_in, preferred_element_type=jnp.float32)
    low_in = partial_in
    for step in range(half - 1):
        pairs = [(step, step + 1), (n - 1 - step, n - 2 - step)]
        low_in = partial_in + lax.ppermute(low_in, "mp", pairs)

    low_out = jnp.zeros((n * CHUNKS, chunk_rows, 2 * rank), jnp.float32)
    for step in range(half + 1):
        for c in range(CHUNKS):
            parts = [(near_block(step), own[c] if step == 0 else near(step, c))]
            if 0 < step < half:
                parts.append((jnp.where(lower, me - step + n, me + step) % n, other(step, c)))
            for block, chunk in parts:
                low_out = lax.dynamic_update_slice(
                    low_out,
                    low_rank_rows(chunk, proj_out)[None],
                    (block * CHUNKS + c, jnp.int32(0), jnp.int32(0)),
                )
    left = low_in.reshape(count, SEQ, 2 * rank)
    right = low_out.reshape(count, SEQ, 2 * rank)
    half_sums = jnp.concatenate(
        [
            lax.dot_general(
                left[:, :, layer * rank : (layer + 1) * rank],
                right[:, :, layer * rank : (layer + 1) * rank],
                (((1,), (1,)), ((0,), (0,))),
                precision=lax.Precision.HIGHEST,
                preferred_element_type=jnp.float32,
            )
            for layer in range(2)
        ],
        axis=1,
    )

    slab = 2 * rank // n

    slabs = lax.optimization_barrier(half_sums.reshape(count, n, slab, rank).transpose(1, 0, 2, 3))

    def slab_of(index):
        return lax.dynamic_index_in_dim(slabs, index, axis=0, keepdims=False)

    first, second = half - 1, half
    mine = jnp.where((me == first) | (me == second), slab_of(me), 0.0)
    for away in range(half):
        if away > 0:
            mine = mine + lax.ppermute(
                slab_of(jnp.where(lower, first - away, second + away)),
                "mp",
                [(first, first - away), (second, second + away)],
            )
        mine = mine + lax.ppermute(
            slab_of(jnp.where(lower, second + away, first - away)),
            "mp",
            [(first, second + away), (second, first - away)],
        )

    shards = lax.axis_size("dp")
    shard = lax.axis_index("dp")
    block_rows = queries.shape[0]
    mine = mine.reshape(count, slab * rank)
    all_features = [mine] + [
        lax.ppermute(mine, "dp", [(source, (source + step) % shards) for source in range(shards)])
        for step in range(1, shards)
    ]
    stacked = jnp.concatenate(all_features, axis=0)
    terms = jnp.concatenate(three_terms(stacked), axis=0)
    products = lax.dot_general(
        terms, queries, (((1,), (1,)), ((), ())), preferred_element_type=jnp.float32
    ).reshape(3, shards, count, block_rows)
    partial_scores = products[0] + (products[1] + products[2])

    total = jnp.zeros((count, shards * block_rows), jnp.float32)
    for step in range(shards):
        back = partial_scores[step]
        if step > 0:
            back = lax.ppermute(back, "dp", [(source, (source - step) % shards) for source in range(shards)])
        total = lax.dynamic_update_slice(
            total, back, (jnp.int32(0), (shard + step) % shards * block_rows)
        )
    out_columns = shards * block_rows // n

    def columns_of(index):
        return lax.dynamic_slice(total, (jnp.int32(0), index * out_columns), (count, out_columns))

    scores = columns_of(me)
    for step in range(1, n):
        scores = scores + lax.ppermute(
            columns_of((me + step) % n), "mp", [(source, (source + step) % n) for source in range(n)]
        )
    return (input_grad, scores)


def solution(mesh):
    in_specs = (
        P(("groups", "dp"), "mp"),
        P("mp", None),
        P(("groups", "dp", "mp"), None),
        P("mp", None),
        P(),
        P("dp", "mp"),
    )
    out_specs = (P(("groups", "dp"), "mp"), P(("groups", "dp"), "mp"))
    return jax.shard_map(
        on_device, mesh=mesh, in_specs=in_specs, out_specs=out_specs, check_vma=False
    )
```

```python
import jax
import jax.numpy as jnp
from jax import lax
from jax.sharding import PartitionSpec as P

SEQ = 1024


def three_terms(value):
    high = lax.reduce_precision(value, 8, 7)
    rest = value - high
    middle = lax.reduce_precision(rest, 8, 7)
    low = rest - middle
    return [term.astype(jnp.bfloat16) for term in (high, middle, low)]


def low_rank_rows(rows, proj_out):
    width = rows.shape[1] // 2
    parts = [
        jnp.dot(rows[:, layer * width : (layer + 1) * width], proj_out[layer], preferred_element_type=jnp.float32)
        for layer in range(2)
    ]
    return jnp.concatenate(parts, axis=1)


def times_width(rows, w_kv):
    return lax.dot_general(
        rows, w_kv, (((1,), (1,)), ((), ())), preferred_element_type=jnp.float32
    ).astype(jnp.bfloat16)


def sequence_sums(low_in, low_out, rank):
    count = low_in.shape[0] // SEQ
    left = low_in.reshape(count, SEQ, 2 * rank)
    right = low_out.reshape(count, SEQ, 2 * rank)
    return jnp.concatenate(
        [
            lax.dot_general(
                left[:, :, layer * rank : (layer + 1) * rank],
                right[:, :, layer * rank : (layer + 1) * rank],
                (((1,), (1,)), ((0,), (0,))),
                precision=lax.Precision.HIGHEST,
                preferred_element_type=jnp.float32,
            )
            for layer in range(2)
        ],
        axis=1,
    )


def slabs_of(sums, n):
    count, height, rank = sums.shape
    return lax.optimization_barrier(sums.reshape(count, n, height // n, rank).transpose(1, 0, 2, 3))


def put(whole, piece, index):
    return lax.dynamic_update_slice(whole, piece[None], (index,) + (jnp.int32(0),) * piece.ndim)


def take(whole, index):
    return lax.dynamic_index_in_dim(whole, index, axis=0, keepdims=False)


def gathered(hidden, w_kv, grad_kv, proj_in, proj_out):
    n = lax.axis_size("mp")
    rank = proj_out.shape[2]
    whole = lax.all_gather(grad_kv, "mp", axis=0, tiled=True)
    input_grad = times_width(whole, w_kv)
    low_in = jnp.dot(hidden, proj_in, preferred_element_type=jnp.float32)
    sums = slabs_of(sequence_sums(low_in, low_rank_rows(whole, proj_out), rank), n)
    features = lax.psum_scatter(sums, "mp", scatter_dimension=0, tiled=False)
    return input_grad, features


def line_of_four(hidden, w_kv, grad_kv, proj_in, proj_out):
    rank = proj_out.shape[2]
    local_rows = grad_kv.shape[0]
    me = lax.axis_index("mp")
    middle = (me == 1) | (me == 2)
    exchange_pairs = [(0, 1), (1, 0), (2, 3), (3, 2)]
    across = [(0, 0), (1, 2), (2, 1), (3, 3)]
    outward = [(1, 0), (2, 3)]
    inward = [(0, 1), (3, 2)]

    beside = lax.ppermute(grad_kv, "mp", exchange_pairs)
    facing = lax.ppermute(grad_kv, "mp", across)
    own_low = low_rank_rows(grad_kv, proj_out)
    far_low = lax.ppermute(own_low, "mp", [(3, 1), (0, 2)])
    low_in = jnp.dot(hidden, proj_in, preferred_element_type=jnp.float32)

    output = jnp.zeros((4, local_rows, w_kv.shape[0]), jnp.bfloat16)
    output = put(output, times_width(grad_kv, w_kv), me)

    beside, facing, low_in, output = lax.optimization_barrier((beside, facing, low_in, output))
    second = lax.ppermute(facing, "mp", outward)
    beside_across = lax.ppermute(beside, "mp", across)
    low_in_beside = lax.ppermute(low_in, "mp", inward)

    output = put(output, times_width(beside, w_kv), me ^ 1)

    low_out = jnp.zeros((4, local_rows, 2 * rank), jnp.float32)
    low_out = put(low_out, own_low, me)
    low_out = put(low_out, low_rank_rows(beside, proj_out), me ^ 1)
    low_out = put(low_out, low_rank_rows(facing, proj_out), me ^ 3)
    low_out = put(low_out, far_low, me ^ 2)
    sums = sequence_sums(low_in + low_in_beside, low_out.reshape(4 * local_rows, 2 * rank), rank)
    slabs = slabs_of(sums, 4)
    mine = jnp.where(middle, take(slabs, me), 0.0)
    mine = mine + lax.ppermute(take(slabs, me ^ 3), "mp", [(1, 2), (2, 1)])
    mine = mine + lax.ppermute(take(slabs, me ^ 1), "mp", outward)
    mine = mine + lax.ppermute(take(slabs, me ^ 2), "mp", [(1, 3), (2, 0)])

    beside_across, second, output = lax.optimization_barrier((beside_across, second, output))
    third = lax.ppermute(beside_across, "mp", outward)
    mine, beside_across = lax.optimization_barrier((mine, beside_across))
    output = put(
        output,
        times_width(jnp.where(middle, facing, second), w_kv),
        jnp.where(middle, me ^ 3, me ^ 2),
    )
    output = put(
        output,
        times_width(jnp.where(middle, beside_across, third), w_kv),
        jnp.where(middle, me ^ 2, me ^ 3),
    )
    return output.reshape(4 * local_rows, w_kv.shape[0]), mine


def on_device(hidden, w_kv, grad_kv, proj_in, proj_out, queries):
    n = lax.axis_size("mp")
    me = lax.axis_index("mp")
    input_grad, mine = (line_of_four if n == 4 else gathered)(hidden, w_kv, grad_kv, proj_in, proj_out)
    count = mine.shape[0]

    shards = lax.axis_size("dp")
    shard = lax.axis_index("dp")
    block_rows = queries.shape[0]
    mine = mine.reshape(count, queries.shape[1])
    all_features = [mine] + [
        lax.ppermute(mine, "dp", [(source, (source + step) % shards) for source in range(shards)])
        for step in range(1, shards)
    ]
    terms = jnp.concatenate(three_terms(jnp.concatenate(all_features, axis=0)), axis=0)
    products = lax.dot_general(
        terms, queries, (((1,), (1,)), ((), ())), preferred_element_type=jnp.float32
    ).reshape(3, shards, count, block_rows)
    partial_scores = products[0] + (products[1] + products[2])

    total = jnp.zeros((count, shards * block_rows), jnp.float32)
    for step in range(shards):
        back = partial_scores[step]
        if step > 0:
            back = lax.ppermute(back, "dp", [(source, (source - step) % shards) for source in range(shards)])
        total = lax.dynamic_update_slice(
            total, back, (jnp.int32(0), (shard + step) % shards * block_rows)
        )
    out_columns = shards * block_rows // n

    def columns_of(index):
        return lax.dynamic_slice(total, (jnp.int32(0), index * out_columns), (count, out_columns))

    scores = columns_of(me)
    for step in range(1, n):
        scores = scores + lax.ppermute(
            columns_of((me + step) % n), "mp", [(source, (source + step) % n) for source in range(n)]
        )
    return (input_grad, scores)


def solution(mesh):
    in_specs = (
        P(("groups", "dp"), "mp"),
        P("mp", None),
        P(("groups", "dp", "mp"), None),
        P("mp", None),
        P(),
        P("dp", "mp"),
    )
    out_specs = (P(("groups", "dp"), "mp"), P(("groups", "dp"), "mp"))
    return jax.shard_map(
        on_device, mesh=mesh, in_specs=in_specs, out_specs=out_specs, check_vma=False
    )
```

```python
import functools

import jax
import jax.numpy as jnp
from jax import lax
from jax.experimental import pallas as pl
from jax.experimental.pallas import tpu as pltpu
from jax.sharding import PartitionSpec as P

SEQ = 1024


def three_terms(value):
    high = lax.reduce_precision(value, 8, 7)
    rest = value - high
    middle = lax.reduce_precision(rest, 8, 7)
    low = rest - middle
    return [term.astype(jnp.bfloat16) for term in (high, middle, low)]


def block_diagonal(proj_out):
    layers, width, rank = proj_out.shape
    zeros = jnp.zeros((width, rank), proj_out.dtype)
    return jnp.concatenate(
        [
            jnp.concatenate([proj_out[layer] if column == layer else zeros for column in range(layers)], axis=1)
            for layer in range(layers)
        ],
        axis=0,
    )


def times_width(rows, w_kv):
    return lax.dot_general(
        rows, w_kv, (((1,), (1,)), ((), ())), preferred_element_type=jnp.float32
    ).astype(jnp.bfloat16)


def rows_kernel(part, place, first, second, w_tile, *refs):
    out, held, arrived = refs[-3:]
    rows = held.shape[0]

    @pl.when(pl.program_id(0) == 0)
    def _():
        own_part = first.at[pl.ds(part * rows, rows)]
        for source, chosen in ((own_part, place[1] == 0), (second, place[1] != 0)):

            @pl.when(chosen)
            def _():
                copy = pltpu.make_async_copy(source, held, arrived)
                copy.start()
                copy.wait()

    out[0] = lax.dot_general(
        held[...], w_tile[...], (((1,), (1,)), ((), ())), preferred_element_type=jnp.float32
    ).astype(out.dtype)


def put_rows(output, blocks, first, second, w_kv, index, use_second=0, part=0):
    rows, depth = second.shape
    width = w_kv.shape[0]
    tile = min(width, 512)
    place = jnp.stack([index, use_second]).astype(jnp.int32)
    anywhere = pl.BlockSpec(memory_space=pl.ANY)
    earlier = [] if output is None else [output]
    return pl.pallas_call(
        functools.partial(rows_kernel, part),
        grid_spec=pltpu.PrefetchScalarGridSpec(
            num_scalar_prefetch=1,
            grid=(width // tile,),
            in_specs=[anywhere, anywhere, pl.BlockSpec((tile, depth), lambda j, place: (j, 0))] + [anywhere] * len(earlier),
            out_specs=pl.BlockSpec((1, rows, tile), lambda j, place: (place[0], part, j)),
            scratch_shapes=[pltpu.VMEM((rows, depth), first.dtype), pltpu.SemaphoreType.DMA],
        ),
        out_shape=jax.ShapeDtypeStruct((blocks, first.shape[0], width), jnp.bfloat16),
        input_output_aliases={4: 0} if earlier else {},
        compiler_params=pltpu.CompilerParams(vmem_limit_bytes=16 * 2**20),
        cost_estimate=pl.CostEstimate(flops=rows * width, bytes_accessed=2 * rows * width, transcendentals=0),
        name="input_grad_rows",
    )(place, first, second, w_kv, *earlier)


def sequence_sums(low_in, low_out, rank):
    count = low_in.shape[0] // SEQ
    left = low_in.reshape(count, SEQ, 2 * rank)
    right = low_out.reshape(count, SEQ, 2 * rank)
    return jnp.concatenate(
        [
            lax.dot_general(
                left[:, :, layer * rank : (layer + 1) * rank],
                right[:, :, layer * rank : (layer + 1) * rank],
                (((1,), (1,)), ((0,), (0,))),
                precision=lax.Precision.HIGHEST,
                preferred_element_type=jnp.float32,
            )
            for layer in range(2)
        ],
        axis=1,
    )


def slabs_of(sums, n):
    count, height, rank = sums.shape
    return lax.optimization_barrier(sums.reshape(count, n, height // n, rank).transpose(1, 0, 2, 3))


def put(whole, piece, index):
    return lax.dynamic_update_slice(whole, piece[None], (index,) + (jnp.int32(0),) * piece.ndim)


def take(whole, index):
    return lax.dynamic_index_in_dim(whole, index, axis=0, keepdims=False)


def gathered(hidden, w_kv, grad_kv, proj_in, proj_out):
    n = lax.axis_size("mp")
    rank = proj_out.shape[2]
    whole = lax.all_gather(grad_kv, "mp", axis=0, tiled=True)
    input_grad = times_width(whole, w_kv)
    low_in = jnp.dot(hidden, proj_in, preferred_element_type=jnp.float32)
    sums = slabs_of(sequence_sums(low_in, jnp.dot(whole, block_diagonal(proj_out), preferred_element_type=jnp.float32), rank), n)
    features = lax.psum_scatter(sums, "mp", scatter_dimension=0, tiled=False)
    return features, lambda total: total, lambda: input_grad


def line_of_four(hidden, w_kv, grad_kv, proj_in, proj_out):
    rank = proj_out.shape[2]
    local_rows = grad_kv.shape[0]
    me = lax.axis_index("mp")
    middle = (me == 1) | (me == 2)
    exchange_pairs = [(0, 1), (1, 0), (2, 3), (3, 2)]
    across = [(1, 2), (2, 1)]
    outward = [(1, 0), (2, 3)]
    inward = [(0, 1), (3, 2)]

    beside = lax.ppermute(grad_kv, "mp", exchange_pairs)
    facing = lax.ppermute(grad_kv, "mp", across)
    proj_both = block_diagonal(proj_out)
    own_low = jnp.dot(grad_kv, proj_both, preferred_element_type=jnp.float32)
    far_low = lax.ppermute(own_low, "mp", [(3, 1), (0, 2)])
    low_in = jnp.dot(hidden, proj_in, preferred_element_type=jnp.float32)
    output = put_rows(None, 4, grad_kv, grad_kv, w_kv, me, 0)

    beside, facing, low_in, output = lax.optimization_barrier((beside, facing, low_in, output))
    second = lax.ppermute(facing, "mp", outward)
    beside_across = lax.ppermute(beside, "mp", across)
    low_in_beside = lax.ppermute(low_in, "mp", inward)

    output = put_rows(output, 4, beside, beside, w_kv, me ^ 1, 0)

    low_out = jnp.zeros((4, local_rows, 2 * rank), jnp.float32)
    low_out = put(low_out, own_low, me)
    low_out = put(low_out, jnp.dot(beside, proj_both, preferred_element_type=jnp.float32), me ^ 1)
    low_out = put(low_out, jnp.dot(facing, proj_both, preferred_element_type=jnp.float32), me ^ 3)
    low_out = put(low_out, far_low, me ^ 2)
    sums = sequence_sums(low_in + low_in_beside, low_out.reshape(4 * local_rows, 2 * rank), rank)
    slabs = slabs_of(sums, 4)
    mine = jnp.where(middle, take(slabs, me), 0.0)
    mine = mine + lax.ppermute(take(slabs, me ^ 3), "mp", [(1, 2), (2, 1)])
    mine = mine + lax.ppermute(take(slabs, me ^ 1), "mp", outward)
    mine = mine + lax.ppermute(take(slabs, me ^ 2), "mp", [(1, 3), (2, 0)])

    beside_across, second, output = lax.optimization_barrier((beside_across, second, output))
    half = local_rows // 2
    third = [lax.ppermute(beside_across[part * half : (part + 1) * half], "mp", outward) for part in range(2)]
    mine, beside_across = lax.optimization_barrier((mine, beside_across))
    ends = jnp.logical_not(middle).astype(jnp.int32)
    output = put_rows(output, 4, facing, second, w_kv, jnp.where(middle, me ^ 3, me ^ 2), ends)
    last = jnp.where(middle, me ^ 2, me ^ 3)
    output = put_rows(output, 4, beside_across, third[0], w_kv, last, ends, 0)

    def finish(total):
        total, arrived = lax.optimization_barrier((total, third[0]))
        return total

    def rest():
        return put_rows(output, 4, beside_across, third[1], w_kv, last, ends, 1).reshape(
            4 * local_rows, w_kv.shape[0]
        )

    return mine, finish, rest


def on_device(hidden, w_kv, grad_kv, proj_in, proj_out, queries):
    n = lax.axis_size("mp")
    me = lax.axis_index("mp")
    mine, finish, rest = (line_of_four if n == 4 else gathered)(hidden, w_kv, grad_kv, proj_in, proj_out)
    count = mine.shape[0]

    shards = lax.axis_size("dp")
    shard = lax.axis_index("dp")
    block_rows = queries.shape[0]
    mine = mine.reshape(count, queries.shape[1])
    all_features = [mine] + [
        lax.ppermute(mine, "dp", [(source, (source + step) % shards) for source in range(shards)])
        for step in range(1, shards)
    ]
    terms = jnp.concatenate(three_terms(jnp.concatenate(all_features, axis=0)), axis=0)
    products = lax.dot_general(
        terms, queries, (((1,), (1,)), ((), ())), preferred_element_type=jnp.float32
    ).reshape(3, shards, count, block_rows)
    partial_scores = products[0] + (products[1] + products[2])

    total = jnp.zeros((count, shards * block_rows), jnp.float32)
    for step in range(shards):
        back = partial_scores[step]
        if step > 0:
            back = lax.ppermute(back, "dp", [(source, (source - step) % shards) for source in range(shards)])
        total = lax.dynamic_update_slice(
            total, back, (jnp.int32(0), (shard + step) % shards * block_rows)
        )
    total = finish(total)
    out_columns = shards * block_rows // n

    def columns_of(index):
        return lax.dynamic_slice(total, (jnp.int32(0), index * out_columns), (count, out_columns))

    if n == 4:
        pairs = [(source, source ^ 3) for source in range(n)]
        away = lax.ppermute(jnp.concatenate([columns_of(me ^ 3), columns_of(me ^ 1)], axis=0), "mp", pairs)
        kept = columns_of(me ^ 2) + away[count:]
        scores = columns_of(me) + away[:count]
        scores = scores + lax.ppermute(kept, "mp", [(source, source ^ 2) for source in range(n)])
    else:
        scores = columns_of(me)
        for step in range(1, n):
            scores = scores + lax.ppermute(
                columns_of((me + step) % n), "mp", [(source, (source + step) % n) for source in range(n)]
            )
    return (rest(), scores)


def solution(mesh):
    in_specs = (
        P(("groups", "dp"), "mp"),
        P("mp", None),
        P(("groups", "dp", "mp"), None),
        P("mp", None),
        P(),
        P("dp", "mp"),
    )
    out_specs = (P(("groups", "dp"), "mp"), P(("groups", "dp"), "mp"))
    return jax.shard_map(
        on_device, mesh=mesh, in_specs=in_specs, out_specs=out_specs, check_vma=False
    )
```

```python
import functools

import jax
import jax.numpy as jnp
from jax import lax
from jax.experimental import pallas as pl
from jax.experimental.pallas import tpu as pltpu
from jax.sharding import PartitionSpec as P

SEQ = 1024


def three_terms(value):
    high = lax.reduce_precision(value, 8, 7)
    rest = value - high
    middle = lax.reduce_precision(rest, 8, 7)
    low = rest - middle
    return [term.astype(jnp.bfloat16) for term in (high, middle, low)]


def block_diagonal(proj_out):
    layers, width, rank = proj_out.shape
    zeros = jnp.zeros((width, rank), proj_out.dtype)
    return jnp.concatenate(
        [
            jnp.concatenate([proj_out[layer] if column == layer else zeros for column in range(layers)], axis=1)
            for layer in range(layers)
        ],
        axis=0,
    )


def times_width(rows, w_kv):
    return lax.dot_general(
        rows, w_kv, (((1,), (1,)), ((), ())), preferred_element_type=jnp.float32
    ).astype(jnp.bfloat16)


TILE = 256
GRANT = 56 * 2**20


def first_rows_kernel(place, rows_in, w_tile, out, turned):
    turned[...] = w_tile[...].T
    out[0] = jnp.dot(rows_in[...], turned[...], preferred_element_type=jnp.float32).astype(out.dtype)


def first_rows(blocks, rows_in, w_kv, index):
    rows, depth = rows_in.shape
    width = w_kv.shape[0]
    return pl.pallas_call(
        first_rows_kernel,
        grid_spec=pltpu.PrefetchScalarGridSpec(
            num_scalar_prefetch=1,
            grid=(width // TILE,),
            in_specs=[
                pl.BlockSpec((rows, depth), lambda j, place: (0, 0)),
                pl.BlockSpec((TILE, depth), lambda j, place: (j, 0)),
            ],
            out_specs=[
                pl.BlockSpec((1, rows, TILE), lambda j, place: (place[0], 0, j)),
                pl.BlockSpec((depth, TILE), lambda j, place: (0, j)),
            ],
        ),
        out_shape=[
            jax.ShapeDtypeStruct((blocks, rows, width), jnp.bfloat16),
            jax.ShapeDtypeStruct((depth, width), w_kv.dtype),
        ],
        compiler_params=pltpu.CompilerParams(vmem_limit_bytes=GRANT),
        cost_estimate=pl.CostEstimate(
            flops=2 * rows * depth * width,
            bytes_accessed=2 * (rows * depth + 2 * depth * width + rows * width),
            transcendentals=0,
        ),
        name="input_grad_first_rows",
    )(index.reshape(1).astype(jnp.int32), rows_in, w_kv)


def rows_kernel(part, place, first, second, turned, earlier, out, held, arrived):
    rows = held.shape[0]

    @pl.when(pl.program_id(0) == 0)
    def _():
        own_part = first.at[pl.ds(part * rows, rows)]
        for source, chosen in ((own_part, place[1] == 0), (second, place[1] != 0)):

            @pl.when(chosen)
            def _():
                copy = pltpu.make_async_copy(source, held, arrived)
                copy.start()
                copy.wait()

    out[0] = jnp.dot(held[...], turned[...], preferred_element_type=jnp.float32).astype(out.dtype)


def put_rows(output, first, second, turned, index, use_second=0, part=0):
    rows, depth = second.shape
    width = turned.shape[1]
    place = jnp.stack([index, use_second]).astype(jnp.int32)
    anywhere = pl.BlockSpec(memory_space=pl.ANY)
    return pl.pallas_call(
        functools.partial(rows_kernel, part),
        grid_spec=pltpu.PrefetchScalarGridSpec(
            num_scalar_prefetch=1,
            grid=(width // TILE,),
            in_specs=[anywhere, anywhere, pl.BlockSpec((depth, TILE), lambda j, place: (0, j)), anywhere],
            out_specs=pl.BlockSpec((1, rows, TILE), lambda j, place: (place[0], part, j)),
            scratch_shapes=[pltpu.VMEM((rows, depth), first.dtype), pltpu.SemaphoreType.DMA],
        ),
        out_shape=jax.ShapeDtypeStruct(output.shape, output.dtype),
        input_output_aliases={4: 0},
        compiler_params=pltpu.CompilerParams(vmem_limit_bytes=GRANT),
        cost_estimate=pl.CostEstimate(
            flops=2 * rows * depth * width,
            bytes_accessed=2 * (rows * depth + depth * width + rows * width),
            transcendentals=0,
        ),
        name="input_grad_rows",
    )(place, first, second, turned, output)


def token_sums_kernel(me, low_in, low_in_beside, own_low, far_low, beside, facing, proj, out):
    rows = own_low.shape[0]
    rank = out.shape[2]
    total = jnp.zeros((proj.shape[1], proj.shape[1]), jnp.float32)
    for away, low_out in (
        (0, own_low[...]),
        (1, jnp.dot(beside[...], proj[...], preferred_element_type=jnp.float32)),
        (3, jnp.dot(facing[...], proj[...], preferred_element_type=jnp.float32)),
        (2, far_low[...]),
    ):
        here = pl.ds(pl.multiple_of((me[0] ^ away) * rows, rows), rows)
        total += lax.dot_general(
            low_in[here, :] + low_in_beside[here, :],
            low_out,
            (((0,), (0,)), ((), ())),
            precision=lax.Precision.HIGHEST,
            preferred_element_type=jnp.float32,
        )
    slab = out.shape[1]
    for index in range(out.shape[0]):
        layer = index * slab // rank
        out[index] = total[index * slab : (index + 1) * slab, layer * rank : (layer + 1) * rank]


def token_sums(me, low_in, low_in_beside, own_low, far_low, beside, facing, proj, rank):
    whole = pl.BlockSpec(memory_space=pltpu.VMEM)
    return pl.pallas_call(
        token_sums_kernel,
        in_specs=[pl.BlockSpec(memory_space=pltpu.SMEM)] + [whole] * 7,
        out_specs=whole,
        out_shape=jax.ShapeDtypeStruct((4, 2 * rank // 4, rank), jnp.float32),
        compiler_params=pltpu.CompilerParams(vmem_limit_bytes=GRANT),
        name="token_sums",
    )(me.reshape(1).astype(jnp.int32), low_in, low_in_beside, own_low, far_low, beside, facing, proj)


def sequence_sums(low_in, low_out, rank):
    count = low_in.shape[0] // SEQ
    left = low_in.reshape(count, SEQ, 2 * rank)
    right = low_out.reshape(count, SEQ, 2 * rank)
    return jnp.concatenate(
        [
            lax.dot_general(
                left[:, :, layer * rank : (layer + 1) * rank],
                right[:, :, layer * rank : (layer + 1) * rank],
                (((1,), (1,)), ((0,), (0,))),
                precision=lax.Precision.HIGHEST,
                preferred_element_type=jnp.float32,
            )
            for layer in range(2)
        ],
        axis=1,
    )


def slabs_of(sums, n):
    count, height, rank = sums.shape
    return lax.optimization_barrier(sums.reshape(count, n, height // n, rank).transpose(1, 0, 2, 3))


def put(whole, piece, index):
    return lax.dynamic_update_slice(whole, piece[None], (index,) + (jnp.int32(0),) * piece.ndim)


def take(whole, index):
    return lax.dynamic_index_in_dim(whole, index, axis=0, keepdims=False)


def gathered(hidden, w_kv, grad_kv, proj_in, proj_out):
    n = lax.axis_size("mp")
    rank = proj_out.shape[2]
    whole = lax.all_gather(grad_kv, "mp", axis=0, tiled=True)
    input_grad = times_width(whole, w_kv)
    low_in = jnp.dot(hidden, proj_in, preferred_element_type=jnp.float32)
    sums = slabs_of(sequence_sums(low_in, jnp.dot(whole, block_diagonal(proj_out), preferred_element_type=jnp.float32), rank), n)
    features = lax.psum_scatter(sums, "mp", scatter_dimension=0, tiled=False)
    return features, lambda total: total, lambda: input_grad


def line_of_four(hidden, w_kv, grad_kv, proj_in, proj_out):
    rank = proj_out.shape[2]
    local_rows = grad_kv.shape[0]
    me = lax.axis_index("mp")
    middle = (me == 1) | (me == 2)
    exchange_pairs = [(0, 1), (1, 0), (2, 3), (3, 2)]
    across = [(1, 2), (2, 1)]
    outward = [(1, 0), (2, 3)]
    inward = [(0, 1), (3, 2)]

    beside = lax.ppermute(grad_kv, "mp", exchange_pairs)
    facing = lax.ppermute(grad_kv, "mp", across)
    proj_both = block_diagonal(proj_out)
    own_low = jnp.dot(grad_kv, proj_both, preferred_element_type=jnp.float32)
    far_low = lax.ppermute(own_low, "mp", [(3, 1), (0, 2)])
    low_in = jnp.dot(hidden, proj_in, preferred_element_type=jnp.float32)
    output, turned = first_rows(4, grad_kv, w_kv, me)

    beside, facing, low_in, output = lax.optimization_barrier((beside, facing, low_in, output))
    second = lax.ppermute(facing, "mp", outward)
    beside_across = lax.ppermute(beside, "mp", across)
    low_in_beside = lax.ppermute(low_in, "mp", inward)
    output = put_rows(output, beside, beside, turned, me ^ 1)

    low_in_beside, far_low = lax.optimization_barrier((low_in_beside, far_low))
    if low_in.shape[0] == SEQ:
        slabs = token_sums(me, low_in, low_in_beside, own_low, far_low, beside, facing, proj_both, rank)[:, None]
    else:
        low_out = jnp.zeros((4, local_rows, 2 * rank), jnp.float32)
        low_out = put(low_out, own_low, me)
        low_out = put(low_out, jnp.dot(beside, proj_both, preferred_element_type=jnp.float32), me ^ 1)
        low_out = put(low_out, jnp.dot(facing, proj_both, preferred_element_type=jnp.float32), me ^ 3)
        low_out = put(low_out, far_low, me ^ 2)
        sums = sequence_sums(low_in + low_in_beside, low_out.reshape(4 * local_rows, 2 * rank), rank)
        slabs = slabs_of(sums, 4)
    mine = jnp.where(middle, take(slabs, me), 0.0)
    mine = mine + lax.ppermute(take(slabs, me ^ 3), "mp", [(1, 2), (2, 1)])
    mine = mine + lax.ppermute(take(slabs, me ^ 1), "mp", outward)
    mine = mine + lax.ppermute(take(slabs, me ^ 2), "mp", [(1, 3), (2, 0)])

    beside_across, second, output = lax.optimization_barrier((beside_across, second, output))
    half = local_rows // 2
    third = [lax.ppermute(beside_across[part * half : (part + 1) * half], "mp", outward) for part in range(2)]
    mine, beside_across = lax.optimization_barrier((mine, beside_across))
    ends = jnp.logical_not(middle).astype(jnp.int32)
    output = put_rows(output, facing, second, turned, jnp.where(middle, me ^ 3, me ^ 2), ends)
    last = jnp.where(middle, me ^ 2, me ^ 3)

    def finish(total):
        return lax.optimization_barrier((total, third[0], output))[0]

    def rest():
        upper = put_rows(output, beside_across, third[0], turned, last, ends, 0)
        return put_rows(upper, beside_across, third[1], turned, last, ends, 1).reshape(4 * local_rows, w_kv.shape[0])

    return mine, finish, rest


def on_device(hidden, w_kv, grad_kv, proj_in, proj_out, queries):
    n = lax.axis_size("mp")
    me = lax.axis_index("mp")
    mine, finish, rest = (line_of_four if n == 4 else gathered)(hidden, w_kv, grad_kv, proj_in, proj_out)
    count = mine.shape[0]

    shards = lax.axis_size("dp")
    shard = lax.axis_index("dp")
    block_rows = queries.shape[0]
    mine = mine.reshape(count, queries.shape[1])
    all_features = [mine] + [
        lax.ppermute(mine, "dp", [(source, (source + step) % shards) for source in range(shards)])
        for step in range(1, shards)
    ]
    terms = jnp.concatenate(three_terms(jnp.concatenate(all_features, axis=0)), axis=0)
    products = lax.dot_general(
        terms, queries, (((1,), (1,)), ((), ())), preferred_element_type=jnp.float32
    ).reshape(3, shards, count, block_rows)
    partial_scores = products[0] + (products[1] + products[2])

    total = jnp.zeros((count, shards * block_rows), jnp.float32)
    for step in range(shards):
        back = partial_scores[step]
        if step > 0:
            back = lax.ppermute(back, "dp", [(source, (source - step) % shards) for source in range(shards)])
        total = lax.dynamic_update_slice(
            total, back, (jnp.int32(0), (shard + step) % shards * block_rows)
        )
    total = finish(total)
    out_columns = shards * block_rows // n

    def columns_of(index):
        return lax.dynamic_slice(total, (jnp.int32(0), index * out_columns), (count, out_columns))

    if n == 4:
        pairs = [(source, source ^ 3) for source in range(n)]
        away = lax.ppermute(jnp.concatenate([columns_of(me ^ 3), columns_of(me ^ 1)], axis=0), "mp", pairs)
        kept = columns_of(me ^ 2) + away[count:]
        scores = columns_of(me) + away[:count]
        scores = scores + lax.ppermute(kept, "mp", [(source, source ^ 2) for source in range(n)])
    else:
        scores = columns_of(me)
        for step in range(1, n):
            scores = scores + lax.ppermute(
                columns_of((me + step) % n), "mp", [(source, (source + step) % n) for source in range(n)]
            )
    return (rest(), scores)


def solution(mesh):
    in_specs = (
        P(("groups", "dp"), "mp"),
        P("mp", None),
        P(("groups", "dp", "mp"), None),
        P("mp", None),
        P(),
        P("dp", "mp"),
    )
    out_specs = (P(("groups", "dp"), "mp"), P(("groups", "dp"), "mp"))
    return jax.shard_map(
        on_device, mesh=mesh, in_specs=in_specs, out_specs=out_specs, check_vma=False
    )
```

```python
import functools

import jax
import jax.numpy as jnp
from jax import lax
from jax.experimental import pallas as pl
from jax.experimental.pallas import tpu as pltpu
from jax.sharding import PartitionSpec as P

SEQ = 1024


def three_terms(value):
    high = lax.reduce_precision(value, 8, 7)
    rest = value - high
    middle = lax.reduce_precision(rest, 8, 7)
    low = rest - middle
    return [term.astype(jnp.bfloat16) for term in (high, middle, low)]


def block_diagonal(proj_out):
    layers, width, rank = proj_out.shape
    zeros = jnp.zeros((width, rank), proj_out.dtype)
    return jnp.concatenate(
        [
            jnp.concatenate([proj_out[layer] if column == layer else zeros for column in range(layers)], axis=1)
            for layer in range(layers)
        ],
        axis=0,
    )


def times_width(rows, w_kv):
    return lax.dot_general(
        rows, w_kv, (((1,), (1,)), ((), ())), preferred_element_type=jnp.float32
    ).astype(jnp.bfloat16)


TILE = 256
GRANT = 24 * 2**20


def rows_kernel(block, part, me, first, second, w_kv, *refs):
    out, held, turned, weight, product, arrived, fetched, written = refs[-8:]
    rows, depth = held.shape
    tiles = weight.shape[0] // TILE
    mine = me[0]
    middle = (mine == 1) | (mine == 2)
    index = [mine, mine ^ 1, jnp.where(middle, mine ^ 3, mine ^ 2), jnp.where(middle, mine ^ 2, mine ^ 3)][block]
    use_second = jnp.logical_not(middle) if block > 1 else mine < 0

    fetches = []
    for tile in range(tiles):
        here = pl.ds(tile * TILE, TILE)
        fetches.append(pltpu.make_async_copy(w_kv.at[here], weight.at[here], fetched.at[tile]))
    sources = [(first.at[pl.ds(part * rows, rows)], jnp.logical_not(use_second))]
    if block > 1:
        sources.append((second, use_second))
    for source, chosen in sources:

        @pl.when(chosen)
        def _():
            pltpu.make_async_copy(source, held, arrived).start()

    for fetch in fetches:
        fetch.start()
    pltpu.make_async_copy(second, held, arrived).wait()
    turned[...] = held[...].T
    writes = []
    for tile in range(tiles):
        here = pl.ds(tile * TILE, TILE)
        fetches[tile].wait()
        columns = jnp.dot(weight[here, :], turned[...], preferred_element_type=jnp.float32)
        product[:, here] = columns.astype(product.dtype).T
        writes.append(
            pltpu.make_async_copy(
                product.at[:, here], out.at[index, pl.ds(part * rows, rows), here], written.at[tile]
            )
        )
        writes[-1].start()
    for write in writes:
        write.wait()


def put_rows(me, block, output, first, second, w_kv, part=0):
    rows, depth = second.shape
    width = w_kv.shape[0]
    anywhere = pl.BlockSpec(memory_space=pl.ANY)
    earlier = [] if output is None else [output]
    return pl.pallas_call(
        functools.partial(rows_kernel, block, part),
        in_specs=[pl.BlockSpec(memory_space=pltpu.SMEM), anywhere, anywhere, pl.BlockSpec(memory_space=pltpu.HBM)]
        + [pl.BlockSpec(memory_space=pltpu.HBM)] * len(earlier),
        out_specs=pl.BlockSpec(memory_space=pltpu.HBM),
        scratch_shapes=[
            pltpu.VMEM((rows, depth), first.dtype),
            pltpu.VMEM((depth, rows), first.dtype),
            pltpu.VMEM((width, depth), w_kv.dtype),
            pltpu.VMEM((rows, width), jnp.bfloat16),
            pltpu.SemaphoreType.DMA,
            pltpu.SemaphoreType.DMA((width // TILE,)),
            pltpu.SemaphoreType.DMA((width // TILE,)),
        ],
        out_shape=jax.ShapeDtypeStruct((4, first.shape[0], width), jnp.bfloat16),
        input_output_aliases={4: 0} if earlier else {},
        compiler_params=pltpu.CompilerParams(vmem_limit_bytes=GRANT),
        cost_estimate=pl.CostEstimate(
            flops=2 * rows * depth * width,
            bytes_accessed=2 * (rows * depth + depth * width + rows * width),
            transcendentals=0,
        ),
        name="input_grad_rows",
    )(me.reshape(1).astype(jnp.int32), first, second, w_kv, *earlier)


def token_sums_kernel(me, low_in, low_in_beside, own_low, far_low, beside, facing, proj, out):
    rows = own_low.shape[0]
    rank = out.shape[2]
    total = jnp.zeros((proj.shape[1], proj.shape[1]), jnp.float32)
    for away, low_out in (
        (0, own_low[...]),
        (1, jnp.dot(beside[...], proj[...], preferred_element_type=jnp.float32)),
        (3, jnp.dot(facing[...], proj[...], preferred_element_type=jnp.float32)),
        (2, far_low[...]),
    ):
        here = pl.ds(pl.multiple_of((me[0] ^ away) * rows, rows), rows)
        total += lax.dot_general(
            low_in[here, :] + low_in_beside[here, :],
            low_out,
            (((0,), (0,)), ((), ())),
            precision=lax.Precision.HIGHEST,
            preferred_element_type=jnp.float32,
        )
    slab = out.shape[1]
    for index in range(out.shape[0]):
        layer = index * slab // rank
        out[index] = total[index * slab : (index + 1) * slab, layer * rank : (layer + 1) * rank]


def token_sums(me, low_in, low_in_beside, own_low, far_low, beside, facing, proj, rank):
    whole = pl.BlockSpec(memory_space=pltpu.VMEM)
    return pl.pallas_call(
        token_sums_kernel,
        in_specs=[pl.BlockSpec(memory_space=pltpu.SMEM)] + [whole] * 7,
        out_specs=whole,
        out_shape=jax.ShapeDtypeStruct((4, 2 * rank // 4, rank), jnp.float32),
        compiler_params=pltpu.CompilerParams(vmem_limit_bytes=GRANT),
        name="token_sums",
    )(me.reshape(1).astype(jnp.int32), low_in, low_in_beside, own_low, far_low, beside, facing, proj)


def sequence_sums(low_in, low_out, rank):
    count = low_in.shape[0] // SEQ
    left = low_in.reshape(count, SEQ, 2 * rank)
    right = low_out.reshape(count, SEQ, 2 * rank)
    return jnp.concatenate(
        [
            lax.dot_general(
                left[:, :, layer * rank : (layer + 1) * rank],
                right[:, :, layer * rank : (layer + 1) * rank],
                (((1,), (1,)), ((0,), (0,))),
                precision=lax.Precision.HIGHEST,
                preferred_element_type=jnp.float32,
            )
            for layer in range(2)
        ],
        axis=1,
    )


def slabs_of(sums, n):
    count, height, rank = sums.shape
    return lax.optimization_barrier(sums.reshape(count, n, height // n, rank).transpose(1, 0, 2, 3))


def put(whole, piece, index):
    return lax.dynamic_update_slice(whole, piece[None], (index,) + (jnp.int32(0),) * piece.ndim)


def take(whole, index):
    return lax.dynamic_index_in_dim(whole, index, axis=0, keepdims=False)


def gathered(hidden, w_kv, grad_kv, proj_in, proj_out):
    n = lax.axis_size("mp")
    rank = proj_out.shape[2]
    whole = lax.all_gather(grad_kv, "mp", axis=0, tiled=True)
    input_grad = times_width(whole, w_kv)
    low_in = jnp.dot(hidden, proj_in, preferred_element_type=jnp.float32)
    sums = slabs_of(sequence_sums(low_in, jnp.dot(whole, block_diagonal(proj_out), preferred_element_type=jnp.float32), rank), n)
    features = lax.psum_scatter(sums, "mp", scatter_dimension=0, tiled=False)
    return features, lambda total: total, lambda: input_grad


def line_of_four(hidden, w_kv, grad_kv, proj_in, proj_out):
    rank = proj_out.shape[2]
    local_rows = grad_kv.shape[0]
    me = lax.axis_index("mp")
    middle = (me == 1) | (me == 2)
    exchange_pairs = [(0, 1), (1, 0), (2, 3), (3, 2)]
    across = [(1, 2), (2, 1)]
    outward = [(1, 0), (2, 3)]
    inward = [(0, 1), (3, 2)]

    beside = lax.ppermute(grad_kv, "mp", exchange_pairs)
    proj_both, grad_after = lax.optimization_barrier((block_diagonal(proj_out), grad_kv))
    facing = lax.ppermute(grad_after, "mp", across)
    own_low = jnp.dot(grad_kv, proj_both, preferred_element_type=jnp.float32)
    low_in = jnp.dot(hidden, proj_in, preferred_element_type=jnp.float32)
    output = put_rows(me, 0, None, grad_kv, grad_kv, w_kv)

    beside, facing, low_in, own_low, output = lax.optimization_barrier((beside, facing, low_in, own_low, output))
    second = lax.ppermute(facing, "mp", outward)
    beside_across = lax.ppermute(beside, "mp", across)
    far_low = lax.ppermute(own_low, "mp", [(3, 1), (0, 2)])
    output = put_rows(me, 1, output, beside, beside, w_kv)
    low_in, far_low, output = lax.optimization_barrier((low_in, far_low, output))
    low_in_beside = lax.ppermute(low_in, "mp", inward)

    if low_in.shape[0] == SEQ:
        slabs = token_sums(me, low_in, low_in_beside, own_low, far_low, beside, facing, proj_both, rank)[:, None]
    else:
        low_out = jnp.zeros((4, local_rows, 2 * rank), jnp.float32)
        low_out = put(low_out, own_low, me)
        low_out = put(low_out, jnp.dot(beside, proj_both, preferred_element_type=jnp.float32), me ^ 1)
        low_out = put(low_out, jnp.dot(facing, proj_both, preferred_element_type=jnp.float32), me ^ 3)
        low_out = put(low_out, far_low, me ^ 2)
        sums = sequence_sums(low_in + low_in_beside, low_out.reshape(4 * local_rows, 2 * rank), rank)
        slabs = slabs_of(sums, 4)
    mine = jnp.where(middle, take(slabs, me), 0.0)
    mine = mine + lax.ppermute(take(slabs, me ^ 3), "mp", [(1, 2), (2, 1)])
    mine = mine + lax.ppermute(take(slabs, me ^ 1), "mp", outward)
    mine = mine + lax.ppermute(take(slabs, me ^ 2), "mp", [(1, 3), (2, 0)])

    beside_across, second, output = lax.optimization_barrier((beside_across, second, output))
    half = local_rows // 2
    third = [lax.ppermute(beside_across[part * half : (part + 1) * half], "mp", outward) for part in range(2)]
    mine, beside_across = lax.optimization_barrier((mine, beside_across))
    output = put_rows(me, 2, output, facing, second, w_kv)

    def finish(total):
        return lax.optimization_barrier((total, third[0], output))[0]

    def rest():
        upper = put_rows(me, 3, output, beside_across, third[0], w_kv, 0)
        return put_rows(me, 3, upper, beside_across, third[1], w_kv, 1).reshape(4 * local_rows, w_kv.shape[0])

    return mine, finish, rest


def on_device(hidden, w_kv, grad_kv, proj_in, proj_out, queries):
    n = lax.axis_size("mp")
    me = lax.axis_index("mp")
    mine, finish, rest = (line_of_four if n == 4 else gathered)(hidden, w_kv, grad_kv, proj_in, proj_out)
    count = mine.shape[0]

    shards = lax.axis_size("dp")
    shard = lax.axis_index("dp")
    block_rows = queries.shape[0]
    mine = mine.reshape(count, queries.shape[1])
    all_features = [mine] + [
        lax.ppermute(mine, "dp", [(source, (source + step) % shards) for source in range(shards)])
        for step in range(1, shards)
    ]
    terms = jnp.concatenate(three_terms(jnp.concatenate(all_features, axis=0)), axis=0)
    products = lax.dot_general(
        terms, queries, (((1,), (1,)), ((), ())), preferred_element_type=jnp.float32
    ).reshape(3, shards, count, block_rows)
    partial_scores = products[0] + (products[1] + products[2])

    total = jnp.zeros((count, shards * block_rows), jnp.float32)
    for step in range(shards):
        back = partial_scores[step]
        if step > 0:
            back = lax.ppermute(back, "dp", [(source, (source - step) % shards) for source in range(shards)])
        total = lax.dynamic_update_slice(
            total, back, (jnp.int32(0), (shard + step) % shards * block_rows)
        )
    total = finish(total)
    out_columns = shards * block_rows // n

    def columns_of(index):
        return lax.dynamic_slice(total, (jnp.int32(0), index * out_columns), (count, out_columns))

    if n == 4:
        pairs = [(source, source ^ 3) for source in range(n)]
        away = lax.ppermute(jnp.concatenate([columns_of(me ^ 3), columns_of(me ^ 1)], axis=0), "mp", pairs)
        kept = columns_of(me ^ 2) + away[count:]
        scores = columns_of(me) + away[:count]
        scores = scores + lax.ppermute(kept, "mp", [(source, source ^ 2) for source in range(n)])
    else:
        scores = columns_of(me)
        for step in range(1, n):
            scores = scores + lax.ppermute(
                columns_of((me + step) % n), "mp", [(source, (source + step) % n) for source in range(n)]
            )
    return (rest(), scores)


def solution(mesh):
    in_specs = (
        P(("groups", "dp"), "mp"),
        P("mp", None),
        P(("groups", "dp", "mp"), None),
        P("mp", None),
        P(),
        P("dp", "mp"),
    )
    out_specs = (P(("groups", "dp"), "mp"), P(("groups", "dp"), "mp"))
    return jax.shard_map(
        on_device, mesh=mesh, in_specs=in_specs, out_specs=out_specs, check_vma=False
    )
```

```python
import functools

import jax
import jax.numpy as jnp
from jax import lax
from jax.experimental import pallas as pl
from jax.experimental.pallas import tpu as pltpu
from jax.sharding import PartitionSpec as P

SEQ = 1024


def three_terms(value):
    high = lax.reduce_precision(value, 8, 7)
    rest = value - high
    middle = lax.reduce_precision(rest, 8, 7)
    low = rest - middle
    return [term.astype(jnp.bfloat16) for term in (high, middle, low)]


def block_diagonal(proj_out):
    layers, width, rank = proj_out.shape
    zeros = jnp.zeros((width, rank), proj_out.dtype)
    return jnp.concatenate(
        [
            jnp.concatenate([proj_out[layer] if column == layer else zeros for column in range(layers)], axis=1)
            for layer in range(layers)
        ],
        axis=0,
    )


def times_width(rows, w_kv):
    return lax.dot_general(
        rows, w_kv, (((1,), (1,)), ((), ())), preferred_element_type=jnp.float32
    ).astype(jnp.bfloat16)


FETCH = 256
TILE = 512
GRANT = 24 * 2**20


def rows_kernel(block, start, count, me, *refs):
    firsts, seconds = refs[:count], refs[count : 2 * count]
    w_kv = refs[2 * count]
    out, held, weight, product, arrived, fetched, written = refs[-7:]
    mine = me[0]
    middle = (mine == 1) | (mine == 2)
    index = [mine, mine ^ 1, jnp.where(middle, mine ^ 3, mine ^ 2), jnp.where(middle, mine ^ 2, mine ^ 3)][block]
    use_second = jnp.logical_not(middle) if block > 1 else mine < 0

    fetches = []
    for piece in range(weight.shape[0] // FETCH):
        here = pl.ds(piece * FETCH, FETCH)
        fetches.append(pltpu.make_async_copy(w_kv.at[here], weight.at[here], fetched.at[piece]))
    loads = []
    filled = 0
    for part in range(count):
        rows = firsts[part].shape[0]
        here = held.at[pl.ds(filled, rows)]
        filled += rows
        loads.append(pltpu.make_async_copy(firsts[part], here, arrived.at[part]))
        late = pltpu.make_async_copy(seconds[part], here, arrived.at[part])
        if block > 1:
            pl.when(jnp.logical_not(use_second))(loads[-1].start)
            pl.when(use_second)(late.start)
        else:
            loads[-1].start()
    for fetch in fetches:
        fetch.start()
    for load in loads:
        load.wait()
    writes = []
    for tile in range(weight.shape[0] // TILE):
        here = pl.ds(tile * TILE, TILE)
        for piece in range(tile * TILE // FETCH, (tile + 1) * TILE // FETCH):
            fetches[piece].wait()
        product[:, here] = lax.dot_general(
            held[...], weight[here, :], (((1,), (1,)), ((), ())), preferred_element_type=jnp.float32
        ).astype(product.dtype)
        writes.append(
            pltpu.make_async_copy(
                product.at[:, here], out.at[index, pl.ds(start, product.shape[0]), here], written.at[tile]
            )
        )
        writes[-1].start()
    for write in writes:
        write.wait()


def put_rows(me, block, output, firsts, seconds, w_kv, block_rows, start=0):
    count = len(firsts)
    depth = firsts[0].shape[1]
    rows = sum(part.shape[0] for part in firsts)
    width = w_kv.shape[0]
    earlier = [] if output is None else [output]
    return pl.pallas_call(
        functools.partial(rows_kernel, block, start, count),
        in_specs=[pl.BlockSpec(memory_space=pltpu.SMEM)]
        + [pl.BlockSpec(memory_space=pl.ANY)] * (2 * count)
        + [pl.BlockSpec(memory_space=pltpu.HBM)] * (1 + len(earlier)),
        out_specs=pl.BlockSpec(memory_space=pltpu.HBM),
        scratch_shapes=[
            pltpu.VMEM((rows, depth), firsts[0].dtype),
            pltpu.VMEM((width, depth), w_kv.dtype),
            pltpu.VMEM((rows, width), jnp.bfloat16),
            pltpu.SemaphoreType.DMA((count,)),
            pltpu.SemaphoreType.DMA((width // FETCH,)),
            pltpu.SemaphoreType.DMA((width // TILE,)),
        ],
        out_shape=jax.ShapeDtypeStruct((4, block_rows, width), jnp.bfloat16),
        input_output_aliases={2 * count + 2: 0} if earlier else {},
        compiler_params=pltpu.CompilerParams(vmem_limit_bytes=GRANT),
        cost_estimate=pl.CostEstimate(flops=rows * width, bytes_accessed=rows * width, transcendentals=0),
        name="input_grad_rows",
    )(me.reshape(1).astype(jnp.int32), *firsts, *seconds, w_kv, *earlier)


def token_sums_kernel(me, low_in, low_in_beside, own_low, beside_low, facing_low, far_low, out):
    rows = own_low.shape[0]
    rank = out.shape[2]
    total = jnp.zeros((own_low.shape[1], own_low.shape[1]), jnp.float32)
    for away, low_out in (
        (0, own_low[...]),
        (1, beside_low[...]),
        (3, facing_low[...]),
        (2, far_low[...]),
    ):
        here = pl.ds(pl.multiple_of((me[0] ^ away) * rows, rows), rows)
        total += lax.dot_general(
            low_in[here, :] + low_in_beside[here, :],
            low_out,
            (((0,), (0,)), ((), ())),
            precision=lax.Precision.HIGHEST,
            preferred_element_type=jnp.float32,
        )
    slab = out.shape[1]
    for index in range(out.shape[0]):
        layer = index * slab // rank
        out[index] = total[index * slab : (index + 1) * slab, layer * rank : (layer + 1) * rank]


def token_sums(me, low_in, low_in_beside, own_low, beside_low, facing_low, far_low, rank):
    whole = pl.BlockSpec(memory_space=pltpu.VMEM)
    return pl.pallas_call(
        token_sums_kernel,
        in_specs=[pl.BlockSpec(memory_space=pltpu.SMEM)] + [whole] * 6,
        out_specs=whole,
        out_shape=jax.ShapeDtypeStruct((4, 2 * rank // 4, rank), jnp.float32),
        compiler_params=pltpu.CompilerParams(vmem_limit_bytes=GRANT),
        name="token_sums",
    )(me.reshape(1).astype(jnp.int32), low_in, low_in_beside, own_low, beside_low, facing_low, far_low)


def sequence_sums(low_in, low_out, rank):
    count = low_in.shape[0] // SEQ
    left = low_in.reshape(count, SEQ, 2 * rank)
    right = low_out.reshape(count, SEQ, 2 * rank)
    return jnp.concatenate(
        [
            lax.dot_general(
                left[:, :, layer * rank : (layer + 1) * rank],
                right[:, :, layer * rank : (layer + 1) * rank],
                (((1,), (1,)), ((0,), (0,))),
                precision=lax.Precision.HIGHEST,
                preferred_element_type=jnp.float32,
            )
            for layer in range(2)
        ],
        axis=1,
    )


def slabs_of(sums, n):
    count, height, rank = sums.shape
    return lax.optimization_barrier(sums.reshape(count, n, height // n, rank).transpose(1, 0, 2, 3))


def put(whole, piece, index):
    return lax.dynamic_update_slice(whole, piece[None], (index,) + (jnp.int32(0),) * piece.ndim)


def take(whole, index):
    return lax.dynamic_index_in_dim(whole, index, axis=0, keepdims=False)


def gathered(hidden, w_kv, grad_kv, proj_in, proj_out):
    n = lax.axis_size("mp")
    rank = proj_out.shape[2]
    whole = lax.all_gather(grad_kv, "mp", axis=0, tiled=True)
    input_grad = times_width(whole, w_kv)
    low_in = jnp.dot(hidden, proj_in, preferred_element_type=jnp.float32)
    sums = slabs_of(sequence_sums(low_in, jnp.dot(whole, block_diagonal(proj_out), preferred_element_type=jnp.float32), rank), n)
    features = lax.psum_scatter(sums, "mp", scatter_dimension=0, tiled=False)
    return features, lambda scores: scores, lambda: input_grad


def line_of_four(hidden, w_kv, grad_kv, proj_in, proj_out):
    rank = proj_out.shape[2]
    local_rows = grad_kv.shape[0]
    cut = local_rows * 5 // 8 // 16 * 16
    me = lax.axis_index("mp")
    middle = (me == 1) | (me == 2)
    exchange_pairs = [(0, 1), (1, 0), (2, 3), (3, 2)]
    across = [(1, 2), (2, 1)]
    outward = [(1, 0), (2, 3)]
    inward = [(0, 1), (3, 2)]
    tied = lax.optimization_barrier

    def pieces(rows):
        return [rows[:cut], rows[cut:]]

    def low_rank(rows):
        return jnp.dot(rows, proj_both, preferred_element_type=jnp.float32)

    beside = lax.ppermute(grad_kv, "mp", exchange_pairs)
    facing = [lax.ppermute(part, "mp", across) for part in pieces(grad_kv)]
    proj_both = tied(block_diagonal(proj_out))
    own_low = low_rank(grad_kv)
    low_in = jnp.dot(hidden, proj_in, preferred_element_type=jnp.float32)

    facing[0], own_low, low_in = tied((facing[0], own_low, low_in))
    second = [lax.ppermute(facing[0], "mp", outward)]
    far_low = lax.ppermute(own_low, "mp", [(3, 1), (0, 2)])
    low_in_beside = lax.ppermute(low_in, "mp", inward)
    output = put_rows(me, 0, None, [grad_kv], [grad_kv], w_kv, local_rows)

    beside, facing[1], output = tied((beside, facing[1], output))
    second.append(lax.ppermute(facing[1], "mp", outward))
    beside_across = [lax.ppermute(part, "mp", across) for part in pieces(beside)]
    output = put_rows(me, 1, output, [beside], [beside], w_kv, local_rows)

    beside_across[0], second[0], far_low, low_in_beside, output = tied(
        (beside_across[0], second[0], far_low, low_in_beside, output)
    )
    third = [lax.ppermute(beside_across[0], "mp", outward)]

    beside_low = low_rank(beside)
    facing_low = jnp.concatenate([low_rank(part) for part in facing], axis=0)
    if low_in.shape[0] == SEQ:
        slabs = token_sums(me, low_in, low_in_beside, own_low, beside_low, facing_low, far_low, rank)[:, None]
    else:
        low_out = jnp.zeros((4, local_rows, 2 * rank), jnp.float32)
        for away, rows in ((0, own_low), (1, beside_low), (3, facing_low), (2, far_low)):
            low_out = put(low_out, rows, me ^ away)
        sums = sequence_sums(low_in + low_in_beside, low_out.reshape(4 * local_rows, 2 * rank), rank)
        slabs = slabs_of(sums, 4)
    slabs_across = lax.ppermute(slabs, "mp", across)

    beside_across[1], second[1], slabs_across = tied((beside_across[1], second[1], slabs_across))
    third.append(lax.ppermute(beside_across[1], "mp", outward))
    slabs = slabs + slabs_across
    mine = lax.ppermute(take(slabs, me ^ 2), "mp", [(2, 0), (1, 3)])
    mine = jnp.where(middle, take(slabs, me), mine)
    output = put_rows(me, 2, output, facing, second, w_kv, local_rows)

    def finish(scores):
        return tied((scores, third[0], output))[0]

    def rest():
        done = output
        for part in range(2):
            done = put_rows(me, 3, done, [beside_across[part]], [third[part]], w_kv, local_rows, part * cut)
        return done.reshape(4 * local_rows, w_kv.shape[0])

    return mine, finish, rest


def on_device(hidden, w_kv, grad_kv, proj_in, proj_out, queries):
    n = lax.axis_size("mp")
    me = lax.axis_index("mp")
    mine, finish, rest = (line_of_four if n == 4 else gathered)(hidden, w_kv, grad_kv, proj_in, proj_out)
    count = mine.shape[0]

    shards = lax.axis_size("dp")
    shard = lax.axis_index("dp")
    block_rows = queries.shape[0]
    mine = mine.reshape(count, queries.shape[1])
    all_features = [mine] + [
        lax.ppermute(mine, "dp", [(source, (source + step) % shards) for source in range(shards)])
        for step in range(1, shards)
    ]
    terms = jnp.concatenate(three_terms(jnp.concatenate(all_features, axis=0)), axis=0)
    products = lax.dot_general(
        terms, queries, (((1,), (1,)), ((), ())), preferred_element_type=jnp.float32
    ).reshape(3, shards, count, block_rows)
    partial_scores = finish(products[0] + (products[1] + products[2]))

    total = jnp.zeros((count, shards * block_rows), jnp.float32)
    for step in range(shards):
        back = partial_scores[step]
        if step > 0:
            back = lax.ppermute(back, "dp", [(source, (source - step) % shards) for source in range(shards)])
        total = lax.dynamic_update_slice(
            total, back, (jnp.int32(0), (shard + step) % shards * block_rows)
        )
    out_columns = shards * block_rows // n

    def columns_of(index):
        return lax.dynamic_slice(total, (jnp.int32(0), index * out_columns), (count, out_columns))

    if n == 4:
        pairs = [(source, source ^ 3) for source in range(n)]
        away = lax.ppermute(jnp.concatenate([columns_of(me ^ 3), columns_of(me ^ 1)], axis=0), "mp", pairs)
        kept = columns_of(me ^ 2) + away[count:]
        scores = columns_of(me) + away[:count]
        scores = scores + lax.ppermute(kept, "mp", [(source, source ^ 2) for source in range(n)])
    else:
        scores = columns_of(me)
        for step in range(1, n):
            scores = scores + lax.ppermute(
                columns_of((me + step) % n), "mp", [(source, (source + step) % n) for source in range(n)]
            )
    return (rest(), scores)


def solution(mesh):
    in_specs = (
        P(("groups", "dp"), "mp"),
        P("mp", None),
        P(("groups", "dp", "mp"), None),
        P("mp", None),
        P(),
        P("dp", "mp"),
    )
    out_specs = (P(("groups", "dp"), "mp"), P(("groups", "dp"), "mp"))
    return jax.shard_map(
        on_device, mesh=mesh, in_specs=in_specs, out_specs=out_specs, check_vma=False
    )
```

```python
import functools

import jax
import jax.numpy as jnp
from jax import lax
from jax.experimental import pallas as pl
from jax.experimental.pallas import tpu as pltpu
from jax.sharding import PartitionSpec as P

SEQ = 1024


def three_terms(value):
    high = lax.reduce_precision(value, 8, 7)
    rest = value - high
    middle = lax.reduce_precision(rest, 8, 7)
    low = rest - middle
    return [term.astype(jnp.bfloat16) for term in (high, middle, low)]


def block_diagonal(proj_out):
    layers, width, rank = proj_out.shape
    zeros = jnp.zeros((width, rank), proj_out.dtype)
    return jnp.concatenate(
        [
            jnp.concatenate([proj_out[layer] if column == layer else zeros for column in range(layers)], axis=1)
            for layer in range(layers)
        ],
        axis=0,
    )


def times_width(rows, w_kv):
    return lax.dot_general(
        rows, w_kv, (((1,), (1,)), ((), ())), preferred_element_type=jnp.float32
    ).astype(jnp.bfloat16)


FETCH = 256
TILE = 512
GRANT = 24 * 2**20


def rows_kernel(block, start, count, me, *refs):
    firsts, seconds = refs[:count], refs[count : 2 * count]
    w_kv = refs[2 * count]
    out, held, weight, product, arrived, fetched, written = refs[-7:]
    mine = me[0]
    middle = (mine == 1) | (mine == 2)
    index = [mine, mine ^ 1, jnp.where(middle, mine ^ 3, mine ^ 2), jnp.where(middle, mine ^ 2, mine ^ 3)][block]
    use_second = jnp.logical_not(middle) if block > 1 else mine < 0

    fetches = []
    for piece in range(weight.shape[0] // FETCH):
        here = pl.ds(piece * FETCH, FETCH)
        fetches.append(pltpu.make_async_copy(w_kv.at[here], weight.at[here], fetched.at[piece]))
    loads = []
    filled = 0
    for part in range(count):
        rows = firsts[part].shape[0]
        here = held.at[pl.ds(filled, rows)]
        filled += rows
        loads.append(pltpu.make_async_copy(firsts[part], here, arrived.at[part]))
        late = pltpu.make_async_copy(seconds[part], here, arrived.at[part])
        if block > 1:
            pl.when(jnp.logical_not(use_second))(loads[-1].start)
            pl.when(use_second)(late.start)
        else:
            loads[-1].start()
    for fetch in fetches:
        fetch.start()
    for load in loads:
        load.wait()
    writes = []
    for tile in range(weight.shape[0] // TILE):
        here = pl.ds(tile * TILE, TILE)
        for piece in range(tile * TILE // FETCH, (tile + 1) * TILE // FETCH):
            fetches[piece].wait()
        product[:, here] = lax.dot_general(
            held[...], weight[here, :], (((1,), (1,)), ((), ())), preferred_element_type=jnp.float32
        ).astype(product.dtype)
        writes.append(
            pltpu.make_async_copy(
                product.at[:, here], out.at[index, pl.ds(start, product.shape[0]), here], written.at[tile]
            )
        )
        writes[-1].start()
    for write in writes:
        write.wait()


def put_rows(me, block, output, firsts, seconds, w_kv, block_rows, start=0):
    count = len(firsts)
    depth = firsts[0].shape[1]
    rows = sum(part.shape[0] for part in firsts)
    width = w_kv.shape[0]
    earlier = [] if output is None else [output]
    return pl.pallas_call(
        functools.partial(rows_kernel, block, start, count),
        in_specs=[pl.BlockSpec(memory_space=pltpu.SMEM)]
        + [pl.BlockSpec(memory_space=pl.ANY)] * (2 * count)
        + [pl.BlockSpec(memory_space=pltpu.HBM)] * (1 + len(earlier)),
        out_specs=pl.BlockSpec(memory_space=pltpu.HBM),
        scratch_shapes=[
            pltpu.VMEM((rows, depth), firsts[0].dtype),
            pltpu.VMEM((width, depth), w_kv.dtype),
            pltpu.VMEM((rows, width), jnp.bfloat16),
            pltpu.SemaphoreType.DMA((count,)),
            pltpu.SemaphoreType.DMA((width // FETCH,)),
            pltpu.SemaphoreType.DMA((width // TILE,)),
        ],
        out_shape=jax.ShapeDtypeStruct((4, block_rows, width), jnp.bfloat16),
        input_output_aliases={2 * count + 2: 0} if earlier else {},
        compiler_params=pltpu.CompilerParams(vmem_limit_bytes=GRANT),
        cost_estimate=pl.CostEstimate(flops=rows * width, bytes_accessed=rows * width, transcendentals=0),
        name="input_grad_rows",
    )(me.reshape(1).astype(jnp.int32), *firsts, *seconds, w_kv, *earlier)


def token_sums_kernel(me, low_in, low_in_beside, own_low, beside_low, facing_low, far_low, note, out):
    rows = own_low.shape[0]
    rank = out.shape[2]
    total = jnp.zeros((own_low.shape[1], own_low.shape[1]), jnp.float32)
    for away, low_out in (
        (0, own_low[...]),
        (1, beside_low[...]),
        (3, facing_low[...]),
        (2, far_low[...]),
    ):
        here = pl.ds(pl.multiple_of((me[0] ^ away) * rows, rows), rows)
        total += lax.dot_general(
            low_in[here, :] + low_in_beside[here, :],
            low_out,
            (((0,), (0,)), ((), ())),
            precision=lax.Precision.HIGHEST,
            preferred_element_type=jnp.float32,
        )
    slab = out.shape[1]
    for index in range(out.shape[0]):
        layer = index * slab // rank
        out[index] = total[index * slab : (index + 1) * slab, layer * rank : (layer + 1) * rank]


def token_sums(me, low_in, low_in_beside, own_low, beside_low, facing_low, far_low, note, rank):
    whole = pl.BlockSpec(memory_space=pltpu.VMEM)
    return pl.pallas_call(
        token_sums_kernel,
        in_specs=[pl.BlockSpec(memory_space=pltpu.SMEM)] + [whole] * 7,
        out_specs=whole,
        out_shape=jax.ShapeDtypeStruct((4, 2 * rank // 4, rank), jnp.float32),
        compiler_params=pltpu.CompilerParams(vmem_limit_bytes=GRANT),
        name="token_sums",
    )(me.reshape(1).astype(jnp.int32), low_in, low_in_beside, own_low, beside_low, facing_low, far_low, note)


def sequence_sums(low_in, low_out, rank):
    count = low_in.shape[0] // SEQ
    left = low_in.reshape(count, SEQ, 2 * rank)
    right = low_out.reshape(count, SEQ, 2 * rank)
    return jnp.concatenate(
        [
            lax.dot_general(
                left[:, :, layer * rank : (layer + 1) * rank],
                right[:, :, layer * rank : (layer + 1) * rank],
                (((1,), (1,)), ((0,), (0,))),
                precision=lax.Precision.HIGHEST,
                preferred_element_type=jnp.float32,
            )
            for layer in range(2)
        ],
        axis=1,
    )


def slabs_of(sums, n):
    count, height, rank = sums.shape
    return lax.optimization_barrier(sums.reshape(count, n, height // n, rank).transpose(1, 0, 2, 3))


def put(whole, piece, index):
    return lax.dynamic_update_slice(whole, piece[None], (index,) + (jnp.int32(0),) * piece.ndim)


def take(whole, index):
    return lax.dynamic_index_in_dim(whole, index, axis=0, keepdims=False)


def gathered(hidden, w_kv, grad_kv, proj_in, proj_out):
    n = lax.axis_size("mp")
    rank = proj_out.shape[2]
    whole = lax.all_gather(grad_kv, "mp", axis=0, tiled=True)
    input_grad = times_width(whole, w_kv)
    low_in = jnp.dot(hidden, proj_in, preferred_element_type=jnp.float32)
    sums = slabs_of(sequence_sums(low_in, jnp.dot(whole, block_diagonal(proj_out), preferred_element_type=jnp.float32), rank), n)
    features = lax.psum_scatter(sums, "mp", scatter_dimension=0, tiled=False)
    return features, lambda scores: scores, lambda: input_grad


def line_of_four(hidden, w_kv, grad_kv, proj_in, proj_out):
    rank = proj_out.shape[2]
    local_rows = grad_kv.shape[0]
    me = lax.axis_index("mp")
    middle = (me == 1) | (me == 2)
    exchange_pairs = [(0, 1), (1, 0), (2, 3), (3, 2)]
    across = [(1, 2), (2, 1)]
    outward = [(1, 0), (2, 3)]
    inward = [(0, 1), (3, 2)]
    tied = lax.optimization_barrier

    def low_rank(rows):
        return jnp.dot(rows, proj_both, preferred_element_type=jnp.float32)

    facing = lax.ppermute(grad_kv, "mp", across)
    beside = lax.ppermute(grad_kv, "mp", exchange_pairs)
    proj_both = tied(block_diagonal(proj_out))
    own_low = low_rank(grad_kv)
    low_in = jnp.dot(hidden, proj_in, preferred_element_type=jnp.float32)
    output = put_rows(me, 0, None, [grad_kv], [grad_kv], w_kv, local_rows)

    beside, facing, low_in, output = tied((beside, facing, low_in, output))
    beside_across = lax.ppermute(beside, "mp", across)
    second = lax.ppermute(facing, "mp", outward)
    output = put_rows(me, 1, output, [beside], [beside], w_kv, local_rows)
    low_in, output = tied((low_in, output))
    low_in_beside = lax.ppermute(low_in, "mp", inward)

    beside_low = low_rank(beside)
    facing_low = low_rank(facing)

    beside_across, second, low_in_beside, output = tied((beside_across, second, low_in_beside, output))
    third = lax.ppermute(beside_across, "mp", outward)
    shards = lax.axis_size("dp")
    note = lax.ppermute(low_in_beside[:1], "dp", [(source, (source + 1) % shards) for source in range(shards)])

    far_low = low_rank(beside_across)
    if low_in.shape[0] == SEQ:
        slabs = token_sums(me, low_in, low_in_beside, own_low, beside_low, facing_low, far_low, note, rank)[:, None]
    else:
        low_out = jnp.zeros((4, local_rows, 2 * rank), jnp.float32)
        for away, rows in ((0, own_low), (1, beside_low), (3, facing_low), (2, far_low)):
            low_out = put(low_out, rows, me ^ away)
        sums = sequence_sums(low_in + low_in_beside, low_out.reshape(4 * local_rows, 2 * rank), rank)
        slabs = slabs_of(sums, 4)
    slabs = slabs + lax.ppermute(slabs, "mp", across)
    mine = lax.ppermute(take(slabs, me ^ 2), "mp", [(2, 0), (1, 3)])
    mine = jnp.where(middle, take(slabs, me), mine)
    output = put_rows(me, 2, output, [facing], [second], w_kv, local_rows)

    def finish(scores):
        return tied((scores, output))[0]

    def rest():
        done = put_rows(me, 3, output, [beside_across], [third], w_kv, local_rows)
        return done.reshape(4 * local_rows, w_kv.shape[0])

    return mine, finish, rest


def on_device(hidden, w_kv, grad_kv, proj_in, proj_out, queries):
    n = lax.axis_size("mp")
    me = lax.axis_index("mp")
    mine, finish, rest = (line_of_four if n == 4 else gathered)(hidden, w_kv, grad_kv, proj_in, proj_out)
    count = mine.shape[0]

    shards = lax.axis_size("dp")
    shard = lax.axis_index("dp")
    block_rows = queries.shape[0]
    mine = mine.reshape(count, queries.shape[1])
    all_features = [mine] + [
        lax.ppermute(mine, "dp", [(source, (source + step) % shards) for source in range(shards)])
        for step in range(1, shards)
    ]
    terms = jnp.concatenate(three_terms(jnp.concatenate(all_features, axis=0)), axis=0)
    products = lax.dot_general(
        terms, queries, (((1,), (1,)), ((), ())), preferred_element_type=jnp.float32
    ).reshape(3, shards, count, block_rows)
    partial_scores = finish(products[0] + (products[1] + products[2]))

    if shards == n:
        scores = jnp.zeros((count, block_rows), jnp.float32)
        for step in range(n):
            pairs = [
                (q * n + slab, (slab + step) % n * n + q) for q in range(n) for slab in range(n)
            ]
            row = take(partial_scores, (shard - me - step + 2 * n) % n)
            scores = scores + lax.ppermute(row, ("dp", "mp"), pairs)
        return (rest(), scores)

    total = jnp.zeros((count, shards * block_rows), jnp.float32)
    for step in range(shards):
        back = partial_scores[step]
        if step > 0:
            back = lax.ppermute(back, "dp", [(source, (source - step) % shards) for source in range(shards)])
        total = lax.dynamic_update_slice(
            total, back, (jnp.int32(0), (shard + step) % shards * block_rows)
        )
    out_columns = shards * block_rows // n

    def columns_of(index):
        return lax.dynamic_slice(total, (jnp.int32(0), index * out_columns), (count, out_columns))

    scores = columns_of(me)
    for step in range(1, n):
        scores = scores + lax.ppermute(
            columns_of((me + step) % n), "mp", [(source, (source + step) % n) for source in range(n)]
        )
    return (rest(), scores)


def solution(mesh):
    in_specs = (
        P(("groups", "dp"), "mp"),
        P("mp", None),
        P(("groups", "dp", "mp"), None),
        P("mp", None),
        P(),
        P("dp", "mp"),
    )
    out_specs = (P(("groups", "dp"), "mp"), P(("groups", "dp"), "mp"))
    return jax.shard_map(
        on_device, mesh=mesh, in_specs=in_specs, out_specs=out_specs, check_vma=False
    )
```

```python
import functools

import jax
import jax.numpy as jnp
from jax import lax
from jax.experimental import pallas as pl
from jax.experimental.pallas import tpu as pltpu
from jax.sharding import PartitionSpec as P

SEQ = 1024


def three_terms(value):
    high = lax.reduce_precision(value, 8, 7)
    rest = value - high
    middle = lax.reduce_precision(rest, 8, 7)
    low = rest - middle
    return [term.astype(jnp.bfloat16) for term in (high, middle, low)]


def block_diagonal(proj_out):
    layers, width, rank = proj_out.shape
    zeros = jnp.zeros((width, rank), proj_out.dtype)
    return jnp.concatenate(
        [
            jnp.concatenate([proj_out[layer] if column == layer else zeros for column in range(layers)], axis=1)
            for layer in range(layers)
        ],
        axis=0,
    )


def times_width(rows, w_kv):
    return lax.dot_general(
        rows, w_kv, (((1,), (1,)), ((), ())), preferred_element_type=jnp.float32
    ).astype(jnp.bfloat16)


FETCH = 256
TILE = 512
GRANT = 24 * 2**20


def rows_kernel(block, start, count, me, *refs):
    firsts, seconds = refs[:count], refs[count : 2 * count]
    w_kv = refs[2 * count]
    out, held, weight, product, arrived, fetched, written = refs[-7:]
    mine = me[0]
    middle = (mine == 1) | (mine == 2)
    index = [mine, mine ^ 1, jnp.where(middle, mine ^ 3, mine ^ 2), jnp.where(middle, mine ^ 2, mine ^ 3)][block]
    use_second = jnp.logical_not(middle) if block > 1 else mine < 0

    fetches = []
    for piece in range(weight.shape[0] // FETCH):
        here = pl.ds(piece * FETCH, FETCH)
        fetches.append(pltpu.make_async_copy(w_kv.at[here], weight.at[here], fetched.at[piece]))
    loads = []
    filled = 0
    for part in range(count):
        rows = firsts[part].shape[0]
        here = held.at[pl.ds(filled, rows)]
        filled += rows
        loads.append(pltpu.make_async_copy(firsts[part], here, arrived.at[part]))
        late = pltpu.make_async_copy(seconds[part], here, arrived.at[part])
        if block > 1:
            pl.when(jnp.logical_not(use_second))(loads[-1].start)
            pl.when(use_second)(late.start)
        else:
            loads[-1].start()
    for fetch in fetches:
        fetch.start()
    for load in loads:
        load.wait()
    writes = []
    for tile in range(weight.shape[0] // TILE):
        here = pl.ds(tile * TILE, TILE)
        for piece in range(tile * TILE // FETCH, (tile + 1) * TILE // FETCH):
            fetches[piece].wait()
        product[:, here] = lax.dot_general(
            held[...], weight[here, :], (((1,), (1,)), ((), ())), preferred_element_type=jnp.float32
        ).astype(product.dtype)
        writes.append(
            pltpu.make_async_copy(
                product.at[:, here], out.at[index, pl.ds(start, product.shape[0]), here], written.at[tile]
            )
        )
        writes[-1].start()
    for write in writes:
        write.wait()


def put_rows(me, block, output, firsts, seconds, w_kv, block_rows, start=0):
    count = len(firsts)
    depth = firsts[0].shape[1]
    rows = sum(part.shape[0] for part in firsts)
    width = w_kv.shape[0]
    earlier = [] if output is None else [output]
    return pl.pallas_call(
        functools.partial(rows_kernel, block, start, count),
        in_specs=[pl.BlockSpec(memory_space=pltpu.SMEM)]
        + [pl.BlockSpec(memory_space=pl.ANY)] * (2 * count)
        + [pl.BlockSpec(memory_space=pltpu.HBM)] * (1 + len(earlier)),
        out_specs=pl.BlockSpec(memory_space=pltpu.HBM),
        scratch_shapes=[
            pltpu.VMEM((rows, depth), firsts[0].dtype),
            pltpu.VMEM((width, depth), w_kv.dtype),
            pltpu.VMEM((rows, width), jnp.bfloat16),
            pltpu.SemaphoreType.DMA((count,)),
            pltpu.SemaphoreType.DMA((width // FETCH,)),
            pltpu.SemaphoreType.DMA((width // TILE,)),
        ],
        out_shape=jax.ShapeDtypeStruct((4, block_rows, width), jnp.bfloat16),
        input_output_aliases={2 * count + 2: 0} if earlier else {},
        compiler_params=pltpu.CompilerParams(vmem_limit_bytes=GRANT),
        cost_estimate=pl.CostEstimate(flops=rows * width, bytes_accessed=rows * width, transcendentals=0),
        name="input_grad_rows",
    )(me.reshape(1).astype(jnp.int32), *firsts, *seconds, w_kv, *earlier)


def token_sums_kernel(me, low_in, low_in_beside, own_low, beside_low, facing_low, far_low, out):
    rows = own_low.shape[0]
    rank = out.shape[2]
    total = jnp.zeros((own_low.shape[1], own_low.shape[1]), jnp.float32)
    for away, low_out in (
        (0, own_low[...]),
        (1, beside_low[...]),
        (3, facing_low[...]),
        (2, far_low[...]),
    ):
        here = pl.ds(pl.multiple_of((me[0] ^ away) * rows, rows), rows)
        total += lax.dot_general(
            low_in[here, :] + low_in_beside[here, :],
            low_out,
            (((0,), (0,)), ((), ())),
            precision=lax.Precision.HIGHEST,
            preferred_element_type=jnp.float32,
        )
    slab = out.shape[1]
    for index in range(out.shape[0]):
        layer = index * slab // rank
        out[index] = total[index * slab : (index + 1) * slab, layer * rank : (layer + 1) * rank]


def token_sums(me, low_in, low_in_beside, own_low, beside_low, facing_low, far_low, rank):
    whole = pl.BlockSpec(memory_space=pltpu.VMEM)
    return pl.pallas_call(
        token_sums_kernel,
        in_specs=[pl.BlockSpec(memory_space=pltpu.SMEM)] + [whole] * 6,
        out_specs=whole,
        out_shape=jax.ShapeDtypeStruct((4, 2 * rank // 4, rank), jnp.float32),
        compiler_params=pltpu.CompilerParams(vmem_limit_bytes=GRANT),
        name="token_sums",
    )(me.reshape(1).astype(jnp.int32), low_in, low_in_beside, own_low, beside_low, facing_low, far_low)


def sequence_sums(low_in, low_out, rank):
    count = low_in.shape[0] // SEQ
    left = low_in.reshape(count, SEQ, 2 * rank)
    right = low_out.reshape(count, SEQ, 2 * rank)
    return jnp.concatenate(
        [
            lax.dot_general(
                left[:, :, layer * rank : (layer + 1) * rank],
                right[:, :, layer * rank : (layer + 1) * rank],
                (((1,), (1,)), ((0,), (0,))),
                precision=lax.Precision.HIGHEST,
                preferred_element_type=jnp.float32,
            )
            for layer in range(2)
        ],
        axis=1,
    )


def slabs_of(sums, n):
    count, height, rank = sums.shape
    return lax.optimization_barrier(sums.reshape(count, n, height // n, rank).transpose(1, 0, 2, 3))


def put(whole, piece, index):
    return lax.dynamic_update_slice(whole, piece[None], (index,) + (jnp.int32(0),) * piece.ndim)


def take(whole, index):
    return lax.dynamic_index_in_dim(whole, index, axis=0, keepdims=False)


def gathered(hidden, w_kv, grad_kv, proj_in, proj_out):
    n = lax.axis_size("mp")
    rank = proj_out.shape[2]
    whole = lax.all_gather(grad_kv, "mp", axis=0, tiled=True)
    input_grad = times_width(whole, w_kv)
    low_in = jnp.dot(hidden, proj_in, preferred_element_type=jnp.float32)
    sums = slabs_of(sequence_sums(low_in, jnp.dot(whole, block_diagonal(proj_out), preferred_element_type=jnp.float32), rank), n)
    features = lax.psum_scatter(sums, "mp", scatter_dimension=0, tiled=False)
    return features, lambda scores: (scores, scores), lambda: input_grad


def line_of_four(hidden, w_kv, grad_kv, proj_in, proj_out):
    rank = proj_out.shape[2]
    local_rows = grad_kv.shape[0]
    me = lax.axis_index("mp")
    middle = (me == 1) | (me == 2)
    exchange_pairs = [(0, 1), (1, 0), (2, 3), (3, 2)]
    across = [(1, 2), (2, 1)]
    outward = [(1, 0), (2, 3)]
    inward = [(0, 1), (3, 2)]
    tied = lax.optimization_barrier

    def low_rank(rows):
        return jnp.dot(rows, proj_both, preferred_element_type=jnp.float32)

    facing = lax.ppermute(grad_kv, "mp", across)
    beside = lax.ppermute(grad_kv, "mp", exchange_pairs)
    proj_both = tied(block_diagonal(proj_out))
    own_low = low_rank(grad_kv)
    low_in = jnp.dot(hidden, proj_in, preferred_element_type=jnp.float32)
    output = put_rows(me, 0, None, [grad_kv], [grad_kv], w_kv, local_rows)

    beside, facing, low_in, output = tied((beside, facing, low_in, output))
    beside_across = lax.ppermute(beside, "mp", across)
    second = lax.ppermute(facing, "mp", outward)
    output = put_rows(me, 1, output, [beside], [beside], w_kv, local_rows)
    low_in, output = tied((low_in, output))
    low_in_beside = lax.ppermute(low_in, "mp", inward)

    beside_low = low_rank(beside)
    facing_low = low_rank(facing)

    beside_across, second, low_in_beside, output = tied((beside_across, second, low_in_beside, output))
    third = lax.ppermute(beside_across, "mp", outward)
    far_low = low_rank(beside_across)
    if low_in.shape[0] == SEQ:
        slabs = token_sums(me, low_in, low_in_beside, own_low, beside_low, facing_low, far_low, rank)[:, None]
    else:
        low_out = jnp.zeros((4, local_rows, 2 * rank), jnp.float32)
        for away, rows in ((0, own_low), (1, beside_low), (3, facing_low), (2, far_low)):
            low_out = put(low_out, rows, me ^ away)
        sums = sequence_sums(low_in + low_in_beside, low_out.reshape(4 * local_rows, 2 * rank), rank)
        slabs = slabs_of(sums, 4)
    slabs = slabs + lax.ppermute(slabs, "mp", across)
    mine = lax.ppermute(take(slabs, me ^ 2), "mp", [(2, 0), (1, 3)])
    mine = jnp.where(middle, take(slabs, me), mine)
    output = put_rows(me, 2, output, [facing], [second], w_kv, local_rows)

    def finish(scores):
        scores = tied((scores, output))[0]
        return scores, tied((scores, third))[0]

    def rest():
        done = put_rows(me, 3, output, [beside_across], [third], w_kv, local_rows)
        return done.reshape(4 * local_rows, w_kv.shape[0])

    return mine, finish, rest


def on_device(hidden, w_kv, grad_kv, proj_in, proj_out, queries):
    n = lax.axis_size("mp")
    me = lax.axis_index("mp")
    mine, finish, rest = (line_of_four if n == 4 else gathered)(hidden, w_kv, grad_kv, proj_in, proj_out)
    count = mine.shape[0]

    shards = lax.axis_size("dp")
    shard = lax.axis_index("dp")
    block_rows = queries.shape[0]
    mine = mine.reshape(count, queries.shape[1])
    all_features = [mine] + [
        lax.ppermute(mine, "dp", [(source, (source + step) % shards) for source in range(shards)])
        for step in range(1, shards)
    ]
    terms = jnp.concatenate(three_terms(jnp.concatenate(all_features, axis=0)), axis=0)
    products = lax.dot_general(
        terms, queries, (((1,), (1,)), ((), ())), preferred_element_type=jnp.float32
    ).reshape(3, shards, count, block_rows)
    partial_scores, last_scores = finish(products[0] + (products[1] + products[2]))

    if shards == n:
        scores = jnp.zeros((count, block_rows), jnp.float32)
        for step in range(n):
            pairs = [
                (q * n + slab, (slab + step) % n * n + q) for q in range(n) for slab in range(n)
            ]
            row = take(partial_scores if step < n - 1 else last_scores, (shard - me - step + 2 * n) % n)
            scores = scores + lax.ppermute(row, ("dp", "mp"), pairs)
        return (rest(), scores)

    total = jnp.zeros((count, shards * block_rows), jnp.float32)
    for step in range(shards):
        back = partial_scores[step]
        if step > 0:
            back = lax.ppermute(back, "dp", [(source, (source - step) % shards) for source in range(shards)])
        total = lax.dynamic_update_slice(
            total, back, (jnp.int32(0), (shard + step) % shards * block_rows)
        )
    out_columns = shards * block_rows // n

    def columns_of(index):
        return lax.dynamic_slice(total, (jnp.int32(0), index * out_columns), (count, out_columns))

    scores = columns_of(me)
    for step in range(1, n):
        scores = scores + lax.ppermute(
            columns_of((me + step) % n), "mp", [(source, (source + step) % n) for source in range(n)]
        )
    return (rest(), scores)


def solution(mesh):
    in_specs = (
        P(("groups", "dp"), "mp"),
        P("mp", None),
        P(("groups", "dp", "mp"), None),
        P("mp", None),
        P(),
        P("dp", "mp"),
    )
    out_specs = (P(("groups", "dp"), "mp"), P(("groups", "dp"), "mp"))
    return jax.shard_map(
        on_device, mesh=mesh, in_specs=in_specs, out_specs=out_specs, check_vma=False
    )
```

```python
import functools

import jax
import jax.numpy as jnp
from jax import lax
from jax.experimental import pallas as pl
from jax.experimental.pallas import tpu as pltpu
from jax.sharding import PartitionSpec as P

SEQ = 1024


def three_terms(value):
    high = lax.reduce_precision(value, 8, 7)
    rest = value - high
    middle = lax.reduce_precision(rest, 8, 7)
    low = rest - middle
    return [term.astype(jnp.bfloat16) for term in (high, middle, low)]


def block_diagonal(proj_out):
    layers, width, rank = proj_out.shape
    zeros = jnp.zeros((width, rank), proj_out.dtype)
    return jnp.concatenate(
        [
            jnp.concatenate([proj_out[layer] if column == layer else zeros for column in range(layers)], axis=1)
            for layer in range(layers)
        ],
        axis=0,
    )


def times_width(rows, w_kv):
    return lax.dot_general(
        rows, w_kv, (((1,), (1,)), ((), ())), preferred_element_type=jnp.float32
    ).astype(jnp.bfloat16)


FETCH = 256
TILE = 512
GRANT = 24 * 2**20


def rows_kernel(block, start, count, me, *refs):
    firsts, seconds = refs[:count], refs[count : 2 * count]
    w_kv = refs[2 * count]
    out, held, weight, product, arrived, fetched, written = refs[-7:]
    mine = me[0]
    middle = (mine == 1) | (mine == 2)
    index = [mine, mine ^ 1, jnp.where(middle, mine ^ 3, mine ^ 2), jnp.where(middle, mine ^ 2, mine ^ 3)][block]
    use_second = jnp.logical_not(middle) if block > 1 else mine < 0

    fetches = []
    for piece in range(weight.shape[0] // FETCH):
        here = pl.ds(piece * FETCH, FETCH)
        fetches.append(pltpu.make_async_copy(w_kv.at[here], weight.at[here], fetched.at[piece]))
    loads = []
    filled = 0
    for part in range(count):
        rows = firsts[part].shape[0]
        here = held.at[pl.ds(filled, rows)]
        filled += rows
        loads.append(pltpu.make_async_copy(firsts[part], here, arrived.at[part]))
        late = pltpu.make_async_copy(seconds[part], here, arrived.at[part])
        if block > 1:
            pl.when(jnp.logical_not(use_second))(loads[-1].start)
            pl.when(use_second)(late.start)
        else:
            loads[-1].start()
    for fetch in fetches:
        fetch.start()
    for load in loads:
        load.wait()
    writes = []
    for tile in range(weight.shape[0] // TILE):
        here = pl.ds(tile * TILE, TILE)
        for piece in range(tile * TILE // FETCH, (tile + 1) * TILE // FETCH):
            fetches[piece].wait()
        product[:, here] = lax.dot_general(
            held[...], weight[here, :], (((1,), (1,)), ((), ())), preferred_element_type=jnp.float32
        ).astype(product.dtype)
        writes.append(
            pltpu.make_async_copy(
                product.at[:, here], out.at[index, pl.ds(start, product.shape[0]), here], written.at[tile]
            )
        )
        writes[-1].start()
    for write in writes:
        write.wait()


def put_rows(me, block, output, firsts, seconds, w_kv, block_rows, start=0):
    count = len(firsts)
    depth = firsts[0].shape[1]
    rows = sum(part.shape[0] for part in firsts)
    width = w_kv.shape[0]
    earlier = [] if output is None else [output]
    return pl.pallas_call(
        functools.partial(rows_kernel, block, start, count),
        in_specs=[pl.BlockSpec(memory_space=pltpu.SMEM)]
        + [pl.BlockSpec(memory_space=pl.ANY)] * (2 * count)
        + [pl.BlockSpec(memory_space=pltpu.HBM)] * (1 + len(earlier)),
        out_specs=pl.BlockSpec(memory_space=pltpu.HBM),
        scratch_shapes=[
            pltpu.VMEM((rows, depth), firsts[0].dtype),
            pltpu.VMEM((width, depth), w_kv.dtype),
            pltpu.VMEM((rows, width), jnp.bfloat16),
            pltpu.SemaphoreType.DMA((count,)),
            pltpu.SemaphoreType.DMA((width // FETCH,)),
            pltpu.SemaphoreType.DMA((width // TILE,)),
        ],
        out_shape=jax.ShapeDtypeStruct((4, block_rows, width), jnp.bfloat16),
        input_output_aliases={2 * count + 2: 0} if earlier else {},
        compiler_params=pltpu.CompilerParams(vmem_limit_bytes=GRANT),
        cost_estimate=pl.CostEstimate(flops=rows * width, bytes_accessed=rows * width, transcendentals=0),
        name="input_grad_rows",
    )(me.reshape(1).astype(jnp.int32), *firsts, *seconds, w_kv, *earlier)


def token_sums_kernel(me, low_in, low_in_beside, own_low, beside_low, facing_low, far_low, out):
    rows = own_low.shape[0]
    rank = out.shape[2]
    total = jnp.zeros((own_low.shape[1], own_low.shape[1]), jnp.float32)
    for away, low_out in (
        (0, own_low[...]),
        (1, beside_low[...]),
        (3, facing_low[...]),
        (2, far_low[...]),
    ):
        here = pl.ds(pl.multiple_of((me[0] ^ away) * rows, rows), rows)
        total += lax.dot_general(
            low_in[here, :] + low_in_beside[here, :],
            low_out,
            (((0,), (0,)), ((), ())),
            precision=lax.Precision.HIGHEST,
            preferred_element_type=jnp.float32,
        )
    slab = out.shape[1]
    for index in range(out.shape[0]):
        layer = index * slab // rank
        out[index] = total[index * slab : (index + 1) * slab, layer * rank : (layer + 1) * rank]


def token_sums(me, low_in, low_in_beside, own_low, beside_low, facing_low, far_low, rank):
    whole = pl.BlockSpec(memory_space=pltpu.VMEM)
    return pl.pallas_call(
        token_sums_kernel,
        in_specs=[pl.BlockSpec(memory_space=pltpu.SMEM)] + [whole] * 6,
        out_specs=whole,
        out_shape=jax.ShapeDtypeStruct((4, 2 * rank // 4, rank), jnp.float32),
        compiler_params=pltpu.CompilerParams(vmem_limit_bytes=GRANT),
        name="token_sums",
    )(me.reshape(1).astype(jnp.int32), low_in, low_in_beside, own_low, beside_low, facing_low, far_low)


def sequence_sums(low_in, low_out, rank):
    count = low_in.shape[0] // SEQ
    left = low_in.reshape(count, SEQ, 2 * rank)
    right = low_out.reshape(count, SEQ, 2 * rank)
    return jnp.concatenate(
        [
            lax.dot_general(
                left[:, :, layer * rank : (layer + 1) * rank],
                right[:, :, layer * rank : (layer + 1) * rank],
                (((1,), (1,)), ((0,), (0,))),
                precision=lax.Precision.HIGHEST,
                preferred_element_type=jnp.float32,
            )
            for layer in range(2)
        ],
        axis=1,
    )


def slabs_of(sums, n):
    count, height, rank = sums.shape
    return lax.optimization_barrier(sums.reshape(count, n, height // n, rank).transpose(1, 0, 2, 3))


def put(whole, piece, index):
    return lax.dynamic_update_slice(whole, piece[None], (index,) + (jnp.int32(0),) * piece.ndim)


def take(whole, index):
    return lax.dynamic_index_in_dim(whole, index, axis=0, keepdims=False)


def gathered(hidden, w_kv, grad_kv, proj_in, proj_out):
    n = lax.axis_size("mp")
    rank = proj_out.shape[2]
    whole = lax.all_gather(grad_kv, "mp", axis=0, tiled=True)
    input_grad = times_width(whole, w_kv)
    low_in = jnp.dot(hidden, proj_in, preferred_element_type=jnp.float32)
    sums = slabs_of(sequence_sums(low_in, jnp.dot(whole, block_diagonal(proj_out), preferred_element_type=jnp.float32), rank), n)
    features = lax.psum_scatter(sums, "mp", scatter_dimension=0, tiled=False)
    return features, lambda scores: (scores, scores), lambda: input_grad


def line_of_four(hidden, w_kv, grad_kv, proj_in, proj_out):
    rank = proj_out.shape[2]
    local_rows = grad_kv.shape[0]
    me = lax.axis_index("mp")
    middle = (me == 1) | (me == 2)
    exchange_pairs = [(0, 1), (1, 0), (2, 3), (3, 2)]
    across = [(1, 2), (2, 1)]
    outward = [(1, 0), (2, 3)]
    inward = [(0, 1), (3, 2)]
    tied = lax.optimization_barrier

    def low_rank(rows):
        return jnp.dot(rows, proj_both, preferred_element_type=jnp.float32)

    facing = lax.ppermute(grad_kv, "mp", across)
    beside = lax.ppermute(grad_kv, "mp", exchange_pairs)
    proj_both = tied(block_diagonal(proj_out))
    own_low = low_rank(grad_kv)
    low_in = jnp.dot(hidden, proj_in, preferred_element_type=jnp.float32)
    output = put_rows(me, 0, None, [grad_kv], [grad_kv], w_kv, local_rows)

    far_low = lax.ppermute(own_low, "mp", [(3, 1), (0, 2)])

    beside, facing, low_in, output = tied((beside, facing, low_in, output))
    beside_across = lax.ppermute(beside, "mp", across)
    second = lax.ppermute(facing, "mp", outward)
    low_in_beside = lax.ppermute(low_in, "mp", inward)
    output = put_rows(me, 1, output, [beside], [beside], w_kv, local_rows)

    beside_low = low_rank(beside)
    facing_low = low_rank(facing)
    if low_in.shape[0] == SEQ:
        slabs = token_sums(me, low_in, low_in_beside, own_low, beside_low, facing_low, far_low, rank)[:, None]
    else:
        low_out = jnp.zeros((4, local_rows, 2 * rank), jnp.float32)
        for away, rows in ((0, own_low), (1, beside_low), (3, facing_low), (2, far_low)):
            low_out = put(low_out, rows, me ^ away)
        sums = sequence_sums(low_in + low_in_beside, low_out.reshape(4 * local_rows, 2 * rank), rank)
        slabs = slabs_of(sums, 4)
    slabs = slabs + lax.ppermute(slabs, "mp", across)

    beside_across, second, slabs, output = tied((beside_across, second, slabs, output))
    third = lax.ppermute(beside_across, "mp", outward)
    mine = lax.ppermute(take(slabs, me ^ 2), "mp", [(2, 0), (1, 3)])
    mine = jnp.where(middle, take(slabs, me), mine)
    output = put_rows(me, 2, output, [facing], [second], w_kv, local_rows)

    def finish(scores):
        scores = tied((scores, output))[0]
        return scores, tied((scores, third))[0]

    def rest():
        done = put_rows(me, 3, output, [beside_across], [third], w_kv, local_rows)
        return done.reshape(4 * local_rows, w_kv.shape[0])

    return mine, finish, rest


def on_device(hidden, w_kv, grad_kv, proj_in, proj_out, queries):
    n = lax.axis_size("mp")
    me = lax.axis_index("mp")
    mine, finish, rest = (line_of_four if n == 4 else gathered)(hidden, w_kv, grad_kv, proj_in, proj_out)
    count = mine.shape[0]

    shards = lax.axis_size("dp")
    shard = lax.axis_index("dp")
    block_rows = queries.shape[0]
    mine = mine.reshape(count, queries.shape[1])
    all_features = [mine] + [
        lax.ppermute(mine, "dp", [(source, (source + step) % shards) for source in range(shards)])
        for step in range(1, shards)
    ]
    terms = jnp.concatenate(three_terms(jnp.concatenate(all_features, axis=0)), axis=0)
    products = lax.dot_general(
        terms, queries, (((1,), (1,)), ((), ())), preferred_element_type=jnp.float32
    ).reshape(3, shards, count, block_rows)
    partial_scores, last_scores = finish(products[0] + (products[1] + products[2]))

    if shards == n:
        scores = jnp.zeros((count, block_rows), jnp.float32)
        for step in range(n):
            pairs = [
                (q * n + slab, (slab + step) % n * n + q) for q in range(n) for slab in range(n)
            ]
            row = take(partial_scores if step < n - 1 else last_scores, (shard - me - step + 2 * n) % n)
            scores = scores + lax.ppermute(row, ("dp", "mp"), pairs)
        return (rest(), scores)

    total = jnp.zeros((count, shards * block_rows), jnp.float32)
    for step in range(shards):
        back = partial_scores[step]
        if step > 0:
            back = lax.ppermute(back, "dp", [(source, (source - step) % shards) for source in range(shards)])
        total = lax.dynamic_update_slice(
            total, back, (jnp.int32(0), (shard + step) % shards * block_rows)
        )
    out_columns = shards * block_rows // n

    def columns_of(index):
        return lax.dynamic_slice(total, (jnp.int32(0), index * out_columns), (count, out_columns))

    scores = columns_of(me)
    for step in range(1, n):
        scores = scores + lax.ppermute(
            columns_of((me + step) % n), "mp", [(source, (source + step) % n) for source in range(n)]
        )
    return (rest(), scores)


def solution(mesh):
    in_specs = (
        P(("groups", "dp"), "mp"),
        P("mp", None),
        P(("groups", "dp", "mp"), None),
        P("mp", None),
        P(),
        P("dp", "mp"),
    )
    out_specs = (P(("groups", "dp"), "mp"), P(("groups", "dp"), "mp"))
    return jax.shard_map(
        on_device, mesh=mesh, in_specs=in_specs, out_specs=out_specs, check_vma=False
    )
```

```python
import functools

import jax
import jax.numpy as jnp
from jax import lax
from jax.experimental import pallas as pl
from jax.experimental.pallas import tpu as pltpu
from jax.sharding import PartitionSpec as P

SEQ = 1024


def three_terms(value):
    high = lax.reduce_precision(value, 8, 7)
    rest = value - high
    middle = lax.reduce_precision(rest, 8, 7)
    low = rest - middle
    return [term.astype(jnp.bfloat16) for term in (high, middle, low)]


def block_diagonal(proj_out):
    layers, width, rank = proj_out.shape
    zeros = jnp.zeros((width, rank), proj_out.dtype)
    return jnp.concatenate(
        [
            jnp.concatenate([proj_out[layer] if column == layer else zeros for column in range(layers)], axis=1)
            for layer in range(layers)
        ],
        axis=0,
    )


def times_width(rows, w_kv):
    return lax.dot_general(
        rows, w_kv, (((1,), (1,)), ((), ())), preferred_element_type=jnp.float32
    ).astype(jnp.bfloat16)


FETCH = 256
TILE = 512
GRANT = 24 * 2**20


def rows_kernel(block, start, count, me, *refs):
    firsts, seconds = refs[:count], refs[count : 2 * count]
    w_kv = refs[2 * count]
    out, held, weight, product, arrived, fetched, written = refs[-7:]
    mine = me[0]
    middle = (mine == 1) | (mine == 2)
    index = [mine, mine ^ 1, jnp.where(middle, mine ^ 3, mine ^ 2), jnp.where(middle, mine ^ 2, mine ^ 3)][block]
    use_second = jnp.logical_not(middle) if block > 1 else mine < 0

    fetches = []
    for piece in range(weight.shape[0] // FETCH):
        here = pl.ds(piece * FETCH, FETCH)
        fetches.append(pltpu.make_async_copy(w_kv.at[here], weight.at[here], fetched.at[piece]))
    loads = []
    filled = 0
    for part in range(count):
        rows = firsts[part].shape[0]
        here = held.at[pl.ds(filled, rows)]
        filled += rows
        loads.append(pltpu.make_async_copy(firsts[part], here, arrived.at[part]))
        late = pltpu.make_async_copy(seconds[part], here, arrived.at[part])
        if block > 1:
            pl.when(jnp.logical_not(use_second))(loads[-1].start)
            pl.when(use_second)(late.start)
        else:
            loads[-1].start()
    for fetch in fetches:
        fetch.start()
    for load in loads:
        load.wait()
    writes = []
    for tile in range(weight.shape[0] // TILE):
        here = pl.ds(tile * TILE, TILE)
        for piece in range(tile * TILE // FETCH, (tile + 1) * TILE // FETCH):
            fetches[piece].wait()
        product[:, here] = lax.dot_general(
            held[...], weight[here, :], (((1,), (1,)), ((), ())), preferred_element_type=jnp.float32
        ).astype(product.dtype)
        writes.append(
            pltpu.make_async_copy(
                product.at[:, here], out.at[index, pl.ds(start, product.shape[0]), here], written.at[tile]
            )
        )
        writes[-1].start()
    for write in writes:
        write.wait()


def put_rows(me, block, output, firsts, seconds, w_kv, block_rows, start=0):
    count = len(firsts)
    depth = firsts[0].shape[1]
    rows = sum(part.shape[0] for part in firsts)
    width = w_kv.shape[0]
    earlier = [] if output is None else [output]
    return pl.pallas_call(
        functools.partial(rows_kernel, block, start, count),
        in_specs=[pl.BlockSpec(memory_space=pltpu.SMEM)]
        + [pl.BlockSpec(memory_space=pl.ANY)] * (2 * count)
        + [pl.BlockSpec(memory_space=pltpu.HBM)] * (1 + len(earlier)),
        out_specs=pl.BlockSpec(memory_space=pltpu.HBM),
        scratch_shapes=[
            pltpu.VMEM((rows, depth), firsts[0].dtype),
            pltpu.VMEM((width, depth), w_kv.dtype),
            pltpu.VMEM((rows, width), jnp.bfloat16),
            pltpu.SemaphoreType.DMA((count,)),
            pltpu.SemaphoreType.DMA((width // FETCH,)),
            pltpu.SemaphoreType.DMA((width // TILE,)),
        ],
        out_shape=jax.ShapeDtypeStruct((4, block_rows, width), jnp.bfloat16),
        input_output_aliases={2 * count + 2: 0} if earlier else {},
        compiler_params=pltpu.CompilerParams(vmem_limit_bytes=GRANT),
        cost_estimate=pl.CostEstimate(flops=rows * width, bytes_accessed=rows * width, transcendentals=0),
        name="input_grad_rows",
    )(me.reshape(1).astype(jnp.int32), *firsts, *seconds, w_kv, *earlier)


def token_sums_kernel(me, low_in, low_in_beside, own_low, beside_low, facing_low, far_low, out):
    rows = own_low.shape[0]
    rank = out.shape[2]
    total = jnp.zeros((own_low.shape[1], own_low.shape[1]), jnp.float32)
    for away, low_out in (
        (0, own_low[...]),
        (1, beside_low[...]),
        (3, facing_low[...]),
        (2, far_low[...]),
    ):
        here = pl.ds(pl.multiple_of((me[0] ^ away) * rows, rows), rows)
        total += lax.dot_general(
            low_in[here, :] + low_in_beside[here, :],
            low_out,
            (((0,), (0,)), ((), ())),
            precision=lax.Precision.HIGHEST,
            preferred_element_type=jnp.float32,
        )
    slab = out.shape[1]
    for index in range(out.shape[0]):
        layer = index * slab // rank
        out[index] = total[index * slab : (index + 1) * slab, layer * rank : (layer + 1) * rank]


def token_sums(me, low_in, low_in_beside, own_low, beside_low, facing_low, far_low, rank):
    whole = pl.BlockSpec(memory_space=pltpu.VMEM)
    return pl.pallas_call(
        token_sums_kernel,
        in_specs=[pl.BlockSpec(memory_space=pltpu.SMEM)] + [whole] * 6,
        out_specs=whole,
        out_shape=jax.ShapeDtypeStruct((4, 2 * rank // 4, rank), jnp.float32),
        compiler_params=pltpu.CompilerParams(vmem_limit_bytes=GRANT),
        name="token_sums",
    )(me.reshape(1).astype(jnp.int32), low_in, low_in_beside, own_low, beside_low, facing_low, far_low)


def sequence_sums(low_in, low_out, rank):
    count = low_in.shape[0] // SEQ
    left = low_in.reshape(count, SEQ, 2 * rank)
    right = low_out.reshape(count, SEQ, 2 * rank)
    return jnp.concatenate(
        [
            lax.dot_general(
                left[:, :, layer * rank : (layer + 1) * rank],
                right[:, :, layer * rank : (layer + 1) * rank],
                (((1,), (1,)), ((0,), (0,))),
                precision=lax.Precision.HIGHEST,
                preferred_element_type=jnp.float32,
            )
            for layer in range(2)
        ],
        axis=1,
    )


def slabs_of(sums, n):
    count, height, rank = sums.shape
    return lax.optimization_barrier(sums.reshape(count, n, height // n, rank).transpose(1, 0, 2, 3))


def put(whole, piece, index):
    return lax.dynamic_update_slice(whole, piece[None], (index,) + (jnp.int32(0),) * piece.ndim)


def take(whole, index):
    return lax.dynamic_index_in_dim(whole, index, axis=0, keepdims=False)


def gathered(hidden, w_kv, grad_kv, proj_in, proj_out):
    n = lax.axis_size("mp")
    rank = proj_out.shape[2]
    whole = lax.all_gather(grad_kv, "mp", axis=0, tiled=True)
    input_grad = times_width(whole, w_kv)
    low_in = jnp.dot(hidden, proj_in, preferred_element_type=jnp.float32)
    sums = slabs_of(sequence_sums(low_in, jnp.dot(whole, block_diagonal(proj_out), preferred_element_type=jnp.float32), rank), n)
    features = lax.psum_scatter(sums, "mp", scatter_dimension=0, tiled=False)
    return features, lambda scores: (scores, scores), lambda: input_grad


def line_of_four(hidden, w_kv, grad_kv, proj_in, proj_out):
    rank = proj_out.shape[2]
    local_rows = grad_kv.shape[0]
    me = lax.axis_index("mp")
    middle = (me == 1) | (me == 2)
    exchange_pairs = [(0, 1), (1, 0), (2, 3), (3, 2)]
    across = [(1, 2), (2, 1)]
    outward = [(1, 0), (2, 3)]
    inward = [(0, 1), (3, 2)]
    tied = lax.optimization_barrier

    def low_rank(rows):
        return jnp.dot(rows, proj_both, preferred_element_type=jnp.float32)

    facing = lax.ppermute(grad_kv, "mp", across)
    beside = lax.ppermute(grad_kv, "mp", exchange_pairs)
    proj_both = tied(block_diagonal(proj_out))
    own_low = low_rank(grad_kv)
    low_in = jnp.dot(hidden, proj_in, preferred_element_type=jnp.float32)
    output = put_rows(me, 0, None, [grad_kv], [grad_kv], w_kv, local_rows)

    far_low = lax.ppermute(own_low, "mp", [(3, 1), (0, 2)])

    beside, low_in, output = tied((beside, low_in, output))
    beside_across = lax.ppermute(beside, "mp", across)
    second = lax.ppermute(facing, "mp", outward)
    low_in_beside = lax.ppermute(low_in, "mp", inward)
    output = put_rows(me, 1, output, [beside], [beside], w_kv, local_rows)

    far_low, output = tied((far_low, output))
    beside_low = low_rank(beside)
    facing_low = low_rank(facing)
    if low_in.shape[0] == SEQ:
        slabs = token_sums(me, low_in, low_in_beside, own_low, beside_low, facing_low, far_low, rank)[:, None]
    else:
        low_out = jnp.zeros((4, local_rows, 2 * rank), jnp.float32)
        for away, rows in ((0, own_low), (1, beside_low), (3, facing_low), (2, far_low)):
            low_out = put(low_out, rows, me ^ away)
        sums = sequence_sums(low_in + low_in_beside, low_out.reshape(4 * local_rows, 2 * rank), rank)
        slabs = slabs_of(sums, 4)
    slabs = slabs + lax.ppermute(slabs, "mp", across)

    beside_across, second, slabs, output = tied((beside_across, second, slabs, output))
    third = lax.ppermute(beside_across, "mp", outward)
    mine = lax.ppermute(take(slabs, me ^ 2), "mp", [(2, 0), (1, 3)])
    mine = jnp.where(middle, take(slabs, me), mine)
    output = put_rows(me, 2, output, [facing], [second], w_kv, local_rows)

    def finish(scores):
        scores = tied((scores, output))[0]
        return scores, tied((scores, third))[0]

    def rest():
        done = put_rows(me, 3, output, [beside_across], [third], w_kv, local_rows)
        return done.reshape(4 * local_rows, w_kv.shape[0])

    return mine, finish, rest


def on_device(hidden, w_kv, grad_kv, proj_in, proj_out, queries):
    n = lax.axis_size("mp")
    me = lax.axis_index("mp")
    mine, finish, rest = (line_of_four if n == 4 else gathered)(hidden, w_kv, grad_kv, proj_in, proj_out)
    count = mine.shape[0]

    shards = lax.axis_size("dp")
    shard = lax.axis_index("dp")
    block_rows = queries.shape[0]
    mine = mine.reshape(count, queries.shape[1])
    all_features = [mine] + [
        lax.ppermute(mine, "dp", [(source, (source + step) % shards) for source in range(shards)])
        for step in range(1, shards)
    ]
    terms = jnp.concatenate(three_terms(jnp.concatenate(all_features, axis=0)), axis=0)
    products = lax.dot_general(
        terms, queries, (((1,), (1,)), ((), ())), preferred_element_type=jnp.float32
    ).reshape(3, shards, count, block_rows)
    partial_scores, last_scores = finish(products[0] + (products[1] + products[2]))

    if shards == n:
        scores = jnp.zeros((count, block_rows), jnp.float32)
        for step in range(n):
            pairs = [
                (q * n + slab, (slab + step) % n * n + q) for q in range(n) for slab in range(n)
            ]
            row = take(partial_scores if step < n - 1 else last_scores, (shard - me - step + 2 * n) % n)
            scores = scores + lax.ppermute(row, ("dp", "mp"), pairs)
        return (rest(), scores)

    total = jnp.zeros((count, shards * block_rows), jnp.float32)
    for step in range(shards):
        back = partial_scores[step]
        if step > 0:
            back = lax.ppermute(back, "dp", [(source, (source - step) % shards) for source in range(shards)])
        total = lax.dynamic_update_slice(
            total, back, (jnp.int32(0), (shard + step) % shards * block_rows)
        )
    out_columns = shards * block_rows // n

    def columns_of(index):
        return lax.dynamic_slice(total, (jnp.int32(0), index * out_columns), (count, out_columns))

    scores = columns_of(me)
    for step in range(1, n):
        scores = scores + lax.ppermute(
            columns_of((me + step) % n), "mp", [(source, (source + step) % n) for source in range(n)]
        )
    return (rest(), scores)


def solution(mesh):
    in_specs = (
        P(("groups", "dp"), "mp"),
        P("mp", None),
        P(("groups", "dp", "mp"), None),
        P("mp", None),
        P(),
        P("dp", "mp"),
    )
    out_specs = (P(("groups", "dp"), "mp"), P(("groups", "dp"), "mp"))
    return jax.shard_map(
        on_device, mesh=mesh, in_specs=in_specs, out_specs=out_specs, check_vma=False
    )
```

```python
import functools

import jax
import jax.numpy as jnp
from jax import lax
from jax.experimental import pallas as pl
from jax.experimental.pallas import tpu as pltpu
from jax.sharding import PartitionSpec as P

SEQ = 1024


def three_terms(value):
    high = lax.reduce_precision(value, 8, 7)
    rest = value - high
    middle = lax.reduce_precision(rest, 8, 7)
    low = rest - middle
    return [term.astype(jnp.bfloat16) for term in (high, middle, low)]


def block_diagonal(proj_out):
    layers, width, rank = proj_out.shape
    zeros = jnp.zeros((width, rank), proj_out.dtype)
    return jnp.concatenate(
        [
            jnp.concatenate([proj_out[layer] if column == layer else zeros for column in range(layers)], axis=1)
            for layer in range(layers)
        ],
        axis=0,
    )


def times_width(rows, w_kv):
    return lax.dot_general(
        rows, w_kv, (((1,), (1,)), ((), ())), preferred_element_type=jnp.float32
    ).astype(jnp.bfloat16)


FETCH = 256
TILE = 512
GRANT = 24 * 2**20


def rows_kernel(block, start, count, me, *refs):
    firsts, seconds = refs[:count], refs[count : 2 * count]
    w_kv = refs[2 * count]
    out, held, weight, product, arrived, fetched, written = refs[-7:]
    mine = me[0]
    middle = (mine == 1) | (mine == 2)
    index = [mine, mine ^ 1, jnp.where(middle, mine ^ 3, mine ^ 2), jnp.where(middle, mine ^ 2, mine ^ 3)][block]
    use_second = jnp.logical_not(middle) if block > 1 else mine < 0

    fetches = []
    for piece in range(weight.shape[0] // FETCH):
        here = pl.ds(piece * FETCH, FETCH)
        fetches.append(pltpu.make_async_copy(w_kv.at[here], weight.at[here], fetched.at[piece]))
    loads = []
    filled = 0
    for part in range(count):
        rows = firsts[part].shape[0]
        here = held.at[pl.ds(filled, rows)]
        filled += rows
        loads.append(pltpu.make_async_copy(firsts[part], here, arrived.at[part]))
        late = pltpu.make_async_copy(seconds[part], here, arrived.at[part])
        if block > 1:
            pl.when(jnp.logical_not(use_second))(loads[-1].start)
            pl.when(use_second)(late.start)
        else:
            loads[-1].start()
    for fetch in fetches:
        fetch.start()
    for load in loads:
        load.wait()
    writes = []
    for tile in range(weight.shape[0] // TILE):
        here = pl.ds(tile * TILE, TILE)
        for piece in range(tile * TILE // FETCH, (tile + 1) * TILE // FETCH):
            fetches[piece].wait()
        product[:, here] = lax.dot_general(
            held[...], weight[here, :], (((1,), (1,)), ((), ())), preferred_element_type=jnp.float32
        ).astype(product.dtype)
        writes.append(
            pltpu.make_async_copy(
                product.at[:, here], out.at[index, pl.ds(start, product.shape[0]), here], written.at[tile]
            )
        )
        writes[-1].start()
    for write in writes:
        write.wait()


def put_rows(me, block, output, firsts, seconds, w_kv, block_rows, start=0):
    count = len(firsts)
    depth = firsts[0].shape[1]
    rows = sum(part.shape[0] for part in firsts)
    width = w_kv.shape[0]
    earlier = [] if output is None else [output]
    return pl.pallas_call(
        functools.partial(rows_kernel, block, start, count),
        in_specs=[pl.BlockSpec(memory_space=pltpu.SMEM)]
        + [pl.BlockSpec(memory_space=pl.ANY)] * (2 * count)
        + [pl.BlockSpec(memory_space=pltpu.HBM)] * (1 + len(earlier)),
        out_specs=pl.BlockSpec(memory_space=pltpu.HBM),
        scratch_shapes=[
            pltpu.VMEM((rows, depth), firsts[0].dtype),
            pltpu.VMEM((width, depth), w_kv.dtype),
            pltpu.VMEM((rows, width), jnp.bfloat16),
            pltpu.SemaphoreType.DMA((count,)),
            pltpu.SemaphoreType.DMA((width // FETCH,)),
            pltpu.SemaphoreType.DMA((width // TILE,)),
        ],
        out_shape=jax.ShapeDtypeStruct((4, block_rows, width), jnp.bfloat16),
        input_output_aliases={2 * count + 2: 0} if earlier else {},
        compiler_params=pltpu.CompilerParams(vmem_limit_bytes=GRANT),
        cost_estimate=pl.CostEstimate(flops=rows * width, bytes_accessed=rows * width, transcendentals=0),
        name="input_grad_rows",
    )(me.reshape(1).astype(jnp.int32), *firsts, *seconds, w_kv, *earlier)


def token_sums_kernel(me, low_in, low_in_beside, own_low, beside_low, facing_low, far_low, out):
    rows = own_low.shape[0]
    rank = out.shape[2]
    total = jnp.zeros((own_low.shape[1], own_low.shape[1]), jnp.float32)
    for away, low_out in (
        (0, own_low[...]),
        (1, beside_low[...]),
        (3, facing_low[...]),
        (2, far_low[...]),
    ):
        here = pl.ds(pl.multiple_of((me[0] ^ away) * rows, rows), rows)
        total += lax.dot_general(
            low_in[here, :] + low_in_beside[here, :],
            low_out,
            (((0,), (0,)), ((), ())),
            precision=lax.Precision.HIGHEST,
            preferred_element_type=jnp.float32,
        )
    slab = out.shape[1]
    for index in range(out.shape[0]):
        layer = index * slab // rank
        out[index] = total[index * slab : (index + 1) * slab, layer * rank : (layer + 1) * rank]


def token_sums(me, low_in, low_in_beside, own_low, beside_low, facing_low, far_low, rank):
    whole = pl.BlockSpec(memory_space=pltpu.VMEM)
    return pl.pallas_call(
        token_sums_kernel,
        in_specs=[pl.BlockSpec(memory_space=pltpu.SMEM)] + [whole] * 6,
        out_specs=whole,
        out_shape=jax.ShapeDtypeStruct((4, 2 * rank // 4, rank), jnp.float32),
        compiler_params=pltpu.CompilerParams(vmem_limit_bytes=GRANT),
        name="token_sums",
    )(me.reshape(1).astype(jnp.int32), low_in, low_in_beside, own_low, beside_low, facing_low, far_low)


def sequence_sums(low_in, low_out, rank):
    count = low_in.shape[0] // SEQ
    left = low_in.reshape(count, SEQ, 2 * rank)
    right = low_out.reshape(count, SEQ, 2 * rank)
    return jnp.concatenate(
        [
            lax.dot_general(
                left[:, :, layer * rank : (layer + 1) * rank],
                right[:, :, layer * rank : (layer + 1) * rank],
                (((1,), (1,)), ((0,), (0,))),
                precision=lax.Precision.HIGHEST,
                preferred_element_type=jnp.float32,
            )
            for layer in range(2)
        ],
        axis=1,
    )


def slabs_of(sums, n):
    count, height, rank = sums.shape
    return lax.optimization_barrier(sums.reshape(count, n, height // n, rank).transpose(1, 0, 2, 3))


def put(whole, piece, index):
    return lax.dynamic_update_slice(whole, piece[None], (index,) + (jnp.int32(0),) * piece.ndim)


def take(whole, index):
    return lax.dynamic_index_in_dim(whole, index, axis=0, keepdims=False)


def gathered(hidden, w_kv, grad_kv, proj_in, proj_out):
    n = lax.axis_size("mp")
    rank = proj_out.shape[2]
    whole = lax.all_gather(grad_kv, "mp", axis=0, tiled=True)
    input_grad = times_width(whole, w_kv)
    low_in = jnp.dot(hidden, proj_in, preferred_element_type=jnp.float32)
    sums = slabs_of(sequence_sums(low_in, jnp.dot(whole, block_diagonal(proj_out), preferred_element_type=jnp.float32), rank), n)
    features = lax.psum_scatter(sums, "mp", scatter_dimension=0, tiled=False)
    return features, lambda scores: (scores, scores), lambda: input_grad


def line_of_four(hidden, w_kv, grad_kv, proj_in, proj_out):
    rank = proj_out.shape[2]
    local_rows = grad_kv.shape[0]
    me = lax.axis_index("mp")
    middle = (me == 1) | (me == 2)
    exchange_pairs = [(0, 1), (1, 0), (2, 3), (3, 2)]
    across = [(1, 2), (2, 1)]
    outward = [(1, 0), (2, 3)]
    inward = [(0, 1), (3, 2)]
    tied = lax.optimization_barrier

    def low_rank(rows):
        return jnp.dot(rows, proj_both, preferred_element_type=jnp.float32)

    facing = lax.ppermute(grad_kv, "mp", across)
    beside = lax.ppermute(grad_kv, "mp", exchange_pairs)
    proj_both = tied(block_diagonal(proj_out))
    own_low = low_rank(grad_kv)
    low_in = jnp.dot(hidden, proj_in, preferred_element_type=jnp.float32)
    output = put_rows(me, 0, None, [grad_kv], [grad_kv], w_kv, local_rows)

    far_low = lax.ppermute(own_low, "mp", [(3, 1), (0, 2)])

    beside, low_in, far_low, output = tied((beside, low_in, far_low, output))
    beside_across = lax.ppermute(beside, "mp", across)
    second = lax.ppermute(facing, "mp", outward)
    low_in_beside = lax.ppermute(low_in, "mp", inward)
    output = put_rows(me, 1, output, [beside], [beside], w_kv, local_rows)

    low_in_beside, output = tied((low_in_beside, output))
    beside_low = low_rank(beside)
    facing_low = low_rank(facing)
    if low_in.shape[0] == SEQ:
        slabs = token_sums(me, low_in, low_in_beside, own_low, beside_low, facing_low, far_low, rank)[:, None]
    else:
        low_out = jnp.zeros((4, local_rows, 2 * rank), jnp.float32)
        for away, rows in ((0, own_low), (1, beside_low), (3, facing_low), (2, far_low)):
            low_out = put(low_out, rows, me ^ away)
        sums = sequence_sums(low_in + low_in_beside, low_out.reshape(4 * local_rows, 2 * rank), rank)
        slabs = slabs_of(sums, 4)
    slabs = slabs + lax.ppermute(slabs, "mp", across)

    beside_across, second, slabs, output = tied((beside_across, second, slabs, output))
    third = lax.ppermute(beside_across, "mp", outward)
    mine = lax.ppermute(take(slabs, me ^ 2), "mp", [(2, 0), (1, 3)])
    mine = jnp.where(middle, take(slabs, me), mine)
    output = put_rows(me, 2, output, [facing], [second], w_kv, local_rows)

    def finish(scores):
        scores = tied((scores, output))[0]
        return scores, tied((scores, third))[0]

    def rest():
        done = put_rows(me, 3, output, [beside_across], [third], w_kv, local_rows)
        return done.reshape(4 * local_rows, w_kv.shape[0])

    return mine, finish, rest


def on_device(hidden, w_kv, grad_kv, proj_in, proj_out, queries):
    n = lax.axis_size("mp")
    me = lax.axis_index("mp")
    mine, finish, rest = (line_of_four if n == 4 else gathered)(hidden, w_kv, grad_kv, proj_in, proj_out)
    count = mine.shape[0]

    shards = lax.axis_size("dp")
    shard = lax.axis_index("dp")
    block_rows = queries.shape[0]
    mine = mine.reshape(count, queries.shape[1])
    all_features = [mine] + [
        lax.ppermute(mine, "dp", [(source, (source + step) % shards) for source in range(shards)])
        for step in range(1, shards)
    ]
    terms = jnp.concatenate(three_terms(jnp.concatenate(all_features, axis=0)), axis=0)
    products = lax.dot_general(
        terms, queries, (((1,), (1,)), ((), ())), preferred_element_type=jnp.float32
    ).reshape(3, shards, count, block_rows)
    partial_scores, last_scores = finish(products[0] + (products[1] + products[2]))

    if shards == n:
        scores = jnp.zeros((count, block_rows), jnp.float32)
        for step in range(n):
            pairs = [
                (q * n + slab, (slab + step) % n * n + q) for q in range(n) for slab in range(n)
            ]
            row = take(partial_scores if step < n - 1 else last_scores, (shard - me - step + 2 * n) % n)
            scores = scores + lax.ppermute(row, ("dp", "mp"), pairs)
        return (rest(), scores)

    total = jnp.zeros((count, shards * block_rows), jnp.float32)
    for step in range(shards):
        back = partial_scores[step]
        if step > 0:
            back = lax.ppermute(back, "dp", [(source, (source - step) % shards) for source in range(shards)])
        total = lax.dynamic_update_slice(
            total, back, (jnp.int32(0), (shard + step) % shards * block_rows)
        )
    out_columns = shards * block_rows // n

    def columns_of(index):
        return lax.dynamic_slice(total, (jnp.int32(0), index * out_columns), (count, out_columns))

    scores = columns_of(me)
    for step in range(1, n):
        scores = scores + lax.ppermute(
            columns_of((me + step) % n), "mp", [(source, (source + step) % n) for source in range(n)]
        )
    return (rest(), scores)


def solution(mesh):
    in_specs = (
        P(("groups", "dp"), "mp"),
        P("mp", None),
        P(("groups", "dp", "mp"), None),
        P("mp", None),
        P(),
        P("dp", "mp"),
    )
    out_specs = (P(("groups", "dp"), "mp"), P(("groups", "dp"), "mp"))
    return jax.shard_map(
        on_device, mesh=mesh, in_specs=in_specs, out_specs=out_specs, check_vma=False
    )
```

```python
import functools

import jax
import jax.numpy as jnp
from jax import lax
from jax.experimental import pallas as pl
from jax.experimental.pallas import tpu as pltpu
from jax.sharding import PartitionSpec as P

SEQ = 1024


def three_terms(value):
    high = lax.reduce_precision(value, 8, 7)
    rest = value - high
    middle = lax.reduce_precision(rest, 8, 7)
    low = rest - middle
    return [term.astype(jnp.bfloat16) for term in (high, middle, low)]


def scores_kernel(shards, first, *refs):
    features, queries = refs[:shards], refs[shards]
    rows, found = refs[shards + 1 : -1], refs[-1]
    count = features[0].shape[0]
    value = jnp.concatenate([part[...] for part in features], axis=0)
    total = jnp.zeros(found.shape, jnp.float32)
    for _ in range(3):
        term = value.astype(jnp.bfloat16)
        value = value - term.astype(jnp.float32)
        total += lax.dot_general(
            term, queries[...], (((1,), (1,)), ((), ())), preferred_element_type=jnp.float32
        )
    found[...] = total
    for step, row in enumerate(rows):
        row[...] = found[pl.ds((first[0] - step + shards) % shards * count, count), :]


def scores_by_step(features, queries, first):
    shards = len(features)
    count = features[0].shape[0]
    block_rows = queries.shape[0]
    whole = pl.BlockSpec(memory_space=pltpu.VMEM)
    return pl.pallas_call(
        functools.partial(scores_kernel, shards),
        in_specs=[pl.BlockSpec(memory_space=pltpu.SMEM)] + [whole] * (shards + 1),
        out_specs=[whole] * shards,
        out_shape=[jax.ShapeDtypeStruct((count, block_rows), jnp.float32)] * shards,
        scratch_shapes=[pltpu.VMEM((shards * count, block_rows), jnp.float32)],
        compiler_params=pltpu.CompilerParams(vmem_limit_bytes=GRANT),
        name="scores",
    )(first.reshape(1).astype(jnp.int32), *features, queries)


def block_diagonal(proj_out):
    layers, width, rank = proj_out.shape
    zeros = jnp.zeros((width, rank), proj_out.dtype)
    return jnp.concatenate(
        [
            jnp.concatenate([proj_out[layer] if column == layer else zeros for column in range(layers)], axis=1)
            for layer in range(layers)
        ],
        axis=0,
    )


def times_width(rows, w_kv):
    return lax.dot_general(
        rows, w_kv, (((1,), (1,)), ((), ())), preferred_element_type=jnp.float32
    ).astype(jnp.bfloat16)


FETCH = 256
TILE = 512
GRANT = 24 * 2**20


def rows_kernel(block, start, count, me, *refs):
    firsts, seconds = refs[:count], refs[count : 2 * count]
    w_kv = refs[2 * count]
    out, held, weight, product, arrived, fetched, written = refs[-7:]
    mine = me[0]
    middle = (mine == 1) | (mine == 2)
    index = [mine, mine ^ 1, jnp.where(middle, mine ^ 3, mine ^ 2), jnp.where(middle, mine ^ 2, mine ^ 3)][block]
    use_second = jnp.logical_not(middle) if block > 1 else mine < 0

    fetches = []
    for piece in range(weight.shape[0] // FETCH):
        here = pl.ds(piece * FETCH, FETCH)
        fetches.append(pltpu.make_async_copy(w_kv.at[here], weight.at[here], fetched.at[piece]))
    loads = []
    filled = 0
    for part in range(count):
        rows = firsts[part].shape[0]
        here = held.at[pl.ds(filled, rows)]
        filled += rows
        loads.append(pltpu.make_async_copy(firsts[part], here, arrived.at[part]))
        late = pltpu.make_async_copy(seconds[part], here, arrived.at[part])
        if block > 1:
            pl.when(jnp.logical_not(use_second))(loads[-1].start)
            pl.when(use_second)(late.start)
        else:
            loads[-1].start()
    for fetch in fetches:
        fetch.start()
    for load in loads:
        load.wait()
    writes = []
    for tile in range(weight.shape[0] // TILE):
        here = pl.ds(tile * TILE, TILE)
        for piece in range(tile * TILE // FETCH, (tile + 1) * TILE // FETCH):
            fetches[piece].wait()
        product[:, here] = lax.dot_general(
            held[...], weight[here, :], (((1,), (1,)), ((), ())), preferred_element_type=jnp.float32
        ).astype(product.dtype)
        writes.append(
            pltpu.make_async_copy(
                product.at[:, here], out.at[index, pl.ds(start, product.shape[0]), here], written.at[tile]
            )
        )
        writes[-1].start()
    for write in writes:
        write.wait()


def put_rows(me, block, output, firsts, seconds, w_kv, block_rows, start=0):
    count = len(firsts)
    depth = firsts[0].shape[1]
    rows = sum(part.shape[0] for part in firsts)
    width = w_kv.shape[0]
    earlier = [] if output is None else [output]
    return pl.pallas_call(
        functools.partial(rows_kernel, block, start, count),
        in_specs=[pl.BlockSpec(memory_space=pltpu.SMEM)]
        + [pl.BlockSpec(memory_space=pl.ANY)] * (2 * count)
        + [pl.BlockSpec(memory_space=pltpu.HBM)] * (1 + len(earlier)),
        out_specs=pl.BlockSpec(memory_space=pltpu.HBM),
        scratch_shapes=[
            pltpu.VMEM((rows, depth), firsts[0].dtype),
            pltpu.VMEM((width, depth), w_kv.dtype),
            pltpu.VMEM((rows, width), jnp.bfloat16),
            pltpu.SemaphoreType.DMA((count,)),
            pltpu.SemaphoreType.DMA((width // FETCH,)),
            pltpu.SemaphoreType.DMA((width // TILE,)),
        ],
        out_shape=jax.ShapeDtypeStruct((4, block_rows, width), jnp.bfloat16),
        input_output_aliases={2 * count + 2: 0} if earlier else {},
        compiler_params=pltpu.CompilerParams(vmem_limit_bytes=GRANT),
        cost_estimate=pl.CostEstimate(flops=rows * width, bytes_accessed=rows * width, transcendentals=0),
        name="input_grad_rows",
    )(me.reshape(1).astype(jnp.int32), *firsts, *seconds, w_kv, *earlier)


def token_sums_kernel(me, low_in, low_in_beside, own_low, beside_low, facing_low, far_low, out):
    rows = own_low.shape[0]
    rank = out.shape[2]
    total = jnp.zeros((own_low.shape[1], own_low.shape[1]), jnp.float32)
    for away, low_out in (
        (0, own_low[...]),
        (1, beside_low[...]),
        (3, facing_low[...]),
        (2, far_low[...]),
    ):
        here = pl.ds(pl.multiple_of((me[0] ^ away) * rows, rows), rows)
        total += lax.dot_general(
            low_in[here, :] + low_in_beside[here, :],
            low_out,
            (((0,), (0,)), ((), ())),
            precision=lax.Precision.HIGHEST,
            preferred_element_type=jnp.float32,
        )
    slab = out.shape[1]
    for index in range(out.shape[0]):
        layer = index * slab // rank
        out[index] = total[index * slab : (index + 1) * slab, layer * rank : (layer + 1) * rank]


def token_sums(me, low_in, low_in_beside, own_low, beside_low, facing_low, far_low, rank):
    whole = pl.BlockSpec(memory_space=pltpu.VMEM)
    return pl.pallas_call(
        token_sums_kernel,
        in_specs=[pl.BlockSpec(memory_space=pltpu.SMEM)] + [whole] * 6,
        out_specs=whole,
        out_shape=jax.ShapeDtypeStruct((4, 2 * rank // 4, rank), jnp.float32),
        compiler_params=pltpu.CompilerParams(vmem_limit_bytes=GRANT),
        name="token_sums",
    )(me.reshape(1).astype(jnp.int32), low_in, low_in_beside, own_low, beside_low, facing_low, far_low)


def sequence_sums(low_in, low_out, rank):
    count = low_in.shape[0] // SEQ
    left = low_in.reshape(count, SEQ, 2 * rank)
    right = low_out.reshape(count, SEQ, 2 * rank)
    return jnp.concatenate(
        [
            lax.dot_general(
                left[:, :, layer * rank : (layer + 1) * rank],
                right[:, :, layer * rank : (layer + 1) * rank],
                (((1,), (1,)), ((0,), (0,))),
                precision=lax.Precision.HIGHEST,
                preferred_element_type=jnp.float32,
            )
            for layer in range(2)
        ],
        axis=1,
    )


def slabs_of(sums, n):
    count, height, rank = sums.shape
    return lax.optimization_barrier(sums.reshape(count, n, height // n, rank).transpose(1, 0, 2, 3))


def put(whole, piece, index):
    return lax.dynamic_update_slice(whole, piece[None], (index,) + (jnp.int32(0),) * piece.ndim)


def take(whole, index):
    return lax.dynamic_index_in_dim(whole, index, axis=0, keepdims=False)


def gathered(hidden, w_kv, grad_kv, proj_in, proj_out):
    n = lax.axis_size("mp")
    rank = proj_out.shape[2]
    whole = lax.all_gather(grad_kv, "mp", axis=0, tiled=True)
    input_grad = times_width(whole, w_kv)
    low_in = jnp.dot(hidden, proj_in, preferred_element_type=jnp.float32)
    sums = slabs_of(sequence_sums(low_in, jnp.dot(whole, block_diagonal(proj_out), preferred_element_type=jnp.float32), rank), n)
    features = lax.psum_scatter(sums, "mp", scatter_dimension=0, tiled=False)
    return features, lambda rows: rows, lambda: input_grad


def line_of_four(hidden, w_kv, grad_kv, proj_in, proj_out):
    rank = proj_out.shape[2]
    local_rows = grad_kv.shape[0]
    me = lax.axis_index("mp")
    middle = (me == 1) | (me == 2)
    exchange_pairs = [(0, 1), (1, 0), (2, 3), (3, 2)]
    across = [(1, 2), (2, 1)]
    outward = [(1, 0), (2, 3)]
    inward = [(0, 1), (3, 2)]
    tied = lax.optimization_barrier

    def low_rank(rows):
        return jnp.dot(rows, proj_both, preferred_element_type=jnp.float32)

    facing = lax.ppermute(grad_kv, "mp", across)
    beside = lax.ppermute(grad_kv, "mp", exchange_pairs)
    proj_both = tied(block_diagonal(proj_out))
    own_low = low_rank(grad_kv)
    low_in = jnp.dot(hidden, proj_in, preferred_element_type=jnp.float32)
    output = put_rows(me, 0, None, [grad_kv], [grad_kv], w_kv, local_rows)

    far_low = lax.ppermute(own_low, "mp", [(3, 1), (0, 2)])

    beside, low_in, far_low, output = tied((beside, low_in, far_low, output))
    beside_across = lax.ppermute(beside, "mp", across)
    second = lax.ppermute(facing, "mp", outward)
    low_in_beside = lax.ppermute(low_in, "mp", inward)
    output = put_rows(me, 1, output, [beside], [beside], w_kv, local_rows)

    low_in_beside, output = tied((low_in_beside, output))
    beside_low = low_rank(beside)
    facing_low = low_rank(facing)
    if low_in.shape[0] == SEQ:
        slabs = token_sums(me, low_in, low_in_beside, own_low, beside_low, facing_low, far_low, rank)[:, None]
    else:
        low_out = jnp.zeros((4, local_rows, 2 * rank), jnp.float32)
        for away, rows in ((0, own_low), (1, beside_low), (3, facing_low), (2, far_low)):
            low_out = put(low_out, rows, me ^ away)
        sums = sequence_sums(low_in + low_in_beside, low_out.reshape(4 * local_rows, 2 * rank), rank)
        slabs = slabs_of(sums, 4)
    slabs = slabs + lax.ppermute(slabs, "mp", across)

    beside_across, second, slabs, output = tied((beside_across, second, slabs, output))
    third = lax.ppermute(beside_across, "mp", outward)
    mine = lax.ppermute(take(slabs, me ^ 2), "mp", [(2, 0), (1, 3)])
    mine = jnp.where(middle, take(slabs, me), mine)
    output = put_rows(me, 2, output, [facing], [second], w_kv, local_rows)

    def finish(rows):
        rows = list(tied((*rows, output))[:-1])
        rows[-1] = tied((rows[-1], third))[0]
        return rows

    def rest():
        done = put_rows(me, 3, output, [beside_across], [third], w_kv, local_rows)
        return done.reshape(4 * local_rows, w_kv.shape[0])

    return mine, finish, rest


def on_device(hidden, w_kv, grad_kv, proj_in, proj_out, queries):
    n = lax.axis_size("mp")
    me = lax.axis_index("mp")
    mine, finish, rest = (line_of_four if n == 4 else gathered)(hidden, w_kv, grad_kv, proj_in, proj_out)
    count = mine.shape[0]

    shards = lax.axis_size("dp")
    shard = lax.axis_index("dp")
    block_rows = queries.shape[0]
    mine = mine.reshape(count, queries.shape[1])
    all_features = [mine] + [
        lax.ppermute(mine, "dp", [(source, (source + step) % shards) for source in range(shards)])
        for step in range(1, shards)
    ]
    if shards == n == 4:
        rows = finish(scores_by_step(all_features, queries, (shard - me + n) % n))
        scores = jnp.zeros((count, block_rows), jnp.float32)
        for step in range(n):
            pairs = [
                (q * n + slab, (slab + step) % n * n + q) for q in range(n) for slab in range(n)
            ]
            scores = scores + lax.ppermute(rows[step], ("dp", "mp"), pairs)
        return (rest(), scores)

    terms = jnp.concatenate(three_terms(jnp.concatenate(all_features, axis=0)), axis=0)
    products = lax.dot_general(
        terms, queries, (((1,), (1,)), ((), ())), preferred_element_type=jnp.float32
    ).reshape(3, shards, count, block_rows)
    partial_scores = products[0] + (products[1] + products[2])

    total = jnp.zeros((count, shards * block_rows), jnp.float32)
    for step in range(shards):
        back = partial_scores[step]
        if step > 0:
            back = lax.ppermute(back, "dp", [(source, (source - step) % shards) for source in range(shards)])
        total = lax.dynamic_update_slice(
            total, back, (jnp.int32(0), (shard + step) % shards * block_rows)
        )
    out_columns = shards * block_rows // n

    def columns_of(index):
        return lax.dynamic_slice(total, (jnp.int32(0), index * out_columns), (count, out_columns))

    scores = columns_of(me)
    for step in range(1, n):
        scores = scores + lax.ppermute(
            columns_of((me + step) % n), "mp", [(source, (source + step) % n) for source in range(n)]
        )
    return (rest(), scores)


def solution(mesh):
    in_specs = (
        P(("groups", "dp"), "mp"),
        P("mp", None),
        P(("groups", "dp", "mp"), None),
        P("mp", None),
        P(),
        P("dp", "mp"),
    )
    out_specs = (P(("groups", "dp"), "mp"), P(("groups", "dp"), "mp"))
    return jax.shard_map(
        on_device, mesh=mesh, in_specs=in_specs, out_specs=out_specs, check_vma=False
    )
```

```python
import functools

import jax
import jax.numpy as jnp
from jax import lax
from jax.experimental import pallas as pl
from jax.experimental.pallas import tpu as pltpu
from jax.sharding import PartitionSpec as P

SEQ = 1024


def three_terms(value):
    high = lax.reduce_precision(value, 8, 7)
    rest = value - high
    middle = lax.reduce_precision(rest, 8, 7)
    low = rest - middle
    return [term.astype(jnp.bfloat16) for term in (high, middle, low)]


def scores_kernel(shards, first, *refs):
    features, queries = refs[:shards], refs[shards]
    rows, found = refs[shards + 1 : -1], refs[-1]
    count = features[0].shape[0]
    value = jnp.concatenate([part[...] for part in features], axis=0)
    total = jnp.zeros(found.shape, jnp.float32)
    for _ in range(3):
        term = value.astype(jnp.bfloat16)
        value = value - term.astype(jnp.float32)
        total += lax.dot_general(
            term, queries[...], (((1,), (1,)), ((), ())), preferred_element_type=jnp.float32
        )
    found[...] = total
    for step, row in enumerate(rows):
        row[...] = found[pl.ds((first[0] - step + shards) % shards * count, count), :]


def scores_by_step(features, queries, first):
    shards = len(features)
    count = features[0].shape[0]
    block_rows = queries.shape[0]
    whole = pl.BlockSpec(memory_space=pltpu.VMEM)
    return pl.pallas_call(
        functools.partial(scores_kernel, shards),
        in_specs=[pl.BlockSpec(memory_space=pltpu.SMEM)] + [whole] * (shards + 1),
        out_specs=[whole] * shards,
        out_shape=[jax.ShapeDtypeStruct((count, block_rows), jnp.float32)] * shards,
        scratch_shapes=[pltpu.VMEM((shards * count, block_rows), jnp.float32)],
        compiler_params=pltpu.CompilerParams(vmem_limit_bytes=GRANT),
        name="scores",
    )(first.reshape(1).astype(jnp.int32), *features, queries)


def block_diagonal(proj_out):
    layers, width, rank = proj_out.shape
    zeros = jnp.zeros((width, rank), proj_out.dtype)
    return jnp.concatenate(
        [
            jnp.concatenate([proj_out[layer] if column == layer else zeros for column in range(layers)], axis=1)
            for layer in range(layers)
        ],
        axis=0,
    )


def times_width(rows, w_kv):
    return lax.dot_general(
        rows, w_kv, (((1,), (1,)), ((), ())), preferred_element_type=jnp.float32
    ).astype(jnp.bfloat16)


FETCH = 256
TILE = 512
GRANT = 48 * 2**20


def rows_kernel(block, start, count, me, *refs):
    firsts, seconds = refs[:count], refs[count : 2 * count]
    w_kv = refs[2 * count]
    out, held, weight, product, arrived, fetched, written = refs[-7:]
    mine = me[0]
    middle = (mine == 1) | (mine == 2)
    index = [mine, mine ^ 1, jnp.where(middle, mine ^ 3, mine ^ 2), jnp.where(middle, mine ^ 2, mine ^ 3)][block]
    use_second = jnp.logical_not(middle) if block > 1 else mine < 0

    fetches = []
    for piece in range(weight.shape[0] // FETCH):
        here = pl.ds(piece * FETCH, FETCH)
        fetches.append(pltpu.make_async_copy(w_kv.at[here], weight.at[here], fetched.at[piece]))
    loads = []
    filled = 0
    for part in range(count):
        rows = firsts[part].shape[0]
        here = held.at[pl.ds(filled, rows)]
        filled += rows
        loads.append(pltpu.make_async_copy(firsts[part], here, arrived.at[part]))
        late = pltpu.make_async_copy(seconds[part], here, arrived.at[part])
        if block > 1:
            pl.when(jnp.logical_not(use_second))(loads[-1].start)
            pl.when(use_second)(late.start)
        else:
            loads[-1].start()
    for fetch in fetches:
        fetch.start()
    for load in loads:
        load.wait()
    writes = []
    for tile in range(weight.shape[0] // TILE):
        here = pl.ds(tile * TILE, TILE)
        for piece in range(tile * TILE // FETCH, (tile + 1) * TILE // FETCH):
            fetches[piece].wait()
        product[:, here] = lax.dot_general(
            held[...], weight[here, :], (((1,), (1,)), ((), ())), preferred_element_type=jnp.float32
        ).astype(product.dtype)
        writes.append(
            pltpu.make_async_copy(
                product.at[:, here], out.at[index, pl.ds(start, product.shape[0]), here], written.at[tile]
            )
        )
        writes[-1].start()
    for write in writes:
        write.wait()


def put_rows(me, block, output, firsts, seconds, w_kv, block_rows, start=0):
    count = len(firsts)
    depth = firsts[0].shape[1]
    rows = sum(part.shape[0] for part in firsts)
    width = w_kv.shape[0]
    earlier = [] if output is None else [output]
    return pl.pallas_call(
        functools.partial(rows_kernel, block, start, count),
        in_specs=[pl.BlockSpec(memory_space=pltpu.SMEM)]
        + [pl.BlockSpec(memory_space=pl.ANY)] * (2 * count)
        + [pl.BlockSpec(memory_space=pltpu.HBM)] * (1 + len(earlier)),
        out_specs=pl.BlockSpec(memory_space=pltpu.HBM),
        scratch_shapes=[
            pltpu.VMEM((rows, depth), firsts[0].dtype),
            pltpu.VMEM((width, depth), w_kv.dtype),
            pltpu.VMEM((rows, width), jnp.bfloat16),
            pltpu.SemaphoreType.DMA((count,)),
            pltpu.SemaphoreType.DMA((width // FETCH,)),
            pltpu.SemaphoreType.DMA((width // TILE,)),
        ],
        out_shape=jax.ShapeDtypeStruct((4, block_rows, width), jnp.bfloat16),
        input_output_aliases={2 * count + 2: 0} if earlier else {},
        compiler_params=pltpu.CompilerParams(vmem_limit_bytes=GRANT),
        cost_estimate=pl.CostEstimate(flops=rows * width, bytes_accessed=rows * width, transcendentals=0),
        name="input_grad_rows",
    )(me.reshape(1).astype(jnp.int32), *firsts, *seconds, w_kv, *earlier)


def token_sums_kernel(me, low_in, low_in_beside, own_low, beside_low, facing_low, far_low, out):
    rows = own_low.shape[0]
    rank = out.shape[2]
    total = jnp.zeros((own_low.shape[1], own_low.shape[1]), jnp.float32)
    for away, low_out in (
        (0, own_low[...]),
        (1, beside_low[...]),
        (3, facing_low[...]),
        (2, far_low[...]),
    ):
        here = pl.ds(pl.multiple_of((me[0] ^ away) * rows, rows), rows)
        total += lax.dot_general(
            low_in[here, :] + low_in_beside[here, :],
            low_out,
            (((0,), (0,)), ((), ())),
            precision=lax.Precision.HIGHEST,
            preferred_element_type=jnp.float32,
        )
    slab = out.shape[1]
    for index in range(out.shape[0]):
        layer = index * slab // rank
        out[index] = total[index * slab : (index + 1) * slab, layer * rank : (layer + 1) * rank]


def token_sums(me, low_in, low_in_beside, own_low, beside_low, facing_low, far_low, rank):
    whole = pl.BlockSpec(memory_space=pltpu.VMEM)
    return pl.pallas_call(
        token_sums_kernel,
        in_specs=[pl.BlockSpec(memory_space=pltpu.SMEM)] + [whole] * 6,
        out_specs=whole,
        out_shape=jax.ShapeDtypeStruct((4, 2 * rank // 4, rank), jnp.float32),
        compiler_params=pltpu.CompilerParams(vmem_limit_bytes=GRANT),
        name="token_sums",
    )(me.reshape(1).astype(jnp.int32), low_in, low_in_beside, own_low, beside_low, facing_low, far_low)


def sequence_sums(low_in, low_out, rank):
    count = low_in.shape[0] // SEQ
    left = low_in.reshape(count, SEQ, 2 * rank)
    right = low_out.reshape(count, SEQ, 2 * rank)
    return jnp.concatenate(
        [
            lax.dot_general(
                left[:, :, layer * rank : (layer + 1) * rank],
                right[:, :, layer * rank : (layer + 1) * rank],
                (((1,), (1,)), ((0,), (0,))),
                precision=lax.Precision.HIGHEST,
                preferred_element_type=jnp.float32,
            )
            for layer in range(2)
        ],
        axis=1,
    )


def slabs_of(sums, n):
    count, height, rank = sums.shape
    return lax.optimization_barrier(sums.reshape(count, n, height // n, rank).transpose(1, 0, 2, 3))


def put(whole, piece, index):
    return lax.dynamic_update_slice(whole, piece[None], (index,) + (jnp.int32(0),) * piece.ndim)


def take(whole, index):
    return lax.dynamic_index_in_dim(whole, index, axis=0, keepdims=False)


def gathered(hidden, w_kv, grad_kv, proj_in, proj_out):
    n = lax.axis_size("mp")
    rank = proj_out.shape[2]
    whole = lax.all_gather(grad_kv, "mp", axis=0, tiled=True)
    input_grad = times_width(whole, w_kv)
    low_in = jnp.dot(hidden, proj_in, preferred_element_type=jnp.float32)
    sums = slabs_of(sequence_sums(low_in, jnp.dot(whole, block_diagonal(proj_out), preferred_element_type=jnp.float32), rank), n)
    features = lax.psum_scatter(sums, "mp", scatter_dimension=0, tiled=False)
    return features, lambda rows: rows, lambda: input_grad


def line_of_four(hidden, w_kv, grad_kv, proj_in, proj_out):
    rank = proj_out.shape[2]
    local_rows = grad_kv.shape[0]
    me = lax.axis_index("mp")
    middle = (me == 1) | (me == 2)
    exchange_pairs = [(0, 1), (1, 0), (2, 3), (3, 2)]
    across = [(1, 2), (2, 1)]
    outward = [(1, 0), (2, 3)]
    inward = [(0, 1), (3, 2)]
    tied = lax.optimization_barrier

    def low_rank(rows):
        return jnp.dot(rows, proj_both, preferred_element_type=jnp.float32)

    facing = lax.ppermute(grad_kv, "mp", across)
    beside = lax.ppermute(grad_kv, "mp", exchange_pairs)
    proj_both = tied(block_diagonal(proj_out))
    own_low = low_rank(grad_kv)
    low_in = jnp.dot(hidden, proj_in, preferred_element_type=jnp.float32)
    output = put_rows(me, 0, None, [grad_kv], [grad_kv], w_kv, local_rows)

    far_low = lax.ppermute(own_low, "mp", [(3, 1), (0, 2)])

    beside, low_in, far_low, output = tied((beside, low_in, far_low, output))
    beside_across = lax.ppermute(beside, "mp", across)
    second = lax.ppermute(facing, "mp", outward)
    low_in_beside = lax.ppermute(low_in, "mp", inward)
    output = put_rows(me, 1, output, [beside], [beside], w_kv, local_rows)

    low_in_beside, output = tied((low_in_beside, output))
    beside_low = low_rank(beside)
    facing_low = low_rank(facing)
    if low_in.shape[0] == SEQ:
        slabs = token_sums(me, low_in, low_in_beside, own_low, beside_low, facing_low, far_low, rank)[:, None]
    else:
        low_out = jnp.zeros((4, local_rows, 2 * rank), jnp.float32)
        for away, rows in ((0, own_low), (1, beside_low), (3, facing_low), (2, far_low)):
            low_out = put(low_out, rows, me ^ away)
        sums = sequence_sums(low_in + low_in_beside, low_out.reshape(4 * local_rows, 2 * rank), rank)
        slabs = slabs_of(sums, 4)
    slabs = slabs + lax.ppermute(slabs, "mp", across)

    beside_across, second, slabs, output = tied((beside_across, second, slabs, output))
    third = lax.ppermute(beside_across, "mp", outward)
    mine = lax.ppermute(take(slabs, me ^ 2), "mp", [(2, 0), (1, 3)])
    mine = jnp.where(middle, take(slabs, me), mine)
    output = put_rows(me, 2, output, [facing], [second], w_kv, local_rows)

    def finish(rows):
        rows = list(tied((*rows, output))[:-1])
        rows[-1] = tied((rows[-1], third))[0]
        return rows

    def rest():
        done = put_rows(me, 3, output, [beside_across], [third], w_kv, local_rows)
        return done.reshape(4 * local_rows, w_kv.shape[0])

    return mine, finish, rest


def on_device(hidden, w_kv, grad_kv, proj_in, proj_out, queries):
    n = lax.axis_size("mp")
    me = lax.axis_index("mp")
    mine, finish, rest = (line_of_four if n == 4 else gathered)(hidden, w_kv, grad_kv, proj_in, proj_out)
    count = mine.shape[0]

    shards = lax.axis_size("dp")
    shard = lax.axis_index("dp")
    block_rows = queries.shape[0]
    mine = mine.reshape(count, queries.shape[1])
    all_features = [mine] + [
        lax.ppermute(mine, "dp", [(source, (source + step) % shards) for source in range(shards)])
        for step in range(1, shards)
    ]
    if shards == n == 4:
        rows = finish(scores_by_step(all_features, queries, (shard - me + n) % n))
        scores = jnp.zeros((count, block_rows), jnp.float32)
        for step in range(n):
            pairs = [
                (q * n + slab, (slab + step) % n * n + q) for q in range(n) for slab in range(n)
            ]
            scores = scores + lax.ppermute(rows[step], ("dp", "mp"), pairs)
        return (rest(), scores)

    terms = jnp.concatenate(three_terms(jnp.concatenate(all_features, axis=0)), axis=0)
    products = lax.dot_general(
        terms, queries, (((1,), (1,)), ((), ())), preferred_element_type=jnp.float32
    ).reshape(3, shards, count, block_rows)
    partial_scores = products[0] + (products[1] + products[2])

    total = jnp.zeros((count, shards * block_rows), jnp.float32)
    for step in range(shards):
        back = partial_scores[step]
        if step > 0:
            back = lax.ppermute(back, "dp", [(source, (source - step) % shards) for source in range(shards)])
        total = lax.dynamic_update_slice(
            total, back, (jnp.int32(0), (shard + step) % shards * block_rows)
        )
    out_columns = shards * block_rows // n

    def columns_of(index):
        return lax.dynamic_slice(total, (jnp.int32(0), index * out_columns), (count, out_columns))

    scores = columns_of(me)
    for step in range(1, n):
        scores = scores + lax.ppermute(
            columns_of((me + step) % n), "mp", [(source, (source + step) % n) for source in range(n)]
        )
    return (rest(), scores)


def solution(mesh):
    in_specs = (
        P(("groups", "dp"), "mp"),
        P("mp", None),
        P(("groups", "dp", "mp"), None),
        P("mp", None),
        P(),
        P("dp", "mp"),
    )
    out_specs = (P(("groups", "dp"), "mp"), P(("groups", "dp"), "mp"))
    return jax.shard_map(
        on_device, mesh=mesh, in_specs=in_specs, out_specs=out_specs, check_vma=False
    )
```

```python
import functools

import jax
import jax.numpy as jnp
from jax import lax
from jax.experimental import pallas as pl
from jax.experimental.pallas import tpu as pltpu
from jax.sharding import PartitionSpec as P

SEQ = 1024


def three_terms(value):
    high = lax.reduce_precision(value, 8, 7)
    rest = value - high
    middle = lax.reduce_precision(rest, 8, 7)
    low = rest - middle
    return [term.astype(jnp.bfloat16) for term in (high, middle, low)]


def scores_kernel(shards, first, *refs):
    features, queries = refs[:shards], refs[shards]
    rows, found = refs[shards + 1 : -1], refs[-1]
    count = features[0].shape[0]
    value = jnp.concatenate([part[...] for part in features], axis=0)
    total = jnp.zeros(found.shape, jnp.float32)
    for _ in range(3):
        term = value.astype(jnp.bfloat16)
        value = value - term.astype(jnp.float32)
        total += lax.dot_general(
            term, queries[...], (((1,), (1,)), ((), ())), preferred_element_type=jnp.float32
        )
    found[...] = total
    for step, row in enumerate(rows):
        row[...] = found[pl.ds((first[0] - step + shards) % shards * count, count), :]


def scores_by_step(features, queries, first):
    shards = len(features)
    count = features[0].shape[0]
    block_rows = queries.shape[0]
    whole = pl.BlockSpec(memory_space=pltpu.VMEM)
    return pl.pallas_call(
        functools.partial(scores_kernel, shards),
        in_specs=[pl.BlockSpec(memory_space=pltpu.SMEM)] + [whole] * (shards + 1),
        out_specs=[whole] * shards,
        out_shape=[jax.ShapeDtypeStruct((count, block_rows), jnp.float32)] * shards,
        scratch_shapes=[pltpu.VMEM((shards * count, block_rows), jnp.float32)],
        compiler_params=pltpu.CompilerParams(vmem_limit_bytes=GRANT),
        name="scores",
    )(first.reshape(1).astype(jnp.int32), *features, queries)


def block_diagonal(proj_out):
    layers, width, rank = proj_out.shape
    zeros = jnp.zeros((width, rank), proj_out.dtype)
    return jnp.concatenate(
        [
            jnp.concatenate([proj_out[layer] if column == layer else zeros for column in range(layers)], axis=1)
            for layer in range(layers)
        ],
        axis=0,
    )


def times_width(rows, w_kv):
    return lax.dot_general(
        rows, w_kv, (((1,), (1,)), ((), ())), preferred_element_type=jnp.float32
    ).astype(jnp.bfloat16)


FETCH = 256
TILE = 512
GRANT = 48 * 2**20


def rows_kernel(block, start, count, me, *refs):
    firsts, seconds = refs[:count], refs[count : 2 * count]
    w_kv = refs[2 * count]
    out, held, weight, product, arrived, fetched, written = refs[-7:]
    mine = me[0]
    middle = (mine == 1) | (mine == 2)
    index = [mine, mine ^ 1, jnp.where(middle, mine ^ 3, mine ^ 2), jnp.where(middle, mine ^ 2, mine ^ 3)][block]
    use_second = jnp.logical_not(middle) if block > 1 else mine < 0

    fetches = []
    for piece in range(weight.shape[0] // FETCH):
        here = pl.ds(piece * FETCH, FETCH)
        fetches.append(pltpu.make_async_copy(w_kv.at[here], weight.at[here], fetched.at[piece]))
    loads = []
    filled = 0
    for part in range(count):
        rows = firsts[part].shape[0]
        here = held.at[pl.ds(filled, rows)]
        filled += rows
        loads.append(pltpu.make_async_copy(firsts[part], here, arrived.at[part]))
        late = pltpu.make_async_copy(seconds[part], here, arrived.at[part])
        if block > 1:
            pl.when(jnp.logical_not(use_second))(loads[-1].start)
            pl.when(use_second)(late.start)
        else:
            loads[-1].start()
    for fetch in fetches:
        fetch.start()
    for load in loads:
        load.wait()
    writes = []
    for tile in range(weight.shape[0] // TILE):
        here = pl.ds(tile * TILE, TILE)
        for piece in range(tile * TILE // FETCH, (tile + 1) * TILE // FETCH):
            fetches[piece].wait()
        product[:, here] = lax.dot_general(
            held[...], weight[here, :], (((1,), (1,)), ((), ())), preferred_element_type=jnp.float32
        ).astype(product.dtype)
        writes.append(
            pltpu.make_async_copy(
                product.at[:, here], out.at[index, pl.ds(start, product.shape[0]), here], written.at[tile]
            )
        )
        writes[-1].start()
    for write in writes:
        write.wait()


def put_rows(me, block, output, firsts, seconds, w_kv, block_rows, start=0):
    count = len(firsts)
    depth = firsts[0].shape[1]
    rows = sum(part.shape[0] for part in firsts)
    width = w_kv.shape[0]
    earlier = [] if output is None else [output]
    return pl.pallas_call(
        functools.partial(rows_kernel, block, start, count),
        in_specs=[pl.BlockSpec(memory_space=pltpu.SMEM)]
        + [pl.BlockSpec(memory_space=pl.ANY)] * (2 * count)
        + [pl.BlockSpec(memory_space=pltpu.HBM)] * (1 + len(earlier)),
        out_specs=pl.BlockSpec(memory_space=pltpu.HBM),
        scratch_shapes=[
            pltpu.VMEM((rows, depth), firsts[0].dtype),
            pltpu.VMEM((width, depth), w_kv.dtype),
            pltpu.VMEM((rows, width), jnp.bfloat16),
            pltpu.SemaphoreType.DMA((count,)),
            pltpu.SemaphoreType.DMA((width // FETCH,)),
            pltpu.SemaphoreType.DMA((width // TILE,)),
        ],
        out_shape=jax.ShapeDtypeStruct((4, block_rows, width), jnp.bfloat16),
        input_output_aliases={2 * count + 2: 0} if earlier else {},
        compiler_params=pltpu.CompilerParams(vmem_limit_bytes=GRANT if block < 3 else GRANT // 2 if block < 3 else GRANT // 2),
        cost_estimate=pl.CostEstimate(flops=rows * width, bytes_accessed=rows * width, transcendentals=0),
        name="input_grad_rows",
    )(me.reshape(1).astype(jnp.int32), *firsts, *seconds, w_kv, *earlier)


def token_sums_kernel(me, low_in, low_in_beside, own_low, beside_low, facing_low, far_low, out):
    rows = own_low.shape[0]
    rank = out.shape[2]
    total = jnp.zeros((own_low.shape[1], own_low.shape[1]), jnp.float32)
    for away, low_out in (
        (0, own_low[...]),
        (1, beside_low[...]),
        (3, facing_low[...]),
        (2, far_low[...]),
    ):
        here = pl.ds(pl.multiple_of((me[0] ^ away) * rows, rows), rows)
        total += lax.dot_general(
            low_in[here, :] + low_in_beside[here, :],
            low_out,
            (((0,), (0,)), ((), ())),
            precision=lax.Precision.HIGHEST,
            preferred_element_type=jnp.float32,
        )
    slab = out.shape[1]
    for index in range(out.shape[0]):
        layer = index * slab // rank
        out[index] = total[index * slab : (index + 1) * slab, layer * rank : (layer + 1) * rank]


def token_sums(me, low_in, low_in_beside, own_low, beside_low, facing_low, far_low, rank):
    whole = pl.BlockSpec(memory_space=pltpu.VMEM)
    return pl.pallas_call(
        token_sums_kernel,
        in_specs=[pl.BlockSpec(memory_space=pltpu.SMEM)] + [whole] * 6,
        out_specs=whole,
        out_shape=jax.ShapeDtypeStruct((4, 2 * rank // 4, rank), jnp.float32),
        compiler_params=pltpu.CompilerParams(vmem_limit_bytes=GRANT),
        name="token_sums",
    )(me.reshape(1).astype(jnp.int32), low_in, low_in_beside, own_low, beside_low, facing_low, far_low)


def sequence_sums(low_in, low_out, rank):
    count = low_in.shape[0] // SEQ
    left = low_in.reshape(count, SEQ, 2 * rank)
    right = low_out.reshape(count, SEQ, 2 * rank)
    return jnp.concatenate(
        [
            lax.dot_general(
                left[:, :, layer * rank : (layer + 1) * rank],
                right[:, :, layer * rank : (layer + 1) * rank],
                (((1,), (1,)), ((0,), (0,))),
                precision=lax.Precision.HIGHEST,
                preferred_element_type=jnp.float32,
            )
            for layer in range(2)
        ],
        axis=1,
    )


def slabs_of(sums, n):
    count, height, rank = sums.shape
    return lax.optimization_barrier(sums.reshape(count, n, height // n, rank).transpose(1, 0, 2, 3))


def put(whole, piece, index):
    return lax.dynamic_update_slice(whole, piece[None], (index,) + (jnp.int32(0),) * piece.ndim)


def take(whole, index):
    return lax.dynamic_index_in_dim(whole, index, axis=0, keepdims=False)


def gathered(hidden, w_kv, grad_kv, proj_in, proj_out):
    n = lax.axis_size("mp")
    rank = proj_out.shape[2]
    whole = lax.all_gather(grad_kv, "mp", axis=0, tiled=True)
    input_grad = times_width(whole, w_kv)
    low_in = jnp.dot(hidden, proj_in, preferred_element_type=jnp.float32)
    sums = slabs_of(sequence_sums(low_in, jnp.dot(whole, block_diagonal(proj_out), preferred_element_type=jnp.float32), rank), n)
    features = lax.psum_scatter(sums, "mp", scatter_dimension=0, tiled=False)
    return features, lambda rows: rows, lambda: input_grad


def line_of_four(hidden, w_kv, grad_kv, proj_in, proj_out):
    rank = proj_out.shape[2]
    local_rows = grad_kv.shape[0]
    me = lax.axis_index("mp")
    middle = (me == 1) | (me == 2)
    exchange_pairs = [(0, 1), (1, 0), (2, 3), (3, 2)]
    across = [(1, 2), (2, 1)]
    outward = [(1, 0), (2, 3)]
    inward = [(0, 1), (3, 2)]
    tied = lax.optimization_barrier

    def low_rank(rows):
        return jnp.dot(rows, proj_both, preferred_element_type=jnp.float32)

    facing = lax.ppermute(grad_kv, "mp", across)
    beside = lax.ppermute(grad_kv, "mp", exchange_pairs)
    proj_both = tied(block_diagonal(proj_out))
    own_low = low_rank(grad_kv)
    low_in = jnp.dot(hidden, proj_in, preferred_element_type=jnp.float32)
    output = put_rows(me, 0, None, [grad_kv], [grad_kv], w_kv, local_rows)

    far_low = lax.ppermute(own_low, "mp", [(3, 1), (0, 2)])

    beside, low_in, far_low, output = tied((beside, low_in, far_low, output))
    beside_across = lax.ppermute(beside, "mp", across)
    second = lax.ppermute(facing, "mp", outward)
    low_in_beside = lax.ppermute(low_in, "mp", inward)
    output = put_rows(me, 1, output, [beside], [beside], w_kv, local_rows)

    low_in_beside, output = tied((low_in_beside, output))
    beside_low = low_rank(beside)
    facing_low = low_rank(facing)
    if low_in.shape[0] == SEQ:
        slabs = token_sums(me, low_in, low_in_beside, own_low, beside_low, facing_low, far_low, rank)[:, None]
    else:
        low_out = jnp.zeros((4, local_rows, 2 * rank), jnp.float32)
        for away, rows in ((0, own_low), (1, beside_low), (3, facing_low), (2, far_low)):
            low_out = put(low_out, rows, me ^ away)
        sums = sequence_sums(low_in + low_in_beside, low_out.reshape(4 * local_rows, 2 * rank), rank)
        slabs = slabs_of(sums, 4)
    slabs_across = lax.ppermute(slabs, "mp", across)

    beside_across, slabs_across, output = tied((beside_across, slabs_across, output))
    third = lax.ppermute(beside_across, "mp", outward)
    slabs_across, second = tied((slabs_across, second))
    slabs = slabs + slabs_across
    mine = lax.ppermute(take(slabs, me ^ 2), "mp", [(2, 0), (1, 3)])
    mine = jnp.where(middle, take(slabs, me), mine)
    output = put_rows(me, 2, output, [facing], [second], w_kv, local_rows)

    def finish(rows):
        rows = list(tied((*rows, output))[:-1])
        rows[-1] = tied((rows[-1], third))[0]
        return rows

    def rest():
        done = put_rows(me, 3, output, [beside_across], [third], w_kv, local_rows)
        return done.reshape(4 * local_rows, w_kv.shape[0])

    return mine, finish, rest


def on_device(hidden, w_kv, grad_kv, proj_in, proj_out, queries):
    n = lax.axis_size("mp")
    me = lax.axis_index("mp")
    mine, finish, rest = (line_of_four if n == 4 else gathered)(hidden, w_kv, grad_kv, proj_in, proj_out)
    count = mine.shape[0]

    shards = lax.axis_size("dp")
    shard = lax.axis_index("dp")
    block_rows = queries.shape[0]
    mine = mine.reshape(count, queries.shape[1])
    all_features = [mine] + [
        lax.ppermute(mine, "dp", [(source, (source + step) % shards) for source in range(shards)])
        for step in range(1, shards)
    ]
    if shards == n == 4:
        rows = finish(scores_by_step(all_features, queries, (shard - me + n) % n))
        scores = jnp.zeros((count, block_rows), jnp.float32)
        for step in range(n):
            pairs = [
                (q * n + slab, (slab + step) % n * n + q) for q in range(n) for slab in range(n)
            ]
            scores = scores + lax.ppermute(rows[step], ("dp", "mp"), pairs)
        return (rest(), scores)

    terms = jnp.concatenate(three_terms(jnp.concatenate(all_features, axis=0)), axis=0)
    products = lax.dot_general(
        terms, queries, (((1,), (1,)), ((), ())), preferred_element_type=jnp.float32
    ).reshape(3, shards, count, block_rows)
    partial_scores = products[0] + (products[1] + products[2])

    total = jnp.zeros((count, shards * block_rows), jnp.float32)
    for step in range(shards):
        back = partial_scores[step]
        if step > 0:
            back = lax.ppermute(back, "dp", [(source, (source - step) % shards) for source in range(shards)])
        total = lax.dynamic_update_slice(
            total, back, (jnp.int32(0), (shard + step) % shards * block_rows)
        )
    out_columns = shards * block_rows // n

    def columns_of(index):
        return lax.dynamic_slice(total, (jnp.int32(0), index * out_columns), (count, out_columns))

    scores = columns_of(me)
    for step in range(1, n):
        scores = scores + lax.ppermute(
            columns_of((me + step) % n), "mp", [(source, (source + step) % n) for source in range(n)]
        )
    return (rest(), scores)


def solution(mesh):
    in_specs = (
        P(("groups", "dp"), "mp"),
        P("mp", None),
        P(("groups", "dp", "mp"), None),
        P("mp", None),
        P(),
        P("dp", "mp"),
    )
    out_specs = (P(("groups", "dp"), "mp"), P(("groups", "dp"), "mp"))
    return jax.shard_map(
        on_device, mesh=mesh, in_specs=in_specs, out_specs=out_specs, check_vma=False
    )
```

```python
import functools

import jax
import jax.numpy as jnp
from jax import lax
from jax.experimental import pallas as pl
from jax.experimental.pallas import tpu as pltpu
from jax.sharding import PartitionSpec as P

SEQ = 1024


def three_terms(value):
    high = lax.reduce_precision(value, 8, 7)
    rest = value - high
    middle = lax.reduce_precision(rest, 8, 7)
    low = rest - middle
    return [term.astype(jnp.bfloat16) for term in (high, middle, low)]


def scores_kernel(shards, first, *refs):
    features, queries = refs[:shards], refs[shards]
    rows, found = refs[shards + 1 : -1], refs[-1]
    count = features[0].shape[0]
    value = jnp.concatenate([part[...] for part in features], axis=0)
    total = jnp.zeros(found.shape, jnp.float32)
    for _ in range(3):
        term = value.astype(jnp.bfloat16)
        value = value - term.astype(jnp.float32)
        total += lax.dot_general(
            term, queries[...], (((1,), (1,)), ((), ())), preferred_element_type=jnp.float32
        )
    found[...] = total
    for step, row in enumerate(rows):
        row[...] = found[pl.ds((first[0] - step + shards) % shards * count, count), :]


def scores_by_step(features, queries, first):
    shards = len(features)
    count = features[0].shape[0]
    block_rows = queries.shape[0]
    whole = pl.BlockSpec(memory_space=pltpu.VMEM)
    return pl.pallas_call(
        functools.partial(scores_kernel, shards),
        in_specs=[pl.BlockSpec(memory_space=pltpu.SMEM)] + [whole] * (shards + 1),
        out_specs=[whole] * shards,
        out_shape=[jax.ShapeDtypeStruct((count, block_rows), jnp.float32)] * shards,
        scratch_shapes=[pltpu.VMEM((shards * count, block_rows), jnp.float32)],
        compiler_params=pltpu.CompilerParams(vmem_limit_bytes=GRANT),
        name="scores",
    )(first.reshape(1).astype(jnp.int32), *features, queries)


def block_diagonal(proj_out):
    layers, width, rank = proj_out.shape
    zeros = jnp.zeros((width, rank), proj_out.dtype)
    return jnp.concatenate(
        [
            jnp.concatenate([proj_out[layer] if column == layer else zeros for column in range(layers)], axis=1)
            for layer in range(layers)
        ],
        axis=0,
    )


def times_width(rows, w_kv):
    return lax.dot_general(
        rows, w_kv, (((1,), (1,)), ((), ())), preferred_element_type=jnp.float32
    ).astype(jnp.bfloat16)


TILE = 256
AHEAD = 3
GRANT = 48 * 2**20


def rows_kernel(block, start, count, me, *refs):
    firsts, seconds = refs[:count], refs[count : 2 * count]
    w_kv = refs[2 * count]
    out, held, weight, product, arrived, fetched, written = refs[-7:]
    mine = me[0]
    middle = (mine == 1) | (mine == 2)
    index = [mine, mine ^ 1, jnp.where(middle, mine ^ 3, mine ^ 2), jnp.where(middle, mine ^ 2, mine ^ 3)][block]
    use_second = jnp.logical_not(middle) if block > 1 else mine < 0

    fetches = []
    for piece in range(weight.shape[0] // TILE):
        here = pl.ds(piece * TILE, TILE)
        fetches.append(pltpu.make_async_copy(w_kv.at[here], weight.at[here], fetched.at[piece]))
    loads = []
    filled = 0
    for part in range(count):
        rows = firsts[part].shape[0]
        here = held.at[pl.ds(filled, rows)]
        filled += rows
        loads.append(pltpu.make_async_copy(firsts[part], here, arrived.at[part]))
        late = pltpu.make_async_copy(seconds[part], here, arrived.at[part])
        if block > 1:
            pl.when(jnp.logical_not(use_second))(loads[-1].start)
            pl.when(use_second)(late.start)
        else:
            loads[-1].start()
    for fetch in fetches[:AHEAD]:
        fetch.start()
    for load in loads:
        load.wait()
    writes = []
    for tile in range(weight.shape[0] // TILE):
        here = pl.ds(tile * TILE, TILE)
        fetches[tile].wait()
        if tile + AHEAD < len(fetches):
            fetches[tile + AHEAD].start()
        product[:, here] = lax.dot_general(
            held[...], weight[here, :], (((1,), (1,)), ((), ())), preferred_element_type=jnp.float32
        ).astype(product.dtype)
        writes.append(
            pltpu.make_async_copy(
                product.at[:, here], out.at[index, pl.ds(start, product.shape[0]), here], written.at[tile]
            )
        )
        writes[-1].start()
    for write in writes:
        write.wait()


def put_rows(me, block, output, firsts, seconds, w_kv, block_rows, start=0):
    count = len(firsts)
    depth = firsts[0].shape[1]
    rows = sum(part.shape[0] for part in firsts)
    width = w_kv.shape[0]
    earlier = [] if output is None else [output]
    return pl.pallas_call(
        functools.partial(rows_kernel, block, start, count),
        in_specs=[pl.BlockSpec(memory_space=pltpu.SMEM)]
        + [pl.BlockSpec(memory_space=pl.ANY)] * (2 * count)
        + [pl.BlockSpec(memory_space=pltpu.HBM)] * (1 + len(earlier)),
        out_specs=pl.BlockSpec(memory_space=pltpu.HBM),
        scratch_shapes=[
            pltpu.VMEM((rows, depth), firsts[0].dtype),
            pltpu.VMEM((width, depth), w_kv.dtype),
            pltpu.VMEM((rows, width), jnp.bfloat16),
            pltpu.SemaphoreType.DMA((count,)),
            pltpu.SemaphoreType.DMA((width // TILE,)),
            pltpu.SemaphoreType.DMA((width // TILE,)),
        ],
        out_shape=jax.ShapeDtypeStruct((4, block_rows, width), jnp.bfloat16),
        input_output_aliases={2 * count + 2: 0} if earlier else {},
        compiler_params=pltpu.CompilerParams(vmem_limit_bytes=GRANT),
        cost_estimate=pl.CostEstimate(flops=rows * width, bytes_accessed=rows * width, transcendentals=0),
        name="input_grad_rows",
    )(me.reshape(1).astype(jnp.int32), *firsts, *seconds, w_kv, *earlier)


def token_sums_kernel(me, low_in, low_in_beside, own_low, beside_low, facing_low, far_low, out):
    rows = own_low.shape[0]
    rank = out.shape[2]
    total = jnp.zeros((own_low.shape[1], own_low.shape[1]), jnp.float32)
    for away, low_out in (
        (0, own_low[...]),
        (1, beside_low[...]),
        (3, facing_low[...]),
        (2, far_low[...]),
    ):
        here = pl.ds(pl.multiple_of((me[0] ^ away) * rows, rows), rows)
        total += lax.dot_general(
            low_in[here, :] + low_in_beside[here, :],
            low_out,
            (((0,), (0,)), ((), ())),
            precision=lax.Precision.HIGHEST,
            preferred_element_type=jnp.float32,
        )
    slab = out.shape[1]
    for index in range(out.shape[0]):
        layer = index * slab // rank
        out[index] = total[index * slab : (index + 1) * slab, layer * rank : (layer + 1) * rank]


def token_sums(me, low_in, low_in_beside, own_low, beside_low, facing_low, far_low, rank):
    whole = pl.BlockSpec(memory_space=pltpu.VMEM)
    return pl.pallas_call(
        token_sums_kernel,
        in_specs=[pl.BlockSpec(memory_space=pltpu.SMEM)] + [whole] * 6,
        out_specs=whole,
        out_shape=jax.ShapeDtypeStruct((4, 2 * rank // 4, rank), jnp.float32),
        compiler_params=pltpu.CompilerParams(vmem_limit_bytes=GRANT),
        name="token_sums",
    )(me.reshape(1).astype(jnp.int32), low_in, low_in_beside, own_low, beside_low, facing_low, far_low)


def sequence_sums(low_in, low_out, rank):
    count = low_in.shape[0] // SEQ
    left = low_in.reshape(count, SEQ, 2 * rank)
    right = low_out.reshape(count, SEQ, 2 * rank)
    return jnp.concatenate(
        [
            lax.dot_general(
                left[:, :, layer * rank : (layer + 1) * rank],
                right[:, :, layer * rank : (layer + 1) * rank],
                (((1,), (1,)), ((0,), (0,))),
                precision=lax.Precision.HIGHEST,
                preferred_element_type=jnp.float32,
            )
            for layer in range(2)
        ],
        axis=1,
    )


def slabs_of(sums, n):
    count, height, rank = sums.shape
    return lax.optimization_barrier(sums.reshape(count, n, height // n, rank).transpose(1, 0, 2, 3))


def put(whole, piece, index):
    return lax.dynamic_update_slice(whole, piece[None], (index,) + (jnp.int32(0),) * piece.ndim)


def take(whole, index):
    return lax.dynamic_index_in_dim(whole, index, axis=0, keepdims=False)


def gathered(hidden, w_kv, grad_kv, proj_in, proj_out):
    n = lax.axis_size("mp")
    rank = proj_out.shape[2]
    whole = lax.all_gather(grad_kv, "mp", axis=0, tiled=True)
    input_grad = times_width(whole, w_kv)
    low_in = jnp.dot(hidden, proj_in, preferred_element_type=jnp.float32)
    sums = slabs_of(sequence_sums(low_in, jnp.dot(whole, block_diagonal(proj_out), preferred_element_type=jnp.float32), rank), n)
    features = lax.psum_scatter(sums, "mp", scatter_dimension=0, tiled=False)
    return features, lambda rows: rows, lambda: input_grad


def line_of_four(hidden, w_kv, grad_kv, proj_in, proj_out):
    rank = proj_out.shape[2]
    local_rows = grad_kv.shape[0]
    me = lax.axis_index("mp")
    middle = (me == 1) | (me == 2)
    exchange_pairs = [(0, 1), (1, 0), (2, 3), (3, 2)]
    across = [(1, 2), (2, 1)]
    outward = [(1, 0), (2, 3)]
    inward = [(0, 1), (3, 2)]
    tied = lax.optimization_barrier

    def low_rank(rows):
        return jnp.dot(rows, proj_both, preferred_element_type=jnp.float32)

    facing = lax.ppermute(grad_kv, "mp", across)
    beside = lax.ppermute(grad_kv, "mp", exchange_pairs)
    proj_both = tied(block_diagonal(proj_out))
    own_low = low_rank(grad_kv)
    low_in = jnp.dot(hidden, proj_in, preferred_element_type=jnp.float32)
    output = put_rows(me, 0, None, [grad_kv], [grad_kv], w_kv, local_rows)


    beside, low_in, output = tied((beside, low_in, output))
    beside_across = lax.ppermute(beside, "mp", across)
    second = lax.ppermute(facing, "mp", outward)
    low_in_beside = lax.ppermute(low_in, "mp", inward)
    output = put_rows(me, 1, output, [beside], [beside], w_kv, local_rows)

    beside_low = low_rank(beside)
    facing_low = low_rank(facing)

    beside_across, output = tied((beside_across, output))
    third = lax.ppermute(beside_across, "mp", outward)

    far_low = low_rank(beside_across)
    if low_in.shape[0] == SEQ:
        slabs = token_sums(me, low_in, low_in_beside, own_low, beside_low, facing_low, far_low, rank)[:, None]
    else:
        low_out = jnp.zeros((4, local_rows, 2 * rank), jnp.float32)
        for away, rows in ((0, own_low), (1, beside_low), (3, facing_low), (2, far_low)):
            low_out = put(low_out, rows, me ^ away)
        sums = sequence_sums(low_in + low_in_beside, low_out.reshape(4 * local_rows, 2 * rank), rank)
        slabs = slabs_of(sums, 4)
    slabs_across = lax.ppermute(slabs, "mp", across)
    slabs_across, second = tied((slabs_across, second))
    slabs = slabs + slabs_across
    mine = lax.ppermute(take(slabs, me ^ 2), "mp", [(2, 0), (1, 3)])
    mine = jnp.where(middle, take(slabs, me), mine)
    output = put_rows(me, 2, output, [facing], [second], w_kv, local_rows)

    def finish(rows):
        rows = list(tied((*rows, output))[:-1])
        rows[-1] = tied((rows[-1], third))[0]
        return rows

    def rest():
        done = put_rows(me, 3, output, [beside_across], [third], w_kv, local_rows)
        return done.reshape(4 * local_rows, w_kv.shape[0])

    return mine, finish, rest


def on_device(hidden, w_kv, grad_kv, proj_in, proj_out, queries):
    n = lax.axis_size("mp")
    me = lax.axis_index("mp")
    mine, finish, rest = (line_of_four if n == 4 else gathered)(hidden, w_kv, grad_kv, proj_in, proj_out)
    count = mine.shape[0]

    shards = lax.axis_size("dp")
    shard = lax.axis_index("dp")
    block_rows = queries.shape[0]
    mine = mine.reshape(count, queries.shape[1])
    all_features = [mine] + [
        lax.ppermute(mine, "dp", [(source, (source + step) % shards) for source in range(shards)])
        for step in range(1, shards)
    ]
    if shards == n == 4:
        rows = finish(scores_by_step(all_features, queries, (shard - me + n) % n))
        scores = jnp.zeros((count, block_rows), jnp.float32)
        for step in range(n):
            pairs = [
                (q * n + slab, (slab + step) % n * n + q) for q in range(n) for slab in range(n)
            ]
            scores = scores + lax.ppermute(rows[step], ("dp", "mp"), pairs)
        return (rest(), scores)

    terms = jnp.concatenate(three_terms(jnp.concatenate(all_features, axis=0)), axis=0)
    products = lax.dot_general(
        terms, queries, (((1,), (1,)), ((), ())), preferred_element_type=jnp.float32
    ).reshape(3, shards, count, block_rows)
    partial_scores = products[0] + (products[1] + products[2])

    total = jnp.zeros((count, shards * block_rows), jnp.float32)
    for step in range(shards):
        back = partial_scores[step]
        if step > 0:
            back = lax.ppermute(back, "dp", [(source, (source - step) % shards) for source in range(shards)])
        total = lax.dynamic_update_slice(
            total, back, (jnp.int32(0), (shard + step) % shards * block_rows)
        )
    out_columns = shards * block_rows // n

    def columns_of(index):
        return lax.dynamic_slice(total, (jnp.int32(0), index * out_columns), (count, out_columns))

    scores = columns_of(me)
    for step in range(1, n):
        scores = scores + lax.ppermute(
            columns_of((me + step) % n), "mp", [(source, (source + step) % n) for source in range(n)]
        )
    return (rest(), scores)


def solution(mesh):
    in_specs = (
        P(("groups", "dp"), "mp"),
        P("mp", None),
        P(("groups", "dp", "mp"), None),
        P("mp", None),
        P(),
        P("dp", "mp"),
    )
    out_specs = (P(("groups", "dp"), "mp"), P(("groups", "dp"), "mp"))
    return jax.shard_map(
        on_device, mesh=mesh, in_specs=in_specs, out_specs=out_specs, check_vma=False
    )
```

```python
import functools

import jax
import jax.numpy as jnp
from jax import lax
from jax.experimental import pallas as pl
from jax.experimental.pallas import tpu as pltpu
from jax.sharding import PartitionSpec as P

SEQ = 1024


def three_terms(value):
    high = lax.reduce_precision(value, 8, 7)
    rest = value - high
    middle = lax.reduce_precision(rest, 8, 7)
    low = rest - middle
    return [term.astype(jnp.bfloat16) for term in (high, middle, low)]


def scores_kernel(shards, first, *refs):
    features, queries = refs[:shards], refs[shards]
    rows, found = refs[shards + 1 : -1], refs[-1]
    count = features[0].shape[0]
    value = jnp.concatenate([part[...] for part in features], axis=0)
    total = jnp.zeros(found.shape, jnp.float32)
    for _ in range(3):
        term = value.astype(jnp.bfloat16)
        value = value - term.astype(jnp.float32)
        total += lax.dot_general(
            term, queries[...], (((1,), (1,)), ((), ())), preferred_element_type=jnp.float32
        )
    found[...] = total
    for step, row in enumerate(rows):
        row[...] = found[pl.ds((first[0] - step + shards) % shards * count, count), :]


def scores_by_step(features, queries, first):
    shards = len(features)
    count = features[0].shape[0]
    block_rows = queries.shape[0]
    whole = pl.BlockSpec(memory_space=pltpu.VMEM)
    return pl.pallas_call(
        functools.partial(scores_kernel, shards),
        in_specs=[pl.BlockSpec(memory_space=pltpu.SMEM)] + [whole] * (shards + 1),
        out_specs=[whole] * shards,
        out_shape=[jax.ShapeDtypeStruct((count, block_rows), jnp.float32)] * shards,
        scratch_shapes=[pltpu.VMEM((shards * count, block_rows), jnp.float32)],
        compiler_params=pltpu.CompilerParams(vmem_limit_bytes=GRANT),
        name="scores",
    )(first.reshape(1).astype(jnp.int32), *features, queries)


def block_diagonal(proj_out):
    layers, width, rank = proj_out.shape
    zeros = jnp.zeros((width, rank), proj_out.dtype)
    return jnp.concatenate(
        [
            jnp.concatenate([proj_out[layer] if column == layer else zeros for column in range(layers)], axis=1)
            for layer in range(layers)
        ],
        axis=0,
    )


def times_width(rows, w_kv):
    return lax.dot_general(
        rows, w_kv, (((1,), (1,)), ((), ())), preferred_element_type=jnp.float32
    ).astype(jnp.bfloat16)


FETCH = 256
TILE = 512
GRANT = 48 * 2**20


def rows_kernel(block, start, count, me, *refs):
    firsts, seconds = refs[:count], refs[count : 2 * count]
    w_kv = refs[2 * count]
    out, held, weight, product, arrived, fetched, written = refs[-7:]
    mine = me[0]
    middle = (mine == 1) | (mine == 2)
    index = [mine, mine ^ 1, jnp.where(middle, mine ^ 3, mine ^ 2), jnp.where(middle, mine ^ 2, mine ^ 3)][block]
    use_second = jnp.logical_not(middle) if block > 1 else mine < 0

    fetches = []
    for piece in range(weight.shape[0] // FETCH):
        here = pl.ds(piece * FETCH, FETCH)
        fetches.append(pltpu.make_async_copy(w_kv.at[here], weight.at[here], fetched.at[piece]))
    loads = []
    filled = 0
    for part in range(count):
        rows = firsts[part].shape[0]
        here = held.at[pl.ds(filled, rows)]
        filled += rows
        loads.append(pltpu.make_async_copy(firsts[part], here, arrived.at[part]))
        late = pltpu.make_async_copy(seconds[part], here, arrived.at[part])
        if block > 1:
            pl.when(jnp.logical_not(use_second))(loads[-1].start)
            pl.when(use_second)(late.start)
        else:
            loads[-1].start()
    for fetch in fetches:
        fetch.start()
    for load in loads:
        load.wait()
    writes = []
    for tile in range(weight.shape[0] // TILE):
        here = pl.ds(tile * TILE, TILE)
        for piece in range(tile * TILE // FETCH, (tile + 1) * TILE // FETCH):
            fetches[piece].wait()
        product[:, here] = lax.dot_general(
            held[...], weight[here, :], (((1,), (1,)), ((), ())), preferred_element_type=jnp.float32
        ).astype(product.dtype)
        writes.append(
            pltpu.make_async_copy(
                product.at[:, here], out.at[index, pl.ds(start, product.shape[0]), here], written.at[tile]
            )
        )
        writes[-1].start()
    for write in writes:
        write.wait()


def put_rows(me, block, output, firsts, seconds, w_kv, block_rows, start=0):
    count = len(firsts)
    depth = firsts[0].shape[1]
    rows = sum(part.shape[0] for part in firsts)
    width = w_kv.shape[0]
    earlier = [] if output is None else [output]
    return pl.pallas_call(
        functools.partial(rows_kernel, block, start, count),
        in_specs=[pl.BlockSpec(memory_space=pltpu.SMEM)]
        + [pl.BlockSpec(memory_space=pl.ANY)] * (2 * count)
        + [pl.BlockSpec(memory_space=pltpu.HBM)] * (1 + len(earlier)),
        out_specs=pl.BlockSpec(memory_space=pltpu.HBM),
        scratch_shapes=[
            pltpu.VMEM((rows, depth), firsts[0].dtype),
            pltpu.VMEM((width, depth), w_kv.dtype),
            pltpu.VMEM((rows, width), jnp.bfloat16),
            pltpu.SemaphoreType.DMA((count,)),
            pltpu.SemaphoreType.DMA((width // FETCH,)),
            pltpu.SemaphoreType.DMA((width // TILE,)),
        ],
        out_shape=jax.ShapeDtypeStruct((4, block_rows, width), jnp.bfloat16),
        input_output_aliases={2 * count + 2: 0} if earlier else {},
        compiler_params=pltpu.CompilerParams(vmem_limit_bytes=GRANT),
        cost_estimate=pl.CostEstimate(flops=rows * width, bytes_accessed=rows * width, transcendentals=0),
        name="input_grad_rows",
    )(me.reshape(1).astype(jnp.int32), *firsts, *seconds, w_kv, *earlier)


def token_sums_kernel(me, low_in, low_in_beside, own_low, beside_low, facing_low, far_low, out):
    rows = own_low.shape[0]
    rank = out.shape[2]
    total = jnp.zeros((own_low.shape[1], own_low.shape[1]), jnp.float32)
    for away, low_out in (
        (0, own_low[...]),
        (1, beside_low[...]),
        (3, facing_low[...]),
        (2, far_low[...]),
    ):
        here = pl.ds(pl.multiple_of((me[0] ^ away) * rows, rows), rows)
        total += lax.dot_general(
            low_in[here, :] + low_in_beside[here, :],
            low_out,
            (((0,), (0,)), ((), ())),
            precision=lax.Precision.HIGHEST,
            preferred_element_type=jnp.float32,
        )
    slab = out.shape[1]
    for index in range(out.shape[0]):
        layer = index * slab // rank
        out[index] = total[index * slab : (index + 1) * slab, layer * rank : (layer + 1) * rank]


def token_sums(me, low_in, low_in_beside, own_low, beside_low, facing_low, far_low, rank):
    whole = pl.BlockSpec(memory_space=pltpu.VMEM)
    return pl.pallas_call(
        token_sums_kernel,
        in_specs=[pl.BlockSpec(memory_space=pltpu.SMEM)] + [whole] * 6,
        out_specs=whole,
        out_shape=jax.ShapeDtypeStruct((4, 2 * rank // 4, rank), jnp.float32),
        compiler_params=pltpu.CompilerParams(vmem_limit_bytes=GRANT),
        name="token_sums",
    )(me.reshape(1).astype(jnp.int32), low_in, low_in_beside, own_low, beside_low, facing_low, far_low)


def sequence_sums(low_in, low_out, rank):
    count = low_in.shape[0] // SEQ
    left = low_in.reshape(count, SEQ, 2 * rank)
    right = low_out.reshape(count, SEQ, 2 * rank)
    return jnp.concatenate(
        [
            lax.dot_general(
                left[:, :, layer * rank : (layer + 1) * rank],
                right[:, :, layer * rank : (layer + 1) * rank],
                (((1,), (1,)), ((0,), (0,))),
                precision=lax.Precision.HIGHEST,
                preferred_element_type=jnp.float32,
            )
            for layer in range(2)
        ],
        axis=1,
    )


def slabs_of(sums, n):
    count, height, rank = sums.shape
    return lax.optimization_barrier(sums.reshape(count, n, height // n, rank).transpose(1, 0, 2, 3))


def put(whole, piece, index):
    return lax.dynamic_update_slice(whole, piece[None], (index,) + (jnp.int32(0),) * piece.ndim)


def take(whole, index):
    return lax.dynamic_index_in_dim(whole, index, axis=0, keepdims=False)


def gathered(hidden, w_kv, grad_kv, proj_in, proj_out):
    n = lax.axis_size("mp")
    rank = proj_out.shape[2]
    whole = lax.all_gather(grad_kv, "mp", axis=0, tiled=True)
    input_grad = times_width(whole, w_kv)
    low_in = jnp.dot(hidden, proj_in, preferred_element_type=jnp.float32)
    sums = slabs_of(sequence_sums(low_in, jnp.dot(whole, block_diagonal(proj_out), preferred_element_type=jnp.float32), rank), n)
    features = lax.psum_scatter(sums, "mp", scatter_dimension=0, tiled=False)
    return features, lambda rows: rows, lambda: input_grad


def line_of_four(hidden, w_kv, grad_kv, proj_in, proj_out):
    rank = proj_out.shape[2]
    local_rows = grad_kv.shape[0]
    me = lax.axis_index("mp")
    middle = (me == 1) | (me == 2)
    exchange_pairs = [(0, 1), (1, 0), (2, 3), (3, 2)]
    across = [(1, 2), (2, 1)]
    outward = [(1, 0), (2, 3)]
    inward = [(0, 1), (3, 2)]
    tied = lax.optimization_barrier

    def low_rank(rows):
        return jnp.dot(rows, proj_both, preferred_element_type=jnp.float32)

    facing = lax.ppermute(grad_kv, "mp", across)
    beside = lax.ppermute(grad_kv, "mp", exchange_pairs)
    proj_both = tied(block_diagonal(proj_out))
    own_low = low_rank(grad_kv)
    low_in = jnp.dot(hidden, proj_in, preferred_element_type=jnp.float32)
    output = put_rows(me, 0, None, [grad_kv], [grad_kv], w_kv, local_rows)


    beside, low_in, output = tied((beside, low_in, output))
    beside_across = lax.ppermute(beside, "mp", across)
    second = lax.ppermute(facing, "mp", outward)
    low_in_beside = lax.ppermute(low_in, "mp", inward)
    output = put_rows(me, 1, output, [beside], [beside], w_kv, local_rows)

    beside_low = low_rank(beside)
    facing_low = low_rank(facing)

    beside_across, output = tied((beside_across, output))
    third = lax.ppermute(beside_across, "mp", outward)

    far_low = low_rank(beside_across)
    if low_in.shape[0] == SEQ:
        slabs = token_sums(me, low_in, low_in_beside, own_low, beside_low, facing_low, far_low, rank)[:, None]
    else:
        low_out = jnp.zeros((4, local_rows, 2 * rank), jnp.float32)
        for away, rows in ((0, own_low), (1, beside_low), (3, facing_low), (2, far_low)):
            low_out = put(low_out, rows, me ^ away)
        sums = sequence_sums(low_in + low_in_beside, low_out.reshape(4 * local_rows, 2 * rank), rank)
        slabs = slabs_of(sums, 4)
    slabs_across = lax.ppermute(slabs, "mp", across)
    slabs_across, second = tied((slabs_across, second))
    slabs = slabs + slabs_across
    mine = lax.ppermute(take(slabs, me ^ 2), "mp", [(2, 0), (1, 3)])
    mine = jnp.where(middle, take(slabs, me), mine)
    output = put_rows(me, 2, output, [facing], [second], w_kv, local_rows)
    mine, output = tied((mine, output))

    def finish(rows):
        rows = list(tied((*rows, output))[:-1])
        rows[-1] = tied((rows[-1], third))[0]
        return rows

    def rest():
        done = put_rows(me, 3, output, [beside_across], [third], w_kv, local_rows)
        return done.reshape(4 * local_rows, w_kv.shape[0])

    return mine, finish, rest


def on_device(hidden, w_kv, grad_kv, proj_in, proj_out, queries):
    n = lax.axis_size("mp")
    me = lax.axis_index("mp")
    mine, finish, rest = (line_of_four if n == 4 else gathered)(hidden, w_kv, grad_kv, proj_in, proj_out)
    count = mine.shape[0]

    shards = lax.axis_size("dp")
    shard = lax.axis_index("dp")
    block_rows = queries.shape[0]
    mine = mine.reshape(count, queries.shape[1])
    all_features = [mine] + [
        lax.ppermute(mine, "dp", [(source, (source + step) % shards) for source in range(shards)])
        for step in range(1, shards)
    ]
    if shards == n == 4:
        rows = finish(scores_by_step(all_features, queries, (shard - me + n) % n))
        scores = jnp.zeros((count, block_rows), jnp.float32)
        for step in range(n):
            pairs = [
                (q * n + slab, (slab + step) % n * n + q) for q in range(n) for slab in range(n)
            ]
            scores = scores + lax.ppermute(rows[step], ("dp", "mp"), pairs)
        return (rest(), scores)

    terms = jnp.concatenate(three_terms(jnp.concatenate(all_features, axis=0)), axis=0)
    products = lax.dot_general(
        terms, queries, (((1,), (1,)), ((), ())), preferred_element_type=jnp.float32
    ).reshape(3, shards, count, block_rows)
    partial_scores = products[0] + (products[1] + products[2])

    total = jnp.zeros((count, shards * block_rows), jnp.float32)
    for step in range(shards):
        back = partial_scores[step]
        if step > 0:
            back = lax.ppermute(back, "dp", [(source, (source - step) % shards) for source in range(shards)])
        total = lax.dynamic_update_slice(
            total, back, (jnp.int32(0), (shard + step) % shards * block_rows)
        )
    out_columns = shards * block_rows // n

    def columns_of(index):
        return lax.dynamic_slice(total, (jnp.int32(0), index * out_columns), (count, out_columns))

    scores = columns_of(me)
    for step in range(1, n):
        scores = scores + lax.ppermute(
            columns_of((me + step) % n), "mp", [(source, (source + step) % n) for source in range(n)]
        )
    return (rest(), scores)


def solution(mesh):
    in_specs = (
        P(("groups", "dp"), "mp"),
        P("mp", None),
        P(("groups", "dp", "mp"), None),
        P("mp", None),
        P(),
        P("dp", "mp"),
    )
    out_specs = (P(("groups", "dp"), "mp"), P(("groups", "dp"), "mp"))
    return jax.shard_map(
        on_device, mesh=mesh, in_specs=in_specs, out_specs=out_specs, check_vma=False
    )
```

```python
import functools

import jax
import jax.numpy as jnp
from jax import lax
from jax.experimental import pallas as pl
from jax.experimental.pallas import tpu as pltpu
from jax.sharding import PartitionSpec as P

SEQ = 1024


def three_terms(value):
    high = lax.reduce_precision(value, 8, 7)
    rest = value - high
    middle = lax.reduce_precision(rest, 8, 7)
    low = rest - middle
    return [term.astype(jnp.bfloat16) for term in (high, middle, low)]


def scores_kernel(shards, first, *refs):
    features, queries = refs[:shards], refs[shards]
    rows, found = refs[shards + 1 : -1], refs[-1]
    count = features[0].shape[0]
    value = jnp.concatenate([part[...] for part in features], axis=0)
    total = jnp.zeros(found.shape, jnp.float32)
    for _ in range(3):
        term = value.astype(jnp.bfloat16)
        value = value - term.astype(jnp.float32)
        total += lax.dot_general(
            term, queries[...], (((1,), (1,)), ((), ())), preferred_element_type=jnp.float32
        )
    found[...] = total
    for step, row in enumerate(rows):
        row[...] = found[pl.ds((first[0] - step + shards) % shards * count, count), :]


def scores_by_step(features, queries, first):
    shards = len(features)
    count = features[0].shape[0]
    block_rows = queries.shape[0]
    whole = pl.BlockSpec(memory_space=pltpu.VMEM)
    return pl.pallas_call(
        functools.partial(scores_kernel, shards),
        in_specs=[pl.BlockSpec(memory_space=pltpu.SMEM)] + [whole] * (shards + 1),
        out_specs=[whole] * shards,
        out_shape=[jax.ShapeDtypeStruct((count, block_rows), jnp.float32)] * shards,
        scratch_shapes=[pltpu.VMEM((shards * count, block_rows), jnp.float32)],
        compiler_params=pltpu.CompilerParams(vmem_limit_bytes=GRANT),
        name="scores",
    )(first.reshape(1).astype(jnp.int32), *features, queries)


def block_diagonal(proj_out):
    layers, width, rank = proj_out.shape
    zeros = jnp.zeros((width, rank), proj_out.dtype)
    return jnp.concatenate(
        [
            jnp.concatenate([proj_out[layer] if column == layer else zeros for column in range(layers)], axis=1)
            for layer in range(layers)
        ],
        axis=0,
    )


def times_width(rows, w_kv):
    return lax.dot_general(
        rows, w_kv, (((1,), (1,)), ((), ())), preferred_element_type=jnp.float32
    ).astype(jnp.bfloat16)


FETCH = 256
TILE = 1024
GRANT = 48 * 2**20


def rows_kernel(block, start, count, me, *refs):
    firsts, seconds = refs[:count], refs[count : 2 * count]
    w_kv = refs[2 * count]
    out, held, weight, product, arrived, fetched, written = refs[-7:]
    mine = me[0]
    middle = (mine == 1) | (mine == 2)
    index = [mine, mine ^ 1, jnp.where(middle, mine ^ 3, mine ^ 2), jnp.where(middle, mine ^ 2, mine ^ 3)][block]
    use_second = jnp.logical_not(middle) if block > 1 else mine < 0

    fetches = []
    for piece in range(weight.shape[0] // FETCH):
        here = pl.ds(piece * FETCH, FETCH)
        fetches.append(pltpu.make_async_copy(w_kv.at[here], weight.at[here], fetched.at[piece]))
    loads = []
    filled = 0
    for part in range(count):
        rows = firsts[part].shape[0]
        here = held.at[pl.ds(filled, rows)]
        filled += rows
        loads.append(pltpu.make_async_copy(firsts[part], here, arrived.at[part]))
        late = pltpu.make_async_copy(seconds[part], here, arrived.at[part])
        if block > 1:
            pl.when(jnp.logical_not(use_second))(loads[-1].start)
            pl.when(use_second)(late.start)
        else:
            loads[-1].start()
    for fetch in fetches:
        fetch.start()
    for load in loads:
        load.wait()
    writes = []
    for tile in range(weight.shape[0] // TILE):
        here = pl.ds(tile * TILE, TILE)
        for piece in range(tile * TILE // FETCH, (tile + 1) * TILE // FETCH):
            fetches[piece].wait()
        product[:, here] = lax.dot_general(
            held[...], weight[here, :], (((1,), (1,)), ((), ())), preferred_element_type=jnp.float32
        ).astype(product.dtype)
        writes.append(
            pltpu.make_async_copy(
                product.at[:, here], out.at[index, pl.ds(start, product.shape[0]), here], written.at[tile]
            )
        )
        writes[-1].start()
    for write in writes:
        write.wait()


def put_rows(me, block, output, firsts, seconds, w_kv, block_rows, start=0):
    count = len(firsts)
    depth = firsts[0].shape[1]
    rows = sum(part.shape[0] for part in firsts)
    width = w_kv.shape[0]
    earlier = [] if output is None else [output]
    return pl.pallas_call(
        functools.partial(rows_kernel, block, start, count),
        in_specs=[pl.BlockSpec(memory_space=pltpu.SMEM)]
        + [pl.BlockSpec(memory_space=pl.ANY)] * (2 * count)
        + [pl.BlockSpec(memory_space=pltpu.HBM)] * (1 + len(earlier)),
        out_specs=pl.BlockSpec(memory_space=pltpu.HBM),
        scratch_shapes=[
            pltpu.VMEM((rows, depth), firsts[0].dtype),
            pltpu.VMEM((width, depth), w_kv.dtype),
            pltpu.VMEM((rows, width), jnp.bfloat16),
            pltpu.SemaphoreType.DMA((count,)),
            pltpu.SemaphoreType.DMA((width // FETCH,)),
            pltpu.SemaphoreType.DMA((width // TILE,)),
        ],
        out_shape=jax.ShapeDtypeStruct((4, block_rows, width), jnp.bfloat16),
        input_output_aliases={2 * count + 2: 0} if earlier else {},
        compiler_params=pltpu.CompilerParams(vmem_limit_bytes=GRANT),
        cost_estimate=pl.CostEstimate(flops=rows * width, bytes_accessed=rows * width, transcendentals=0),
        name="input_grad_rows",
    )(me.reshape(1).astype(jnp.int32), *firsts, *seconds, w_kv, *earlier)


def token_sums_kernel(me, low_in, low_in_beside, own_low, beside_low, facing_low, far_low, out):
    rows = own_low.shape[0]
    rank = out.shape[2]
    total = jnp.zeros((own_low.shape[1], own_low.shape[1]), jnp.float32)
    for away, low_out in (
        (0, own_low[...]),
        (1, beside_low[...]),
        (3, facing_low[...]),
        (2, far_low[...]),
    ):
        here = pl.ds(pl.multiple_of((me[0] ^ away) * rows, rows), rows)
        total += lax.dot_general(
            low_in[here, :] + low_in_beside[here, :],
            low_out,
            (((0,), (0,)), ((), ())),
            precision=lax.Precision.HIGHEST,
            preferred_element_type=jnp.float32,
        )
    slab = out.shape[1]
    for index in range(out.shape[0]):
        layer = index * slab // rank
        out[index] = total[index * slab : (index + 1) * slab, layer * rank : (layer + 1) * rank]


def token_sums(me, low_in, low_in_beside, own_low, beside_low, facing_low, far_low, rank):
    whole = pl.BlockSpec(memory_space=pltpu.VMEM)
    return pl.pallas_call(
        token_sums_kernel,
        in_specs=[pl.BlockSpec(memory_space=pltpu.SMEM)] + [whole] * 6,
        out_specs=whole,
        out_shape=jax.ShapeDtypeStruct((4, 2 * rank // 4, rank), jnp.float32),
        compiler_params=pltpu.CompilerParams(vmem_limit_bytes=GRANT),
        name="token_sums",
    )(me.reshape(1).astype(jnp.int32), low_in, low_in_beside, own_low, beside_low, facing_low, far_low)


def sequence_sums(low_in, low_out, rank):
    count = low_in.shape[0] // SEQ
    left = low_in.reshape(count, SEQ, 2 * rank)
    right = low_out.reshape(count, SEQ, 2 * rank)
    return jnp.concatenate(
        [
            lax.dot_general(
                left[:, :, layer * rank : (layer + 1) * rank],
                right[:, :, layer * rank : (layer + 1) * rank],
                (((1,), (1,)), ((0,), (0,))),
                precision=lax.Precision.HIGHEST,
                preferred_element_type=jnp.float32,
            )
            for layer in range(2)
        ],
        axis=1,
    )


def slabs_of(sums, n):
    count, height, rank = sums.shape
    return lax.optimization_barrier(sums.reshape(count, n, height // n, rank).transpose(1, 0, 2, 3))


def put(whole, piece, index):
    return lax.dynamic_update_slice(whole, piece[None], (index,) + (jnp.int32(0),) * piece.ndim)


def take(whole, index):
    return lax.dynamic_index_in_dim(whole, index, axis=0, keepdims=False)


def gathered(hidden, w_kv, grad_kv, proj_in, proj_out):
    n = lax.axis_size("mp")
    rank = proj_out.shape[2]
    whole = lax.all_gather(grad_kv, "mp", axis=0, tiled=True)
    input_grad = times_width(whole, w_kv)
    low_in = jnp.dot(hidden, proj_in, preferred_element_type=jnp.float32)
    sums = slabs_of(sequence_sums(low_in, jnp.dot(whole, block_diagonal(proj_out), preferred_element_type=jnp.float32), rank), n)
    features = lax.psum_scatter(sums, "mp", scatter_dimension=0, tiled=False)
    return features, lambda rows: rows, lambda: input_grad


def line_of_four(hidden, w_kv, grad_kv, proj_in, proj_out):
    rank = proj_out.shape[2]
    local_rows = grad_kv.shape[0]
    me = lax.axis_index("mp")
    middle = (me == 1) | (me == 2)
    exchange_pairs = [(0, 1), (1, 0), (2, 3), (3, 2)]
    across = [(1, 2), (2, 1)]
    outward = [(1, 0), (2, 3)]
    inward = [(0, 1), (3, 2)]
    tied = lax.optimization_barrier

    def low_rank(rows):
        return jnp.dot(rows, proj_both, preferred_element_type=jnp.float32)

    facing = lax.ppermute(grad_kv, "mp", across)
    beside = lax.ppermute(grad_kv, "mp", exchange_pairs)
    proj_both = tied(block_diagonal(proj_out))
    own_low = low_rank(grad_kv)
    low_in = jnp.dot(hidden, proj_in, preferred_element_type=jnp.float32)
    output = put_rows(me, 0, None, [grad_kv], [grad_kv], w_kv, local_rows)

    far_low = lax.ppermute(own_low, "mp", [(3, 1), (0, 2)])

    beside, low_in, far_low, output = tied((beside, low_in, far_low, output))
    beside_across = lax.ppermute(beside, "mp", across)
    second = lax.ppermute(facing, "mp", outward)
    low_in_beside = lax.ppermute(low_in, "mp", inward)
    output = put_rows(me, 1, output, [beside], [beside], w_kv, local_rows)

    low_in_beside, output = tied((low_in_beside, output))
    beside_low = low_rank(beside)
    facing_low = low_rank(facing)
    if low_in.shape[0] == SEQ:
        slabs = token_sums(me, low_in, low_in_beside, own_low, beside_low, facing_low, far_low, rank)[:, None]
    else:
        low_out = jnp.zeros((4, local_rows, 2 * rank), jnp.float32)
        for away, rows in ((0, own_low), (1, beside_low), (3, facing_low), (2, far_low)):
            low_out = put(low_out, rows, me ^ away)
        sums = sequence_sums(low_in + low_in_beside, low_out.reshape(4 * local_rows, 2 * rank), rank)
        slabs = slabs_of(sums, 4)
    slabs_across = lax.ppermute(slabs, "mp", across)

    beside_across, slabs_across, output = tied((beside_across, slabs_across, output))
    third = lax.ppermute(beside_across, "mp", outward)
    slabs_across, second = tied((slabs_across, second))
    slabs = slabs + slabs_across
    mine = lax.ppermute(take(slabs, me ^ 2), "mp", [(2, 0), (1, 3)])
    mine = jnp.where(middle, take(slabs, me), mine)
    output = put_rows(me, 2, output, [facing], [second], w_kv, local_rows)

    def finish(rows):
        rows = list(tied((*rows, output))[:-1])
        rows[-1] = tied((rows[-1], third))[0]
        return rows

    def rest():
        done = put_rows(me, 3, output, [beside_across], [third], w_kv, local_rows)
        return done.reshape(4 * local_rows, w_kv.shape[0])

    return mine, finish, rest


def on_device(hidden, w_kv, grad_kv, proj_in, proj_out, queries):
    n = lax.axis_size("mp")
    me = lax.axis_index("mp")
    mine, finish, rest = (line_of_four if n == 4 else gathered)(hidden, w_kv, grad_kv, proj_in, proj_out)
    count = mine.shape[0]

    shards = lax.axis_size("dp")
    shard = lax.axis_index("dp")
    block_rows = queries.shape[0]
    mine = mine.reshape(count, queries.shape[1])
    all_features = [mine] + [
        lax.ppermute(mine, "dp", [(source, (source + step) % shards) for source in range(shards)])
        for step in range(1, shards)
    ]
    if shards == n == 4:
        rows = finish(scores_by_step(all_features, queries, (shard - me + n) % n))
        scores = jnp.zeros((count, block_rows), jnp.float32)
        for step in range(n):
            pairs = [
                (q * n + slab, (slab + step) % n * n + q) for q in range(n) for slab in range(n)
            ]
            scores = scores + lax.ppermute(rows[step], ("dp", "mp"), pairs)
        return (rest(), scores)

    terms = jnp.concatenate(three_terms(jnp.concatenate(all_features, axis=0)), axis=0)
    products = lax.dot_general(
        terms, queries, (((1,), (1,)), ((), ())), preferred_element_type=jnp.float32
    ).reshape(3, shards, count, block_rows)
    partial_scores = products[0] + (products[1] + products[2])

    total = jnp.zeros((count, shards * block_rows), jnp.float32)
    for step in range(shards):
        back = partial_scores[step]
        if step > 0:
            back = lax.ppermute(back, "dp", [(source, (source - step) % shards) for source in range(shards)])
        total = lax.dynamic_update_slice(
            total, back, (jnp.int32(0), (shard + step) % shards * block_rows)
        )
    out_columns = shards * block_rows // n

    def columns_of(index):
        return lax.dynamic_slice(total, (jnp.int32(0), index * out_columns), (count, out_columns))

    scores = columns_of(me)
    for step in range(1, n):
        scores = scores + lax.ppermute(
            columns_of((me + step) % n), "mp", [(source, (source + step) % n) for source in range(n)]
        )
    return (rest(), scores)


def solution(mesh):
    in_specs = (
        P(("groups", "dp"), "mp"),
        P("mp", None),
        P(("groups", "dp", "mp"), None),
        P("mp", None),
        P(),
        P("dp", "mp"),
    )
    out_specs = (P(("groups", "dp"), "mp"), P(("groups", "dp"), "mp"))
    return jax.shard_map(
        on_device, mesh=mesh, in_specs=in_specs, out_specs=out_specs, check_vma=False
    )
```

```python
import functools

import jax
import jax.numpy as jnp
from jax import lax
from jax.experimental import pallas as pl
from jax.experimental.pallas import tpu as pltpu
from jax.sharding import PartitionSpec as P

SEQ = 1024


def three_terms(value):
    high = lax.reduce_precision(value, 8, 7)
    rest = value - high
    middle = lax.reduce_precision(rest, 8, 7)
    low = rest - middle
    return [term.astype(jnp.bfloat16) for term in (high, middle, low)]


def scores_kernel(shards, first, *refs):
    features, queries = refs[:shards], refs[shards]
    rows, found = refs[shards + 1 : -1], refs[-1]
    count = features[0].shape[0]
    value = jnp.concatenate([part[...] for part in features], axis=0)
    total = jnp.zeros(found.shape, jnp.float32)
    for _ in range(3):
        term = value.astype(jnp.bfloat16)
        value = value - term.astype(jnp.float32)
        total += lax.dot_general(
            term, queries[...], (((1,), (1,)), ((), ())), preferred_element_type=jnp.float32
        )
    found[...] = total
    for step, row in enumerate(rows):
        row[...] = found[pl.ds((first[0] - step + shards) % shards * count, count), :]


def scores_by_step(features, queries, first):
    shards = len(features)
    count = features[0].shape[0]
    block_rows = queries.shape[0]
    whole = pl.BlockSpec(memory_space=pltpu.VMEM)
    return pl.pallas_call(
        functools.partial(scores_kernel, shards),
        in_specs=[pl.BlockSpec(memory_space=pltpu.SMEM)] + [whole] * (shards + 1),
        out_specs=[whole] * shards,
        out_shape=[jax.ShapeDtypeStruct((count, block_rows), jnp.float32)] * shards,
        scratch_shapes=[pltpu.VMEM((shards * count, block_rows), jnp.float32)],
        compiler_params=pltpu.CompilerParams(vmem_limit_bytes=GRANT),
        name="scores",
    )(first.reshape(1).astype(jnp.int32), *features, queries)


def block_diagonal(proj_out):
    layers, width, rank = proj_out.shape
    zeros = jnp.zeros((width, rank), proj_out.dtype)
    return jnp.concatenate(
        [
            jnp.concatenate([proj_out[layer] if column == layer else zeros for column in range(layers)], axis=1)
            for layer in range(layers)
        ],
        axis=0,
    )


def times_width(rows, w_kv):
    return lax.dot_general(
        rows, w_kv, (((1,), (1,)), ((), ())), preferred_element_type=jnp.float32
    ).astype(jnp.bfloat16)


FETCH = 256
TILE = 512
GRANT = 48 * 2**20


def rows_kernel(block, start, count, me, *refs):
    firsts, seconds = refs[:count], refs[count : 2 * count]
    w_kv = refs[2 * count]
    out, held, weight, product, arrived, fetched, written = refs[-7:]
    mine = me[0]
    middle = (mine == 1) | (mine == 2)
    index = [mine, mine ^ 1, jnp.where(middle, mine ^ 3, mine ^ 2), jnp.where(middle, mine ^ 2, mine ^ 3)][block]
    use_second = jnp.logical_not(middle) if block > 1 else mine < 0

    fetches = []
    for piece in range(weight.shape[0] // FETCH):
        here = pl.ds(piece * FETCH, FETCH)
        fetches.append(pltpu.make_async_copy(w_kv.at[here], weight.at[here], fetched.at[piece]))
    loads = []
    filled = 0
    for part in range(count):
        rows = firsts[part].shape[0]
        here = held.at[pl.ds(filled, rows)]
        filled += rows
        loads.append(pltpu.make_async_copy(firsts[part], here, arrived.at[part]))
        late = pltpu.make_async_copy(seconds[part], here, arrived.at[part])
        if block > 1:
            pl.when(jnp.logical_not(use_second))(loads[-1].start)
            pl.when(use_second)(late.start)
        else:
            loads[-1].start()
    for fetch in fetches:
        fetch.start()
    for load in loads:
        load.wait()
    writes = []
    for tile in range(weight.shape[0] // TILE):
        here = pl.ds(tile * TILE, TILE)
        for piece in range(tile * TILE // FETCH, (tile + 1) * TILE // FETCH):
            fetches[piece].wait()
        product[:, here] = lax.dot_general(
            held[...], weight[here, :], (((1,), (1,)), ((), ())), preferred_element_type=jnp.float32
        ).astype(product.dtype)
        writes.append(
            pltpu.make_async_copy(
                product.at[:, here], out.at[index, pl.ds(start, product.shape[0]), here], written.at[tile]
            )
        )
        writes[-1].start()
    for write in writes:
        write.wait()


def put_rows(me, block, output, firsts, seconds, w_kv, block_rows, start=0):
    count = len(firsts)
    depth = firsts[0].shape[1]
    rows = sum(part.shape[0] for part in firsts)
    width = w_kv.shape[0]
    earlier = [] if output is None else [output]
    return pl.pallas_call(
        functools.partial(rows_kernel, block, start, count),
        in_specs=[pl.BlockSpec(memory_space=pltpu.SMEM)]
        + [pl.BlockSpec(memory_space=pl.ANY)] * (2 * count)
        + [pl.BlockSpec(memory_space=pltpu.HBM)] * (1 + len(earlier)),
        out_specs=pl.BlockSpec(memory_space=pltpu.HBM),
        scratch_shapes=[
            pltpu.VMEM((rows, depth), firsts[0].dtype),
            pltpu.VMEM((width, depth), w_kv.dtype),
            pltpu.VMEM((rows, width), jnp.bfloat16),
            pltpu.SemaphoreType.DMA((count,)),
            pltpu.SemaphoreType.DMA((width // FETCH,)),
            pltpu.SemaphoreType.DMA((width // TILE,)),
        ],
        out_shape=jax.ShapeDtypeStruct((4, block_rows, width), jnp.bfloat16),
        input_output_aliases={2 * count + 2: 0} if earlier else {},
        compiler_params=pltpu.CompilerParams(vmem_limit_bytes=GRANT),
        cost_estimate=pl.CostEstimate(flops=rows * width, bytes_accessed=rows * width, transcendentals=0),
        name="input_grad_rows",
    )(me.reshape(1).astype(jnp.int32), *firsts, *seconds, w_kv, *earlier)


def token_sums_kernel(me, low_in, low_in_beside, own_low, beside_low, facing_low, far_low, out):
    rows = own_low.shape[0]
    rank = out.shape[2]
    total = jnp.zeros((own_low.shape[1], own_low.shape[1]), jnp.float32)
    for away, low_out in (
        (0, own_low[...]),
        (1, beside_low[...]),
        (3, facing_low[...]),
        (2, far_low[...]),
    ):
        here = pl.ds(pl.multiple_of((me[0] ^ away) * rows, rows), rows)
        total += lax.dot_general(
            low_in[here, :] + low_in_beside[here, :],
            low_out,
            (((0,), (0,)), ((), ())),
            precision=lax.Precision.HIGHEST,
            preferred_element_type=jnp.float32,
        )
    slab = out.shape[1]
    for index in range(out.shape[0]):
        layer = index * slab // rank
        out[index] = total[index * slab : (index + 1) * slab, layer * rank : (layer + 1) * rank]


def token_sums(me, low_in, low_in_beside, own_low, beside_low, facing_low, far_low, rank):
    whole = pl.BlockSpec(memory_space=pltpu.VMEM)
    return pl.pallas_call(
        token_sums_kernel,
        in_specs=[pl.BlockSpec(memory_space=pltpu.SMEM)] + [whole] * 6,
        out_specs=whole,
        out_shape=jax.ShapeDtypeStruct((4, 2 * rank // 4, rank), jnp.float32),
        compiler_params=pltpu.CompilerParams(vmem_limit_bytes=GRANT),
        name="token_sums",
    )(me.reshape(1).astype(jnp.int32), low_in, low_in_beside, own_low, beside_low, facing_low, far_low)


def sequence_sums(low_in, low_out, rank):
    count = low_in.shape[0] // SEQ
    left = low_in.reshape(count, SEQ, 2 * rank)
    right = low_out.reshape(count, SEQ, 2 * rank)
    return jnp.concatenate(
        [
            lax.dot_general(
                left[:, :, layer * rank : (layer + 1) * rank],
                right[:, :, layer * rank : (layer + 1) * rank],
                (((1,), (1,)), ((0,), (0,))),
                precision=lax.Precision.HIGHEST,
                preferred_element_type=jnp.float32,
            )
            for layer in range(2)
        ],
        axis=1,
    )


def slabs_of(sums, n):
    count, height, rank = sums.shape
    return lax.optimization_barrier(sums.reshape(count, n, height // n, rank).transpose(1, 0, 2, 3))


def put(whole, piece, index):
    return lax.dynamic_update_slice(whole, piece[None], (index,) + (jnp.int32(0),) * piece.ndim)


def take(whole, index):
    return lax.dynamic_index_in_dim(whole, index, axis=0, keepdims=False)


def gathered(hidden, w_kv, grad_kv, proj_in, proj_out):
    n = lax.axis_size("mp")
    rank = proj_out.shape[2]
    whole = lax.all_gather(grad_kv, "mp", axis=0, tiled=True)
    input_grad = times_width(whole, w_kv)
    low_in = jnp.dot(hidden, proj_in, preferred_element_type=jnp.float32)
    sums = slabs_of(sequence_sums(low_in, jnp.dot(whole, block_diagonal(proj_out), preferred_element_type=jnp.float32), rank), n)
    features = lax.psum_scatter(sums, "mp", scatter_dimension=0, tiled=False)
    return features, lambda rows: rows, lambda: input_grad


def line_of_four(hidden, w_kv, grad_kv, proj_in, proj_out):
    rank = proj_out.shape[2]
    local_rows = grad_kv.shape[0]
    me = lax.axis_index("mp")
    middle = (me == 1) | (me == 2)
    exchange_pairs = [(0, 1), (1, 0), (2, 3), (3, 2)]
    across = [(1, 2), (2, 1)]
    outward = [(1, 0), (2, 3)]
    inward = [(0, 1), (3, 2)]
    tied = lax.optimization_barrier

    def low_rank(rows):
        return jnp.dot(rows, proj_both, preferred_element_type=jnp.float32)

    facing = lax.ppermute(grad_kv, "mp", across)
    beside = lax.ppermute(grad_kv, "mp", exchange_pairs)
    proj_both = tied(block_diagonal(proj_out))
    own_low = low_rank(grad_kv)
    low_in = jnp.dot(hidden, proj_in, preferred_element_type=jnp.float32)
    output = put_rows(me, 0, None, [grad_kv], [grad_kv], w_kv, local_rows)


    beside, low_in, output = tied((beside, low_in, output))
    beside_across = lax.ppermute(beside, "mp", across)
    second = lax.ppermute(facing, "mp", outward)
    low_in_beside = lax.ppermute(low_in, "mp", inward)
    output = put_rows(me, 1, output, [beside], [beside], w_kv, local_rows)

    beside_low = low_rank(beside)
    facing_low = low_rank(facing)

    beside_across, facing_low, output = tied((beside_across, facing_low, output))
    third = lax.ppermute(beside_across, "mp", outward)

    far_low = low_rank(beside_across)
    if low_in.shape[0] == SEQ:
        slabs = token_sums(me, low_in, low_in_beside, own_low, beside_low, facing_low, far_low, rank)[:, None]
    else:
        low_out = jnp.zeros((4, local_rows, 2 * rank), jnp.float32)
        for away, rows in ((0, own_low), (1, beside_low), (3, facing_low), (2, far_low)):
            low_out = put(low_out, rows, me ^ away)
        sums = sequence_sums(low_in + low_in_beside, low_out.reshape(4 * local_rows, 2 * rank), rank)
        slabs = slabs_of(sums, 4)
    slabs_across = lax.ppermute(slabs, "mp", across)
    slabs_across, second = tied((slabs_across, second))
    slabs = slabs + slabs_across
    mine = lax.ppermute(take(slabs, me ^ 2), "mp", [(2, 0), (1, 3)])
    mine = jnp.where(middle, take(slabs, me), mine)
    output = put_rows(me, 2, output, [facing], [second], w_kv, local_rows)
    mine, output = tied((mine, output))

    def finish(rows):
        rows = list(tied((*rows, output))[:-1])
        rows[-1] = tied((rows[-1], third))[0]
        return rows

    def rest():
        done = put_rows(me, 3, output, [beside_across], [third], w_kv, local_rows)
        return done.reshape(4 * local_rows, w_kv.shape[0])

    return mine, finish, rest


def on_device(hidden, w_kv, grad_kv, proj_in, proj_out, queries):
    n = lax.axis_size("mp")
    me = lax.axis_index("mp")
    mine, finish, rest = (line_of_four if n == 4 else gathered)(hidden, w_kv, grad_kv, proj_in, proj_out)
    count = mine.shape[0]

    shards = lax.axis_size("dp")
    shard = lax.axis_index("dp")
    block_rows = queries.shape[0]
    mine = mine.reshape(count, queries.shape[1])
    all_features = [mine] + [
        lax.ppermute(mine, "dp", [(source, (source + step) % shards) for source in range(shards)])
        for step in range(1, shards)
    ]
    if shards == n == 4:
        rows = finish(scores_by_step(all_features, queries, (shard - me + n) % n))
        scores = jnp.zeros((count, block_rows), jnp.float32)
        for step in range(n):
            pairs = [
                (q * n + slab, (slab + step) % n * n + q) for q in range(n) for slab in range(n)
            ]
            scores = scores + lax.ppermute(rows[step], ("dp", "mp"), pairs)
        return (rest(), scores)

    terms = jnp.concatenate(three_terms(jnp.concatenate(all_features, axis=0)), axis=0)
    products = lax.dot_general(
        terms, queries, (((1,), (1,)), ((), ())), preferred_element_type=jnp.float32
    ).reshape(3, shards, count, block_rows)
    partial_scores = products[0] + (products[1] + products[2])

    total = jnp.zeros((count, shards * block_rows), jnp.float32)
    for step in range(shards):
        back = partial_scores[step]
        if step > 0:
            back = lax.ppermute(back, "dp", [(source, (source - step) % shards) for source in range(shards)])
        total = lax.dynamic_update_slice(
            total, back, (jnp.int32(0), (shard + step) % shards * block_rows)
        )
    out_columns = shards * block_rows // n

    def columns_of(index):
        return lax.dynamic_slice(total, (jnp.int32(0), index * out_columns), (count, out_columns))

    scores = columns_of(me)
    for step in range(1, n):
        scores = scores + lax.ppermute(
            columns_of((me + step) % n), "mp", [(source, (source + step) % n) for source in range(n)]
        )
    return (rest(), scores)


def solution(mesh):
    in_specs = (
        P(("groups", "dp"), "mp"),
        P("mp", None),
        P(("groups", "dp", "mp"), None),
        P("mp", None),
        P(),
        P("dp", "mp"),
    )
    out_specs = (P(("groups", "dp"), "mp"), P(("groups", "dp"), "mp"))
    return jax.shard_map(
        on_device, mesh=mesh, in_specs=in_specs, out_specs=out_specs, check_vma=False
    )
```

```python
import functools

import jax
import jax.numpy as jnp
from jax import lax
from jax.experimental import pallas as pl
from jax.experimental.pallas import tpu as pltpu
from jax.sharding import PartitionSpec as P

SEQ = 1024


def three_terms(value):
    high = lax.reduce_precision(value, 8, 7)
    rest = value - high
    middle = lax.reduce_precision(rest, 8, 7)
    low = rest - middle
    return [term.astype(jnp.bfloat16) for term in (high, middle, low)]


def scores_kernel(shards, first, *refs):
    features, queries = refs[:shards], refs[shards]
    rows, found = refs[shards + 1 : -1], refs[-1]
    count = features[0].shape[0]
    value = jnp.concatenate([part[...] for part in features], axis=0)
    total = jnp.zeros(found.shape, jnp.float32)
    for _ in range(3):
        term = value.astype(jnp.bfloat16)
        value = value - term.astype(jnp.float32)
        total += lax.dot_general(
            term, queries[...], (((1,), (1,)), ((), ())), preferred_element_type=jnp.float32
        )
    found[...] = total
    for step, row in enumerate(rows):
        row[...] = found[pl.ds((first[0] - step + shards) % shards * count, count), :]


def scores_by_step(features, queries, first):
    shards = len(features)
    count = features[0].shape[0]
    block_rows = queries.shape[0]
    whole = pl.BlockSpec(memory_space=pltpu.VMEM)
    return pl.pallas_call(
        functools.partial(scores_kernel, shards),
        in_specs=[pl.BlockSpec(memory_space=pltpu.SMEM)] + [whole] * (shards + 1),
        out_specs=[whole] * shards,
        out_shape=[jax.ShapeDtypeStruct((count, block_rows), jnp.float32)] * shards,
        scratch_shapes=[pltpu.VMEM((shards * count, block_rows), jnp.float32)],
        compiler_params=pltpu.CompilerParams(vmem_limit_bytes=GRANT),
        name="scores",
    )(first.reshape(1).astype(jnp.int32), *features, queries)


def block_diagonal(proj_out):
    layers, width, rank = proj_out.shape
    zeros = jnp.zeros((width, rank), proj_out.dtype)
    return jnp.concatenate(
        [
            jnp.concatenate([proj_out[layer] if column == layer else zeros for column in range(layers)], axis=1)
            for layer in range(layers)
        ],
        axis=0,
    )


def times_width(rows, w_kv):
    return lax.dot_general(
        rows, w_kv, (((1,), (1,)), ((), ())), preferred_element_type=jnp.float32
    ).astype(jnp.bfloat16)


FETCH = 256
TILE = 512
GRANT = 48 * 2**20


def rows_kernel(block, start, count, me, *refs):
    firsts, seconds = refs[:count], refs[count : 2 * count]
    w_kv = refs[2 * count]
    out, held, weight, product, arrived, fetched, written = refs[-7:]
    mine = me[0]
    middle = (mine == 1) | (mine == 2)
    index = [mine, mine ^ 1, jnp.where(middle, mine ^ 3, mine ^ 2), jnp.where(middle, mine ^ 2, mine ^ 3)][block]
    use_second = jnp.logical_not(middle) if block > 1 else mine < 0

    fetches = []
    for piece in range(weight.shape[0] // FETCH):
        here = pl.ds(piece * FETCH, FETCH)
        fetches.append(pltpu.make_async_copy(w_kv.at[here], weight.at[here], fetched.at[piece]))
    loads = []
    filled = 0
    for part in range(count):
        rows = firsts[part].shape[0]
        here = held.at[pl.ds(filled, rows)]
        filled += rows
        loads.append(pltpu.make_async_copy(firsts[part], here, arrived.at[part]))
        late = pltpu.make_async_copy(seconds[part], here, arrived.at[part])
        if block > 1:
            pl.when(jnp.logical_not(use_second))(loads[-1].start)
            pl.when(use_second)(late.start)
        else:
            loads[-1].start()
    for fetch in fetches:
        fetch.start()
    for load in loads:
        load.wait()
    writes = []
    for tile in range(weight.shape[0] // TILE):
        here = pl.ds(tile * TILE, TILE)
        for piece in range(tile * TILE // FETCH, (tile + 1) * TILE // FETCH):
            fetches[piece].wait()
        product[:, here] = lax.dot_general(
            held[...], weight[here, :], (((1,), (1,)), ((), ())), preferred_element_type=jnp.float32
        ).astype(product.dtype)
        writes.append(
            pltpu.make_async_copy(
                product.at[:, here], out.at[index, pl.ds(start, product.shape[0]), here], written.at[tile]
            )
        )
        writes[-1].start()
    for write in writes:
        write.wait()


def put_rows(me, block, output, firsts, seconds, w_kv, block_rows, start=0):
    count = len(firsts)
    depth = firsts[0].shape[1]
    rows = sum(part.shape[0] for part in firsts)
    width = w_kv.shape[0]
    earlier = [] if output is None else [output]
    return pl.pallas_call(
        functools.partial(rows_kernel, block, start, count),
        in_specs=[pl.BlockSpec(memory_space=pltpu.SMEM)]
        + [pl.BlockSpec(memory_space=pl.ANY)] * (2 * count)
        + [pl.BlockSpec(memory_space=pltpu.HBM)] * (1 + len(earlier)),
        out_specs=pl.BlockSpec(memory_space=pltpu.HBM),
        scratch_shapes=[
            pltpu.VMEM((rows, depth), firsts[0].dtype),
            pltpu.VMEM((width, depth), w_kv.dtype),
            pltpu.VMEM((rows, width), jnp.bfloat16),
            pltpu.SemaphoreType.DMA((count,)),
            pltpu.SemaphoreType.DMA((width // FETCH,)),
            pltpu.SemaphoreType.DMA((width // TILE,)),
        ],
        out_shape=jax.ShapeDtypeStruct((4, block_rows, width), jnp.bfloat16),
        input_output_aliases={2 * count + 2: 0} if earlier else {},
        compiler_params=pltpu.CompilerParams(vmem_limit_bytes=GRANT),
        cost_estimate=pl.CostEstimate(flops=rows * width, bytes_accessed=rows * width, transcendentals=0),
        name="input_grad_rows",
    )(me.reshape(1).astype(jnp.int32), *firsts, *seconds, w_kv, *earlier)


def token_sums_kernel(me, low_in, low_in_beside, own_low, beside_low, facing_low, far_low, out):
    rows = own_low.shape[0]
    rank = out.shape[2]
    total = jnp.zeros((own_low.shape[1], own_low.shape[1]), jnp.float32)
    for away, low_out in (
        (0, own_low[...]),
        (1, beside_low[...]),
        (3, facing_low[...]),
        (2, far_low[...]),
    ):
        here = pl.ds(pl.multiple_of((me[0] ^ away) * rows, rows), rows)
        total += lax.dot_general(
            low_in[here, :] + low_in_beside[here, :],
            low_out,
            (((0,), (0,)), ((), ())),
            precision=lax.Precision.HIGHEST,
            preferred_element_type=jnp.float32,
        )
    slab = out.shape[1]
    for index in range(out.shape[0]):
        layer = index * slab // rank
        out[index] = total[index * slab : (index + 1) * slab, layer * rank : (layer + 1) * rank]


def token_sums(me, low_in, low_in_beside, own_low, beside_low, facing_low, far_low, rank):
    whole = pl.BlockSpec(memory_space=pltpu.VMEM)
    return pl.pallas_call(
        token_sums_kernel,
        in_specs=[pl.BlockSpec(memory_space=pltpu.SMEM)] + [whole] * 6,
        out_specs=whole,
        out_shape=jax.ShapeDtypeStruct((4, 2 * rank // 4, rank), jnp.float32),
        compiler_params=pltpu.CompilerParams(vmem_limit_bytes=GRANT),
        name="token_sums",
    )(me.reshape(1).astype(jnp.int32), low_in, low_in_beside, own_low, beside_low, facing_low, far_low)


def sequence_sums(low_in, low_out, rank):
    count = low_in.shape[0] // SEQ
    left = low_in.reshape(count, SEQ, 2 * rank)
    right = low_out.reshape(count, SEQ, 2 * rank)
    return jnp.concatenate(
        [
            lax.dot_general(
                left[:, :, layer * rank : (layer + 1) * rank],
                right[:, :, layer * rank : (layer + 1) * rank],
                (((1,), (1,)), ((0,), (0,))),
                precision=lax.Precision.HIGHEST,
                preferred_element_type=jnp.float32,
            )
            for layer in range(2)
        ],
        axis=1,
    )


def slabs_of(sums, n):
    count, height, rank = sums.shape
    return lax.optimization_barrier(sums.reshape(count, n, height // n, rank).transpose(1, 0, 2, 3))


def put(whole, piece, index):
    return lax.dynamic_update_slice(whole, piece[None], (index,) + (jnp.int32(0),) * piece.ndim)


def take(whole, index):
    return lax.dynamic_index_in_dim(whole, index, axis=0, keepdims=False)


def gathered(hidden, w_kv, grad_kv, proj_in, proj_out):
    n = lax.axis_size("mp")
    rank = proj_out.shape[2]
    whole = lax.all_gather(grad_kv, "mp", axis=0, tiled=True)
    input_grad = times_width(whole, w_kv)
    low_in = jnp.dot(hidden, proj_in, preferred_element_type=jnp.float32)
    sums = slabs_of(sequence_sums(low_in, jnp.dot(whole, block_diagonal(proj_out), preferred_element_type=jnp.float32), rank), n)
    features = lax.psum_scatter(sums, "mp", scatter_dimension=0, tiled=False)
    return features, lambda rows: rows, lambda: input_grad


def line_of_four(hidden, w_kv, grad_kv, proj_in, proj_out):
    rank = proj_out.shape[2]
    local_rows = grad_kv.shape[0]
    me = lax.axis_index("mp")
    middle = (me == 1) | (me == 2)
    exchange_pairs = [(0, 1), (1, 0), (2, 3), (3, 2)]
    across = [(1, 2), (2, 1)]
    outward = [(1, 0), (2, 3)]
    inward = [(0, 1), (3, 2)]
    tied = lax.optimization_barrier

    def low_rank(rows):
        return jnp.dot(rows, proj_both, preferred_element_type=jnp.float32)

    facing = lax.ppermute(grad_kv, "mp", across)
    beside = lax.ppermute(grad_kv, "mp", exchange_pairs)
    proj_both = tied(block_diagonal(proj_out))
    own_low = low_rank(grad_kv)
    low_in = jnp.dot(hidden, proj_in, preferred_element_type=jnp.float32)
    output = put_rows(me, 0, None, [grad_kv], [grad_kv], w_kv, local_rows)

    far_low = lax.ppermute(own_low, "mp", [(3, 1), (0, 2)])

    beside, low_in, far_low, output = tied((beside, low_in, far_low, output))
    beside_across = lax.ppermute(beside, "mp", across)
    second = lax.ppermute(facing, "mp", outward)
    low_in_beside = lax.ppermute(low_in, "mp", inward)
    output = put_rows(me, 1, output, [beside], [beside], w_kv, local_rows)

    low_in_beside, output = tied((low_in_beside, output))
    beside_low = low_rank(beside)
    facing_low = low_rank(facing)
    if low_in.shape[0] == SEQ:
        slabs = token_sums(me, low_in, low_in_beside, own_low, beside_low, facing_low, far_low, rank)[:, None]
    else:
        low_out = jnp.zeros((4, local_rows, 2 * rank), jnp.float32)
        for away, rows in ((0, own_low), (1, beside_low), (3, facing_low), (2, far_low)):
            low_out = put(low_out, rows, me ^ away)
        sums = sequence_sums(low_in + low_in_beside, low_out.reshape(4 * local_rows, 2 * rank), rank)
        slabs = slabs_of(sums, 4)
    slabs_across = lax.ppermute(slabs, "mp", across)

    beside_across, slabs_across, output = tied((beside_across, slabs_across, output))
    third = lax.ppermute(beside_across, "mp", outward)
    slabs_across, second = tied((slabs_across, second))
    slabs = slabs + slabs_across
    mine = lax.ppermute(take(slabs, me ^ 2), "mp", [(2, 0), (1, 3)])
    mine = jnp.where(middle, take(slabs, me), mine)
    output = put_rows(me, 2, output, [facing], [second], w_kv, local_rows)

    def finish(rows):
        rows = list(tied((*rows, output))[:-1])
        rows[-1] = tied((rows[-1], third))[0]
        return rows

    def rest():
        done = put_rows(me, 3, output, [beside_across], [third], w_kv, local_rows)
        return done.reshape(4 * local_rows, w_kv.shape[0])

    return mine, finish, rest


def on_device(hidden, w_kv, grad_kv, proj_in, proj_out, queries):
    n = lax.axis_size("mp")
    me = lax.axis_index("mp")
    mine, finish, rest = (line_of_four if n == 4 else gathered)(hidden, w_kv, grad_kv, proj_in, proj_out)
    count = mine.shape[0]

    shards = lax.axis_size("dp")
    shard = lax.axis_index("dp")
    block_rows = queries.shape[0]
    mine = mine.reshape(count, queries.shape[1])
    all_features = [mine] + [
        lax.ppermute(mine, "dp", [(source, (source + step) % shards) for source in range(shards)])
        for step in range(1, shards)
    ]
    if shards == n == 4:
        rows = finish(scores_by_step(all_features, queries, (shard - me + n) % n))
        scores = jnp.zeros((count, block_rows), jnp.float32)
        for step in range(n):
            pairs = [
                (q * n + slab, (slab + step) % n * n + q) for q in range(n) for slab in range(n)
            ]
            scores = scores + lax.ppermute(rows[step], ("dp", "mp"), pairs)
        return (rest(), scores)

    terms = jnp.concatenate(three_terms(jnp.concatenate(all_features, axis=0)), axis=0)
    products = lax.dot_general(
        terms, queries, (((1,), (1,)), ((), ())), preferred_element_type=jnp.float32
    ).reshape(3, shards, count, block_rows)
    partial_scores = products[0] + (products[1] + products[2])

    total = jnp.zeros((count, shards * block_rows), jnp.float32)
    for step in range(shards):
        back = partial_scores[step]
        if step > 0:
            back = lax.ppermute(back, "dp", [(source, (source - step) % shards) for source in range(shards)])
        total = lax.dynamic_update_slice(
            total, back, (jnp.int32(0), (shard + step) % shards * block_rows)
        )
    out_columns = shards * block_rows // n

    def columns_of(index):
        return lax.dynamic_slice(total, (jnp.int32(0), index * out_columns), (count, out_columns))

    scores = columns_of(me)
    for step in range(1, n):
        scores = scores + lax.ppermute(
            columns_of((me + step) % n), "mp", [(source, (source + step) % n) for source in range(n)]
        )
    return (rest(), scores)


def solution(mesh):
    in_specs = (
        P(("groups", "dp"), "mp"),
        P("mp", None),
        P(("groups", "dp", "mp"), None),
        P("mp", None),
        P(),
        P("dp", "mp"),
    )
    out_specs = (P(("groups", "dp"), "mp"), P(("groups", "dp"), "mp"))
    return jax.shard_map(
        on_device, mesh=mesh, in_specs=in_specs, out_specs=out_specs, check_vma=False
    )
```
